256 devices in a mesh: owner: 64 (over y, z, core), help: 4 (over x).
Axes of the slice: x: 4, y: 4, z: 8, core: 2. Of those that a mesh axis runs over, the one named last changes fastest.
Arguments:
- embeddings: bfloat16 [262144, 768], P(('owner', 'help')), may hold values from -8 to 8
- cluster_ids: int32 [262144, 1], P(('owner', 'help')), may hold values from 0 to 127; in each aligned block of 1024 rows (0 to 1023, 1024 to 2047, ...) at most 16 rows name the same one
Outputs:
- nearest: float32 [262144], P(('owner', 'help'))
- centre_cosine: float32 [262144], P(('owner', 'help'))
- centroids: float32 [128, 768], P('owner')
The draws below stay inside these ranges and needn't reach their ends.
Inputs may be any that keep to these rules, and one draw needn't show every extreme that they name: `cluster_ids`: within the rows of one device no cluster is named more than 16 times, a bound that some block reaches; every cluster is named by some row.
All inputs are finite; a program needn't handle non-finite values.
Results may differ from the reference program's by a relative error of at most 0.0003.
Values may be sent and summed in bfloat16 or wider, within the bound.
No kernel may reach another device: no remote copies, remote signals or barrier semaphores. Data moves between devices by JAX's collectives and lax.ppermute only.
A program may use at most 64 MiB of HBM per device.

```python
import math
import jax
import jax.numpy as jnp
import numpy as np
from jax import lax

D = 768
ROWS_DEV = 1024
C_SEND = 16
CLUSTERS = 128
ROWS = 262144
N_OWNER = 64
N_HELP = 4


def draw_embeddings(key, part):
    key = jax.random.fold_in(key, 7)
    second = jax.random.fold_in(key, 1)
    noise = jax.random.normal(second, (ROWS, D), jnp.float32)
    values = jnp.clip(noise, -6.0, 6.0)
    return values.astype(jnp.bfloat16)


def deal_out(own_key, own, number, rows, count, top, reach, lean):
    sequence = jax.random.permutation(own_key, count)
    heavy_load, usual = load_shares(count, rows * top, reach, lean, True), load_shares(count, rows * top, reach, lean, False)
    places = jnp.arange(count)

    def named(sizes, rotation):
        used = int((sizes > 0).sum())
        fixed = max(1, used // 4)
        passed = fixed + (places - fixed + rotation * (used - fixed)) % max(1, count - fixed)
        return jnp.zeros((count,), jnp.int32).at[sequence[jnp.where(places < fixed, places, passed)]].set(jnp.asarray(sizes, jnp.int32))

    sizes = jnp.where(number % 4 == 0, named(heavy_load, number // 4), named(usual, number - number // 4 - 1))
    mixed = jax.random.permutation(jax.random.fold_in(own, 3), count)
    source_of, sink = mixed[0:count // 2 * 2:2], mixed[1:count // 2 * 2:2]
    margin = jnp.minimum(sizes[source_of] - 1, reach - sizes[sink]) // 2
    margin = jnp.where((source_of == sequence[0]) | (sink == sequence[0]) | (sizes[sink] == 0), 0, jnp.maximum(margin, 0))
    passed = jax.random.randint(jax.random.fold_in(own, 4), (count // 2,), 0, 1 << 20) % (margin + 1)
    sizes = sizes.at[source_of].add(-passed).at[sink].add(passed)
    members = jnp.searchsorted(jnp.cumsum(sizes), jnp.arange(rows * top), side="right").astype(jnp.int32)
    grid = members.reshape(top, rows).T
    grid = grid[jax.random.permutation(jax.random.fold_in(own, 1), rows)]
    rotation = jax.random.randint(jax.random.fold_in(own, 2), (rows, 1), 0, top)
    return jnp.take_along_axis(grid, (jnp.arange(top)[None, :] + rotation) % top, axis=1)


def load_shares(amount, total, limit, lean, full):
    portions = [(1 << 20) // math.isqrt(grade ** lean) + 1 for grade in range(1, amount + 1)]
    largest = limit if full else min(limit, max(-(-total // amount), total * portions[0] // sum(portions)))
    least = 1 if total - largest >= amount - 1 else 0
    holding, rest = [largest] + [least] * (amount - 1), total - largest - least * (amount - 1)
    while rest > 0:
        candidates = [i for i in range(1, amount) if holding[i] < largest] or [i for i in range(1, amount) if holding[i] < limit]
        pool, budget = sum([portions[i] for i in candidates]), rest
        for i in candidates:
            more = min(limit - holding[i], max(1, budget * portions[i] // pool), rest)
            holding[i] = holding[i] + more
            rest = rest - more
    return np.array(holding)


def setup_inputs(seed: int = 0) -> dict:
    splits = jax.random.split(jax.random.key(seed), 3)
    embeddings = draw_embeddings(jax.random.fold_in(splits[2], 71), 0)
    cluster_ids_keys = jax.random.split(jax.random.fold_in(splits[1], 1), ROWS // ROWS_DEV)
    cluster_ids_turns = jax.random.permutation(jax.random.fold_in(splits[1], 3), ROWS // ROWS_DEV)
    cluster_ids = jax.vmap(lambda own, number: deal_out(jax.random.fold_in(splits[1], 2), own, number, ROWS_DEV, CLUSTERS, 1, C_SEND, 2))(cluster_ids_keys, cluster_ids_turns).reshape((ROWS, 1))
    return dict(embeddings=embeddings, cluster_ids=cluster_ids)


EPS = 1e-06

def reference(embeddings, cluster_ids):
    devs = N_OWNER * N_HELP
    ids = cluster_ids[:, 0].reshape(devs, ROWS_DEV)
    onehot = (ids[:, :, None] == jnp.arange(CLUSTERS, dtype=jnp.int32)[None, None, :]).astype(jnp.int32)
    rank = lax.optimization_barrier(jnp.sum((jnp.cumsum(onehot, axis=1) - onehot) * onehot, axis=2))
    span = devs * C_SEND
    slot = ids * span + jnp.arange(devs, dtype=jnp.int32)[:, None] * C_SEND + rank
    slot = slot.reshape(-1).astype(jnp.int32)
    buffer = jnp.zeros((CLUSTERS * span, D), jnp.bfloat16).at[slot].set(embeddings)
    alive = jnp.zeros((CLUSTERS * span,), jnp.float32).at[slot].set(1.0)
    buffer = buffer.reshape(CLUSTERS, span, D)
    alive = alive.reshape(CLUSTERS, span)

    def one_cluster(pair):
        block, live = pair
        wide = block.astype(jnp.float32)
        inv = lax.rsqrt(lax.optimization_barrier(jnp.sum(wide * wide, axis=1)) / D + EPS)
        dots = jnp.dot(wide, wide.T, precision=lax.Precision.HIGHEST)
        cosine = dots * inv[:, None] * inv[None, :] / D
        index = jnp.arange(span, dtype=jnp.int32)
        keep = (live[None, :] > 0) & (index[:, None] != index[None, :])
        best = lax.optimization_barrier(jnp.max(jnp.where(keep, cosine, -1.0), axis=1))
        totals = jnp.dot(live, wide, precision=lax.Precision.HIGHEST)
        count = jnp.sum(live)
        toward = jnp.dot(wide, totals, precision=lax.Precision.HIGHEST)
        scale = lax.rsqrt(jnp.sum(totals * totals) / D + EPS)
        centre = toward * inv * scale / D
        return (best, centre, totals / count)
    best, centre, means = lax.map(one_cluster, (buffer, alive))
    nearest = best.reshape(-1)[slot]
    centre_cosine = centre.reshape(-1)[slot]
    return (nearest, centre_cosine, means)
```

```python
import jax
import jax.numpy as jnp
from jax import lax
from jax.experimental import pallas as pl
from jax.experimental.pallas import tpu as pltpu
from jax.sharding import Mesh, PartitionSpec as P

EPS = 1e-06
ROWS = 1024
WIDTH = 768
CAP = 16
CHIPS = 128
SLOTS = CHIPS * CAP
MARK = 64.0
LOW = -1e30
TILE = 512
NT = (((1,), (1,)), ((), ()))
TN = (((0,), (0,)), ((), ()))
F32 = jnp.float32
BF16 = jnp.bfloat16


def iota(shape, dim):
    return lax.broadcasted_iota(jnp.int32, shape, dim)


def split3(v):
    hi = v.astype(BF16)
    rest = v - hi.astype(F32)
    mid = rest.astype(BF16)
    lo = (rest - mid.astype(F32)).astype(BF16)
    return hi, mid, lo


def pack_kernel(ids_ref, x_ref, send_ref, rank_ref):
    ids = ids_ref[...]
    same = iota((CHIPS, ROWS), 0) == ids
    onehot = same.astype(F32).astype(BF16)
    before = (iota((ROWS, ROWS), 0) < iota((ROWS, ROWS), 1)).astype(F32).astype(BF16)
    earlier = jnp.dot(onehot, before, preferred_element_type=F32)
    rank = jnp.sum(jnp.where(same, earlier, 0.0), axis=0, keepdims=True).astype(jnp.int32)
    rank_ref[...] = rank
    position = ids * CAP + rank
    step = 256

    def block(b, _):
        start = pl.multiple_of(b * step, step)
        pick = (iota((step, ROWS), 0) + start == position).astype(F32)
        live = jnp.sum(pick, axis=1, keepdims=True)
        rows = jnp.dot(pick.astype(BF16), x_ref[...], preferred_element_type=F32)
        mark = jnp.where(iota((step, 128), 1) == 0, (1.0 - live) * MARK, 0.0)
        send_ref[pl.ds(start, step), 0:128] = (rows[:, 0:128] + mark).astype(BF16)
        send_ref[pl.ds(start, step), 128:] = rows[:, 128:].astype(BF16)
        return 0

    lax.fori_loop(0, SLOTS // step, block, 0)


def stats(x_ref, inv_ref, bias_ref):
    def block(b, carry):
        total, count = carry
        start = pl.multiple_of(b * 128, 128)
        x = x_ref[pl.ds(start, 128), :].astype(F32)
        live = x[:, 0:1] < MARK / 2
        x = jnp.where(live, x, 0.0)
        inv_ref[pl.ds(start, 128), :] = lax.rsqrt(
            jnp.sum(x * x, axis=1, keepdims=True) / WIDTH + EPS
        )
        bias_ref[pl.ds(start, 128), :] = jnp.where(live, 0.0, LOW)
        total = total + jnp.sum(x.reshape(16, 8, WIDTH), axis=0)
        count = count + jnp.sum(live.astype(F32).reshape(16, 8, 1), axis=0)
        return total, count

    zero = (jnp.zeros((8, WIDTH), F32), jnp.zeros((8, 1), F32))
    total, count = lax.fori_loop(0, SLOTS // 128, block, zero)
    return jnp.sum(total, axis=0, keepdims=True), jnp.sum(count, axis=0, keepdims=True)


def tile_best(other_ref, inv_ref, bias_ref, j, mine, diagonal=False):
    start = pl.multiple_of(j * TILE, TILE)
    dots = lax.dot_general(other_ref[pl.ds(start, TILE), :], mine, NT, preferred_element_type=F32)
    value = dots * inv_ref[pl.ds(start, TILE), :] + bias_ref[pl.ds(start, TILE), :]
    square = None
    if diagonal:
        eye = iota((TILE, TILE), 0) == iota((TILE, TILE), 1)
        square = jnp.sum(jnp.where(eye, dots, 0.0), axis=0, keepdims=True)
        value = jnp.where(eye, LOW, value)
    return jnp.max(value.reshape(TILE // 8, 8, TILE), axis=0), square


def own_kernel(x_ref, best_ref, inv_row_ref, total_ref, inv_ref, bias_ref):
    total, count = stats(x_ref, inv_ref, bias_ref)
    total_ref[:, :WIDTH] = total
    total_ref[:, WIDTH:] = jnp.broadcast_to(count, (1, 128))
    tiles = SLOTS // TILE
    for i in range(tiles):
        mine = x_ref[i * TILE : (i + 1) * TILE, :]
        best, square = tile_best(x_ref, inv_ref, bias_ref, i, mine, True)

        def other(k, best):
            j = lax.rem(i + 1 + k, tiles)
            return jnp.maximum(best, tile_best(x_ref, inv_ref, bias_ref, j, mine)[0])

        best = lax.fori_loop(0, tiles - 1, other, best)
        best_ref[:, i * TILE : (i + 1) * TILE] = jnp.max(best, axis=0, keepdims=True)
        inv_row_ref[:, i * TILE : (i + 1) * TILE] = lax.rsqrt(square / WIDTH + EPS)


def rest_kernel(x_ref, sib_ref, best_ref, inv_row_ref, total_ref, out_ref, inv_ref, bias_ref, near_ref):
    sib_total, _ = stats(sib_ref, inv_ref, bias_ref)
    total = total_ref[:, :WIDTH] + sib_total
    tiles = SLOTS // TILE

    def row(i, _):
        start = pl.multiple_of(i * TILE, TILE)
        mine = x_ref[pl.ds(start, TILE), :]

        def other(j, best):
            return jnp.maximum(best, tile_best(sib_ref, inv_ref, bias_ref, j, mine)[0])

        best = lax.fori_loop(0, tiles, other, jnp.full((8, TILE), LOW, F32))
        best = jnp.max(best, axis=0, keepdims=True)
        best = jnp.maximum(best, best_ref[:, pl.ds(start, TILE)])
        inv = inv_row_ref[:, pl.ds(start, TILE)]
        near_ref[:, pl.ds(start, TILE)] = jnp.maximum(-1.0, best * inv / WIDTH)
        return 0

    lax.fori_loop(0, tiles, row, 0)
    scale = lax.rsqrt(jnp.sum(total * total, axis=1, keepdims=True) / WIDTH + EPS)
    parts = jnp.concatenate(split3(total) + (jnp.zeros((13, WIDTH), BF16),), axis=0)
    toward = lax.dot_general(parts, x_ref[...], NT, preferred_element_type=F32)
    toward = toward[0:1] + toward[1:2] + toward[2:3]
    centre = toward * inv_row_ref[...] * scale / WIDTH
    lane = iota((CAP, SLOTS), 1)
    slot = lax.rem(lane, CAP) == iota((CAP, SLOTS), 0)
    near = jnp.where(slot, near_ref[...], 0.0)
    centre = jnp.where(slot, centre, 0.0)
    parts = jnp.concatenate(split3(jnp.concatenate([near, centre], axis=0)), axis=0)
    source = (iota((CHIPS, SLOTS), 1) // CAP == iota((CHIPS, SLOTS), 0)).astype(F32).astype(BF16)
    spread = lax.dot_general(source, parts, NT, preferred_element_type=F32)
    out_ref[...] = (
        spread[:, 0 : 2 * CAP] + spread[:, 2 * CAP : 4 * CAP] + spread[:, 4 * CAP : 6 * CAP]
    )


def unpack_kernel(ids_ref, rank_ref, back_ref, near_ref, centre_ref):
    same = iota((CHIPS, ROWS), 0) == ids_ref[...]
    onehot = same.astype(F32).astype(BF16)
    parts = jnp.concatenate(split3(back_ref[...]), axis=1)
    picked = lax.dot_general(parts, onehot, TN, preferred_element_type=F32)
    picked = picked[0 : 2 * CAP] + picked[2 * CAP : 4 * CAP] + picked[4 * CAP : 6 * CAP]
    slot = iota((CAP, ROWS), 0) == rank_ref[...]
    near_ref[...] = jnp.sum(jnp.where(slot, picked[0:CAP], 0.0), axis=0, keepdims=True)
    centre_ref[...] = jnp.sum(jnp.where(slot, picked[CAP:], 0.0), axis=0, keepdims=True)


def struct(shape, dtype):
    return jax.ShapeDtypeStruct(shape, dtype)


def call(kernel, outs, flops, scratch=()):
    return pl.pallas_call(
        kernel,
        out_shape=outs,
        scratch_shapes=list(scratch),
        compiler_params=pltpu.CompilerParams(vmem_limit_bytes=40 * 1024 * 1024),
        cost_estimate=pl.CostEstimate(
            flops=int(flops), bytes_accessed=6_000_000, transcendentals=0
        ),
    )


def shards(embeddings, cluster_ids):
    ids = cluster_ids.reshape(1, ROWS)
    send, rank = call(
        pack_kernel,
        (struct((SLOTS, WIDTH), BF16), struct((1, ROWS), jnp.int32)),
        2 * SLOTS * ROWS * WIDTH,
    )(ids, embeddings)
    chips = ("y", "z", "x")
    mine = lax.all_to_all(send.reshape(CHIPS, CAP, WIDTH), chips, 0, 0, tiled=True)
    mine = mine.reshape(SLOTS, WIDTH)
    swap = [(0, 1), (1, 0)]
    sib = lax.ppermute(mine, "core", swap)
    column = pltpu.VMEM((SLOTS, 1), F32)
    lanes = struct((1, SLOTS), F32)
    best, inv_row, part = call(
        own_kernel,
        (lanes, lanes, struct((1, WIDTH + 128), F32)),
        2 * SLOTS * SLOTS * WIDTH,
        (column, column),
    )(mine)
    total = part + lax.ppermute(part, "core", swap)
    mean = total[:, :WIDTH] / total[:, WIDTH : WIDTH + 1]
    x = lax.axis_index("x")
    core = lax.axis_index("core")
    means = jnp.zeros((2, WIDTH), F32)
    for k in range(4):
        came = mean if k == 0 else lax.ppermute(mean, "x", [(i, (i + k) % 4) for i in range(4)])
        place = lax.rem(x - k + 4, 4) - 2 * core
        means = jnp.where(jnp.arange(2)[:, None] == place, came, means)
    out = call(
        rest_kernel,
        struct((CHIPS, 2 * CAP), F32),
        2 * SLOTS * SLOTS * WIDTH,
        (column, column, pltpu.VMEM((1, SLOTS), F32)),
    )(mine, sib, best, inv_row, part)
    back = lax.all_to_all(out, chips, 0, 0, tiled=True)
    near, centre = call(
        unpack_kernel, (struct((1, ROWS), F32), struct((1, ROWS), F32)), 1e8
    )(ids, rank, back)
    return near.reshape(ROWS), centre.reshape(ROWS), means


def solution(mesh):
    fine = Mesh(mesh.devices.reshape(4, 8, 2, 4), ("y", "z", "core", "x"))
    owner = ("y", "z", "core")
    every = owner + ("x",)
    return jax.shard_map(
        shards,
        mesh=fine,
        in_specs=(P(every, None), P(every, None)),
        out_specs=(P(every), P(every), P(owner, None)),
        check_vma=False,
    )
```

```python
import jax
import jax.numpy as jnp
from jax import lax
from jax.experimental import pallas as pl
from jax.experimental.pallas import tpu as pltpu
from jax.sharding import Mesh, PartitionSpec as P

EPS = 1e-06
ROWS = 1024
WIDTH = 768
CAP = 16
CHIPS = 128
SLOTS = CHIPS * CAP
MARK = 64.0
LOW = -1e30
TILE = 512
TILES = SLOTS // TILE
NT = (((1,), (1,)), ((), ()))
TN = (((0,), (0,)), ((), ()))
F32 = jnp.float32
BF16 = jnp.bfloat16


def iota(shape, dim):
    return lax.broadcasted_iota(jnp.int32, shape, dim)


def split3(v):
    hi = v.astype(BF16)
    rest = v - hi.astype(F32)
    mid = rest.astype(BF16)
    lo = (rest - mid.astype(F32)).astype(BF16)
    return hi, mid, lo


def chip_of(ids):
    return ((ids >> 2) & 7) * 16 + (ids & 3) * 4 + (ids >> 5)


def eye(n):
    return iota((n, n), 0) == iota((n, n), 1)


def to_row(column):
    blocks = [
        jnp.sum(jnp.where(eye(128), column[k : k + 128], 0.0), axis=0, keepdims=True)
        for k in range(0, column.shape[0], 128)
    ]
    return jnp.concatenate(blocks, axis=1)


def to_column(row):
    blocks = [
        jnp.sum(jnp.where(eye(128), row[:, k : k + 128], 0.0), axis=1, keepdims=True)
        for k in range(0, row.shape[1], 128)
    ]
    return jnp.concatenate(blocks, axis=0)


def fold_lanes(value):
    best = value[:, 0:128]
    for k in range(128, value.shape[1], 128):
        best = jnp.maximum(best, value[:, k : k + 128])
    return best


def part(ref, i):
    return ref[i * TILE : (i + 1) * TILE, :]


def lanes(ref, row, i):
    return ref[row : row + 1, i * TILE : (i + 1) * TILE]


def pack_kernel(ids_ref, x_hbm, send_ref, rank_ref, x_ref, sem):
    copy = pltpu.make_async_copy(x_hbm, x_ref, sem)
    copy.start()
    chip = chip_of(ids_ref[...])
    same = iota((CHIPS, ROWS), 0) == chip
    onehot = same.astype(F32).astype(BF16)
    before = (iota((ROWS, ROWS), 0) < iota((ROWS, ROWS), 1)).astype(F32).astype(BF16)
    earlier = jnp.dot(onehot, before, preferred_element_type=F32)
    rank = jnp.sum(jnp.where(same, earlier, 0.0), axis=0, keepdims=True).astype(jnp.int32)
    rank_ref[...] = rank
    position = chip * CAP + rank
    step = 256
    copy.wait()
    for start in range(0, SLOTS, step):
        pick = (iota((step, ROWS), 0) + start == position).astype(F32)
        live = jnp.sum(pick, axis=1, keepdims=True)
        rows = jnp.dot(pick.astype(BF16), x_ref[...], preferred_element_type=F32)
        mark = jnp.where(iota((step, 128), 1) == 0, (1.0 - live) * MARK, 0.0)
        send_ref[start : start + step, 0:128] = (rows[:, 0:128] + mark).astype(BF16)
        send_ref[start : start + step, 128:] = rows[:, 128:].astype(BF16)


def diagonal_kernel(x_ref, info_ref, best_ref):
    first = (iota((8, WIDTH), 1) == 0).astype(F32).astype(BF16)
    marks = lax.dot_general(first, x_ref[...], NT, preferred_element_type=F32)
    live = (marks < MARK / 2).astype(F32)
    totals = jnp.dot(live.astype(BF16), x_ref[...], preferred_element_type=F32)
    info_ref[1:2, :] = jnp.where(live[0:1] > 0, 0.0, LOW)
    info_ref[2:3, 0:WIDTH] = totals[0:1]
    count = jnp.sum(live[0:1], axis=1, keepdims=True)
    info_ref[2:3, WIDTH:] = jnp.broadcast_to(count, (1, SLOTS - WIDTH))
    for i in range(TILES):
        dots = lax.dot_general(part(x_ref, i), part(x_ref, i), NT, preferred_element_type=F32)
        square = jnp.sum(jnp.where(eye(TILE), dots, 0.0), axis=0, keepdims=True)
        inv = lax.rsqrt(square / WIDTH + EPS)
        info_ref[0:1, i * TILE : (i + 1) * TILE] = inv
        value = jnp.where(eye(TILE), LOW, dots * inv + lanes(info_ref, 1, i))
        best = jnp.max(fold_lanes(value), axis=1, keepdims=True)
        best_ref[:, i * TILE : (i + 1) * TILE] = to_row(best)


def own_kernel(x_ref, info_ref, before_ref, best_ref, fold_ref):
    best_ref[...] = before_ref[...]
    for i in range(TILES - 1):
        inv = to_column(lanes(info_ref, 0, i))
        bias = to_column(lanes(info_ref, 1, i))
        for j in range(i + 1, TILES):
            dots = lax.dot_general(part(x_ref, i), part(x_ref, j), NT, preferred_element_type=F32)
            fold = fold_lanes(dots * lanes(info_ref, 0, j) + lanes(info_ref, 1, j))
            fold_ref[...] = fold if j == i + 1 else jnp.maximum(fold_ref[...], fold)
            down = jnp.max(dots * inv + bias, axis=0, keepdims=True)
            best_ref[:, j * TILE : (j + 1) * TILE] = jnp.maximum(lanes(best_ref, 0, j), down)
        best = to_row(jnp.max(fold_ref[...], axis=1, keepdims=True))
        best_ref[:, i * TILE : (i + 1) * TILE] = jnp.maximum(lanes(best_ref, 0, i), best)


def rest_kernel(x_ref, sib_ref, info_ref, sib_info_ref, best_ref, out_ref, mean_ref, near_ref, fold_ref):
    for i in range(TILES):
        for j in range(TILES):
            dots = lax.dot_general(part(x_ref, i), part(sib_ref, j), NT, preferred_element_type=F32)
            fold = fold_lanes(dots * lanes(sib_info_ref, 0, j) + lanes(sib_info_ref, 1, j))
            fold_ref[...] = fold if j == 0 else jnp.maximum(fold_ref[...], fold)
        best = to_row(jnp.max(fold_ref[...], axis=1, keepdims=True))
        best = jnp.maximum(best, lanes(best_ref, 0, i))
        near_ref[:, i * TILE : (i + 1) * TILE] = jnp.maximum(
            -1.0, best * lanes(info_ref, 0, i) / WIDTH
        )
    total = info_ref[2:3, 0:WIDTH] + sib_info_ref[2:3, 0:WIDTH]
    count = info_ref[2:3, WIDTH : WIDTH + 1] + sib_info_ref[2:3, WIDTH : WIDTH + 1]
    mean_ref[...] = total / count
    scale = lax.rsqrt(jnp.sum(total * total, axis=1, keepdims=True) / WIDTH + EPS)
    parts = jnp.concatenate(split3(total) + (jnp.zeros((13, WIDTH), BF16),), axis=0)
    toward = lax.dot_general(parts, x_ref[...], NT, preferred_element_type=F32)
    toward = toward[0:1] + toward[1:2] + toward[2:3]
    centre = toward * info_ref[0:1, :] * scale / WIDTH
    slot = lax.rem(iota((CAP, SLOTS), 1), CAP) == iota((CAP, SLOTS), 0)
    near = jnp.where(slot, near_ref[...], 0.0)
    centre = jnp.where(slot, centre, 0.0)
    parts = jnp.concatenate(split3(jnp.concatenate([near, centre], axis=0)), axis=0)
    source = (iota((CHIPS, SLOTS), 1) // CAP == iota((CHIPS, SLOTS), 0)).astype(F32).astype(BF16)
    spread = lax.dot_general(source, parts, NT, preferred_element_type=F32)
    out_ref[...] = (
        spread[:, 0 : 2 * CAP] + spread[:, 2 * CAP : 4 * CAP] + spread[:, 4 * CAP : 6 * CAP]
    )


def unpack_kernel(ids_ref, rank_ref, back_ref, near_ref, centre_ref):
    same = iota((CHIPS, ROWS), 0) == chip_of(ids_ref[...])
    onehot = same.astype(F32).astype(BF16)
    parts = jnp.concatenate(split3(back_ref[...]), axis=1)
    picked = lax.dot_general(parts, onehot, TN, preferred_element_type=F32)
    picked = picked[0 : 2 * CAP] + picked[2 * CAP : 4 * CAP] + picked[4 * CAP : 6 * CAP]
    slot = iota((CAP, ROWS), 0) == rank_ref[...]
    near_ref[...] = jnp.sum(jnp.where(slot, picked[0:CAP], 0.0), axis=0, keepdims=True)
    centre_ref[...] = jnp.sum(jnp.where(slot, picked[CAP:], 0.0), axis=0, keepdims=True)


def struct(shape, dtype):
    return jax.ShapeDtypeStruct(shape, dtype)


def call(kernel, outs, flops, scratch=(), **specs):
    return pl.pallas_call(
        kernel,
        out_shape=outs,
        scratch_shapes=list(scratch),
        compiler_params=pltpu.CompilerParams(vmem_limit_bytes=40 * 1024 * 1024),
        cost_estimate=pl.CostEstimate(
            flops=int(flops), bytes_accessed=6_000_000, transcendentals=0
        ),
        **specs,
    )


def shards(embeddings, cluster_ids):
    ids = cluster_ids.reshape(1, ROWS)
    block = 2 * SLOTS * SLOTS * WIDTH
    send, rank = call(
        pack_kernel,
        (struct((SLOTS, WIDTH), BF16), struct((1, ROWS), jnp.int32)),
        2 * SLOTS * ROWS * WIDTH,
        (pltpu.VMEM((ROWS, WIDTH), BF16), pltpu.SemaphoreType.DMA),
        in_specs=[pl.BlockSpec(memory_space=pltpu.VMEM), pl.BlockSpec(memory_space=pltpu.HBM)],
    )(ids, embeddings)
    chips = ("z", "x", "y")
    mine = lax.all_to_all(send.reshape(CHIPS, CAP, WIDTH), chips, 0, 0, tiled=True)
    mine = mine.reshape(SLOTS, WIDTH)
    swap = [(0, 1), (1, 0)]
    sib = lax.ppermute(mine, "core", swap)
    row = struct((1, SLOTS), F32)
    info, best = call(diagonal_kernel, (struct((3, SLOTS), F32), row), block / 4)(mine)
    sib_info = lax.ppermute(info, "core", swap)
    fold = pltpu.VMEM((TILE, 128), F32)
    best = call(own_kernel, row, block * 3 / 8, (fold,))(mine, info, best)
    out, mean = call(
        rest_kernel,
        (struct((CHIPS, 2 * CAP), F32), struct((1, WIDTH), F32)),
        block,
        (pltpu.VMEM((1, SLOTS), F32), fold),
    )(mine, sib, info, sib_info, best)
    back = lax.all_to_all(out, chips, 0, 0, tiled=True)
    x = lax.axis_index("x")
    core = lax.axis_index("core")
    means = jnp.zeros((2, WIDTH), F32)
    for k in range(4):
        came = mean if k == 0 else lax.ppermute(mean, "x", [(i, (i + k) % 4) for i in range(4)])
        place = lax.rem(x - k + 4, 4) - 2 * core
        means = jnp.where(jnp.arange(2)[:, None] == place, came, means)
    near, centre = call(
        unpack_kernel, (struct((1, ROWS), F32), struct((1, ROWS), F32)), 1e8
    )(ids, rank, back)
    return near.reshape(ROWS), centre.reshape(ROWS), means


def solution(mesh):
    fine = Mesh(mesh.devices.reshape(4, 8, 2, 4), ("y", "z", "core", "x"))
    owner = ("y", "z", "core")
    every = owner + ("x",)
    return jax.shard_map(
        shards,
        mesh=fine,
        in_specs=(P(every, None), P(every, None)),
        out_specs=(P(every), P(every), P(owner, None)),
        check_vma=False,
    )
```

```python
import jax
import jax.numpy as jnp
from jax import lax
from jax.experimental import pallas as pl
from jax.experimental.pallas import tpu as pltpu
from jax.sharding import Mesh, PartitionSpec as P

EPS = 1e-06
ROWS = 1024
WIDTH = 768
CAP = 16
CHIPS = 128
SLOTS = CHIPS * CAP
MARK = 64.0
LOW = -1e30
TILE = 512
TILES = SLOTS // TILE
NT = (((1,), (1,)), ((), ()))
TN = (((0,), (0,)), ((), ()))
F32 = jnp.float32
BF16 = jnp.bfloat16


def iota(shape, dim):
    return lax.broadcasted_iota(jnp.int32, shape, dim)


def split3(v):
    hi = v.astype(BF16)
    rest = v - hi.astype(F32)
    mid = rest.astype(BF16)
    lo = (rest - mid.astype(F32)).astype(BF16)
    return hi, mid, lo


def chip_of(ids):
    return ((ids >> 2) & 7) * 16 + (ids & 3) * 4 + (ids >> 5)


def eye(n):
    return iota((n, n), 0) == iota((n, n), 1)


def to_row(column):
    blocks = [
        jnp.sum(jnp.where(eye(128), column[k : k + 128], 0.0), axis=0, keepdims=True)
        for k in range(0, column.shape[0], 128)
    ]
    return jnp.concatenate(blocks, axis=1)


def to_column(row):
    blocks = [
        jnp.sum(jnp.where(eye(128), row[:, k : k + 128], 0.0), axis=1, keepdims=True)
        for k in range(0, row.shape[1], 128)
    ]
    return jnp.concatenate(blocks, axis=0)


def fold_lanes(value):
    best = value[:, 0:128]
    for k in range(128, value.shape[1], 128):
        best = jnp.maximum(best, value[:, k : k + 128])
    return best


def part(ref, i):
    return ref[i * TILE : (i + 1) * TILE, :]


def lanes(ref, row, i):
    return ref[row : row + 1, i * TILE : (i + 1) * TILE]


def pack_kernel(ids_ref, x_hbm, send_hbm, rank_ref, x_ref, sem, send_ref, sems):
    copy = pltpu.make_async_copy(x_hbm, x_ref, sem)
    copy.start()
    chip = chip_of(ids_ref[...])
    same = iota((CHIPS, ROWS), 0) == chip
    onehot = same.astype(F32).astype(BF16)
    before = (iota((ROWS, ROWS), 0) < iota((ROWS, ROWS), 1)).astype(F32).astype(BF16)
    earlier = jnp.dot(onehot, before, preferred_element_type=F32)
    rank = jnp.sum(jnp.where(same, earlier, 0.0), axis=0, keepdims=True).astype(jnp.int32)
    rank_ref[...] = rank
    position = chip * CAP + rank
    step = 256
    copy.wait()
    copies = []
    for start in range(0, SLOTS, step):
        pick = (iota((step, ROWS), 0) + start == position).astype(F32)
        live = jnp.sum(pick, axis=1, keepdims=True)
        rows = jnp.dot(pick.astype(BF16), x_ref[...], preferred_element_type=F32)
        mark = jnp.where(iota((step, 128), 1) == 0, (1.0 - live) * MARK, 0.0)
        send_ref[start : start + step, 0:128] = (rows[:, 0:128] + mark).astype(BF16)
        send_ref[start : start + step, 128:] = rows[:, 128:].astype(BF16)
        copies.append(
            pltpu.make_async_copy(
                send_ref.at[start : start + step, :],
                send_hbm.at[start : start + step, :],
                sems.at[start // step],
            )
        )
        copies[-1].start()
    for copy in copies:
        copy.wait()


def diagonal_kernel(x_ref, info_ref, best_ref):
    live = to_row((x_ref[:, 0:1].astype(F32) < MARK / 2).astype(F32))
    weights = jnp.broadcast_to(live, (8, SLOTS)).astype(BF16)
    totals = jnp.dot(weights, x_ref[...], preferred_element_type=F32)
    info_ref[1:2, :] = jnp.where(live > 0, 0.0, LOW)
    info_ref[2:3, 0:WIDTH] = totals[0:1]
    count = jnp.sum(live, axis=1, keepdims=True)
    info_ref[2:3, WIDTH:] = jnp.broadcast_to(count, (1, SLOTS - WIDTH))
    for i in range(TILES):
        dots = lax.dot_general(part(x_ref, i), part(x_ref, i), NT, preferred_element_type=F32)
        square = jnp.sum(jnp.where(eye(TILE), dots, 0.0), axis=0, keepdims=True)
        inv = lax.rsqrt(square / WIDTH + EPS)
        info_ref[0:1, i * TILE : (i + 1) * TILE] = inv
        value = jnp.where(eye(TILE), LOW, dots * inv + lanes(info_ref, 1, i))
        best = jnp.max(fold_lanes(value), axis=1, keepdims=True)
        best_ref[:, i * TILE : (i + 1) * TILE] = to_row(best)


def own_kernel(x_ref, info_ref, before_ref, best_ref, fold_ref):
    best_ref[...] = before_ref[...]
    for i in range(TILES - 1):
        inv = to_column(lanes(info_ref, 0, i))
        bias = to_column(lanes(info_ref, 1, i))
        for j in range(i + 1, TILES):
            dots = lax.dot_general(part(x_ref, i), part(x_ref, j), NT, preferred_element_type=F32)
            fold = fold_lanes(dots * lanes(info_ref, 0, j) + lanes(info_ref, 1, j))
            fold_ref[...] = fold if j == i + 1 else jnp.maximum(fold_ref[...], fold)
            down = jnp.max(dots * inv + bias, axis=0, keepdims=True)
            best_ref[:, j * TILE : (j + 1) * TILE] = jnp.maximum(lanes(best_ref, 0, j), down)
        best = to_row(jnp.max(fold_ref[...], axis=1, keepdims=True))
        best_ref[:, i * TILE : (i + 1) * TILE] = jnp.maximum(lanes(best_ref, 0, i), best)


def rest_kernel(
    x_ref, sib_hbm, info_ref, sib_info_ref, best_ref, out_ref, mean_ref, near_ref, fold_ref, sib_ref, sems
):
    copies = [
        pltpu.make_async_copy(part(sib_hbm.at, j), part(sib_ref.at, j), sems.at[j])
        for j in range(TILES)
    ]
    for copy in copies:
        copy.start()
    for i in range(TILES):
        for j in range(TILES):
            if i == 0:
                copies[j].wait()
            dots = lax.dot_general(part(x_ref, i), part(sib_ref, j), NT, preferred_element_type=F32)
            fold = fold_lanes(dots * lanes(sib_info_ref, 0, j) + lanes(sib_info_ref, 1, j))
            fold_ref[...] = fold if j == 0 else jnp.maximum(fold_ref[...], fold)
        best = to_row(jnp.max(fold_ref[...], axis=1, keepdims=True))
        best = jnp.maximum(best, lanes(best_ref, 0, i))
        near_ref[:, i * TILE : (i + 1) * TILE] = jnp.maximum(
            -1.0, best * lanes(info_ref, 0, i) / WIDTH
        )
    total = info_ref[2:3, 0:WIDTH] + sib_info_ref[2:3, 0:WIDTH]
    count = info_ref[2:3, WIDTH : WIDTH + 1] + sib_info_ref[2:3, WIDTH : WIDTH + 1]
    mean_ref[...] = total / count
    scale = lax.rsqrt(jnp.sum(total * total, axis=1, keepdims=True) / WIDTH + EPS)
    parts = jnp.concatenate(split3(total) + (jnp.zeros((13, WIDTH), BF16),), axis=0)
    toward = lax.dot_general(parts, x_ref[...], NT, preferred_element_type=F32)
    toward = toward[0:1] + toward[1:2] + toward[2:3]
    centre = toward * info_ref[0:1, :] * scale / WIDTH
    slot = lax.rem(iota((CAP, SLOTS), 1), CAP) == iota((CAP, SLOTS), 0)
    near = jnp.where(slot, near_ref[...], 0.0)
    centre = jnp.where(slot, centre, 0.0)
    parts = jnp.concatenate(split3(jnp.concatenate([near, centre], axis=0)), axis=0)
    source = (iota((CHIPS, SLOTS), 1) // CAP == iota((CHIPS, SLOTS), 0)).astype(F32).astype(BF16)
    spread = lax.dot_general(source, parts, NT, preferred_element_type=F32)
    out_ref[...] = (
        spread[:, 0 : 2 * CAP] + spread[:, 2 * CAP : 4 * CAP] + spread[:, 4 * CAP : 6 * CAP]
    )


def unpack_kernel(ids_ref, rank_ref, back_ref, near_ref, centre_ref):
    same = iota((CHIPS, ROWS), 0) == chip_of(ids_ref[...])
    onehot = same.astype(F32).astype(BF16)
    parts = jnp.concatenate(split3(back_ref[...]), axis=1)
    picked = lax.dot_general(parts, onehot, TN, preferred_element_type=F32)
    picked = picked[0 : 2 * CAP] + picked[2 * CAP : 4 * CAP] + picked[4 * CAP : 6 * CAP]
    slot = iota((CAP, ROWS), 0) == rank_ref[...]
    near_ref[...] = jnp.sum(jnp.where(slot, picked[0:CAP], 0.0), axis=0, keepdims=True)
    centre_ref[...] = jnp.sum(jnp.where(slot, picked[CAP:], 0.0), axis=0, keepdims=True)


def struct(shape, dtype):
    return jax.ShapeDtypeStruct(shape, dtype)


def call(kernel, outs, flops, scratch=(), grant=20, **specs):
    return pl.pallas_call(
        kernel,
        out_shape=outs,
        scratch_shapes=list(scratch),
        compiler_params=pltpu.CompilerParams(vmem_limit_bytes=grant * 1024 * 1024),
        cost_estimate=pl.CostEstimate(
            flops=int(flops), bytes_accessed=6_000_000, transcendentals=0
        ),
        **specs,
    )


def shards(embeddings, cluster_ids):
    ids = cluster_ids.reshape(1, ROWS)
    block = 2 * SLOTS * SLOTS * WIDTH
    here = pl.BlockSpec(memory_space=pltpu.VMEM)
    send, rank = call(
        pack_kernel,
        (struct((SLOTS, WIDTH), BF16), struct((1, ROWS), jnp.int32)),
        2 * SLOTS * ROWS * WIDTH,
        (
            pltpu.VMEM((ROWS, WIDTH), BF16),
            pltpu.SemaphoreType.DMA,
            pltpu.VMEM((SLOTS, WIDTH), BF16),
            pltpu.SemaphoreType.DMA((8,)),
        ),
        grant=60,
        in_specs=[here, pl.BlockSpec(memory_space=pltpu.HBM)],
        out_specs=(pl.BlockSpec(memory_space=pltpu.HBM), here),
    )(ids, embeddings)
    chips = ("z", "x", "y")
    mine = lax.all_to_all(send.reshape(CHIPS, CAP, WIDTH), chips, 0, 0, tiled=True)
    mine = mine.reshape(SLOTS, WIDTH)
    swap = [(0, 1), (1, 0)]
    sib = lax.ppermute(mine, "core", swap)
    row = struct((1, SLOTS), F32)
    info, best = call(diagonal_kernel, (struct((3, SLOTS), F32), row), block / 4)(mine)
    sib_info = lax.ppermute(info, "core", swap)
    fold = pltpu.VMEM((TILE, 128), F32)
    best = call(own_kernel, row, block * 3 / 8, (fold,))(mine, info, best)
    out, mean = call(
        rest_kernel,
        (struct((CHIPS, 2 * CAP), F32), struct((1, WIDTH), F32)),
        block,
        (
            pltpu.VMEM((1, SLOTS), F32),
            fold,
            pltpu.VMEM((SLOTS, WIDTH), BF16),
            pltpu.SemaphoreType.DMA((TILES,)),
        ),
        in_specs=[here, pl.BlockSpec(memory_space=pltpu.HBM), here, here, here],
    )(mine, sib, info, sib_info, best)
    back = lax.all_to_all(out, chips, 0, 0, tiled=True)
    x = lax.axis_index("x")
    core = lax.axis_index("core")
    means = jnp.zeros((2, WIDTH), F32)
    for k in range(4):
        came = mean if k == 0 else lax.ppermute(mean, "x", [(i, (i + k) % 4) for i in range(4)])
        place = lax.rem(x - k + 4, 4) - 2 * core
        means = jnp.where(jnp.arange(2)[:, None] == place, came, means)
    near, centre = call(
        unpack_kernel, (struct((1, ROWS), F32), struct((1, ROWS), F32)), 1e8
    )(ids, rank, back)
    return near.reshape(ROWS), centre.reshape(ROWS), means


def solution(mesh):
    fine = Mesh(mesh.devices.reshape(4, 8, 2, 4), ("y", "z", "core", "x"))
    owner = ("y", "z", "core")
    every = owner + ("x",)
    return jax.shard_map(
        shards,
        mesh=fine,
        in_specs=(P(every, None), P(every, None)),
        out_specs=(P(every), P(every), P(owner, None)),
        check_vma=False,
    )
```

```python
import jax
import jax.numpy as jnp
from jax import lax
from jax.experimental import pallas as pl
from jax.experimental.pallas import tpu as pltpu
from jax.sharding import Mesh, PartitionSpec as P

EPS = 1e-06
ROWS = 1024
WIDTH = 768
CAP = 16
CHIPS = 128
SLOTS = CHIPS * CAP
MARK = 64.0
LOW = -1e30
TILE = 512
TILES = SLOTS // TILE
NT = (((1,), (1,)), ((), ()))
TN = (((0,), (0,)), ((), ()))
F32 = jnp.float32
BF16 = jnp.bfloat16


def iota(shape, dim):
    return lax.broadcasted_iota(jnp.int32, shape, dim)


def split3(v):
    hi = v.astype(BF16)
    rest = v - hi.astype(F32)
    mid = rest.astype(BF16)
    lo = (rest - mid.astype(F32)).astype(BF16)
    return hi, mid, lo


def chip_of(ids):
    return ((ids >> 2) & 7) * 16 + (ids & 3) * 4 + (ids >> 5)


def eye(n):
    return iota((n, n), 0) == iota((n, n), 1)


def to_row(column):
    blocks = [
        jnp.sum(jnp.where(eye(128), column[k : k + 128], 0.0), axis=0, keepdims=True)
        for k in range(0, column.shape[0], 128)
    ]
    return jnp.concatenate(blocks, axis=1)


def to_column(row):
    blocks = [
        jnp.sum(jnp.where(eye(128), row[:, k : k + 128], 0.0), axis=1, keepdims=True)
        for k in range(0, row.shape[1], 128)
    ]
    return jnp.concatenate(blocks, axis=0)


def fold_lanes(value):
    best = value[:, 0:128]
    for k in range(128, value.shape[1], 128):
        best = jnp.maximum(best, value[:, k : k + 128])
    return best


def part(ref, i):
    return ref[i * TILE : (i + 1) * TILE, :]


def lanes(ref, row, i):
    return ref[row : row + 1, i * TILE : (i + 1) * TILE]


def pack_kernel(ids_ref, x_ref, send_ref, rank_ref):
    chip = chip_of(ids_ref[...])
    same = iota((CHIPS, ROWS), 0) == chip
    onehot = same.astype(F32).astype(BF16)
    before = (iota((ROWS, ROWS), 0) < iota((ROWS, ROWS), 1)).astype(F32).astype(BF16)
    earlier = jnp.dot(onehot, before, preferred_element_type=F32)
    rank = jnp.sum(jnp.where(same, earlier, 0.0), axis=0, keepdims=True).astype(jnp.int32)
    rank_ref[...] = rank
    position = chip * CAP + rank
    step = 256
    for start in range(0, SLOTS, step):
        pick = (iota((step, ROWS), 0) + start == position).astype(F32)
        live = jnp.sum(pick, axis=1, keepdims=True)
        rows = jnp.dot(pick.astype(BF16), x_ref[...], preferred_element_type=F32)
        mark = jnp.where(iota((step, 128), 1) == 0, (1.0 - live) * MARK, 0.0)
        send_ref[start : start + step, 0:128] = (rows[:, 0:128] + mark).astype(BF16)
        send_ref[start : start + step, 128:] = rows[:, 128:].astype(BF16)


def diagonal_kernel(x_ref, info_ref, best_ref):
    live = to_row((x_ref[:, 0:1].astype(F32) < MARK / 2).astype(F32))
    weights = jnp.broadcast_to(live, (8, SLOTS)).astype(BF16)
    totals = jnp.dot(weights, x_ref[...], preferred_element_type=F32)
    info_ref[1:2, :] = jnp.where(live > 0, 0.0, LOW)
    info_ref[2:3, 0:WIDTH] = totals[0:1]
    count = jnp.sum(live, axis=1, keepdims=True)
    info_ref[2:3, WIDTH:] = jnp.broadcast_to(count, (1, SLOTS - WIDTH))
    for i in range(TILES):
        dots = lax.dot_general(part(x_ref, i), part(x_ref, i), NT, preferred_element_type=F32)
        square = jnp.sum(jnp.where(eye(TILE), dots, 0.0), axis=0, keepdims=True)
        inv = lax.rsqrt(square / WIDTH + EPS)
        info_ref[0:1, i * TILE : (i + 1) * TILE] = inv
        value = jnp.where(eye(TILE), LOW, dots * inv + lanes(info_ref, 1, i))
        best = jnp.max(fold_lanes(value), axis=1, keepdims=True)
        best_ref[:, i * TILE : (i + 1) * TILE] = to_row(best)


def own_kernel(x_ref, info_ref, before_ref, best_ref, fold_ref):
    best_ref[...] = before_ref[...]
    for i in range(TILES - 1):
        inv = to_column(lanes(info_ref, 0, i))
        bias = to_column(lanes(info_ref, 1, i))
        for j in range(i + 1, TILES):
            dots = lax.dot_general(part(x_ref, i), part(x_ref, j), NT, preferred_element_type=F32)
            fold = fold_lanes(dots * lanes(info_ref, 0, j) + lanes(info_ref, 1, j))
            fold_ref[...] = fold if j == i + 1 else jnp.maximum(fold_ref[...], fold)
            down = jnp.max(dots * inv + bias, axis=0, keepdims=True)
            best_ref[:, j * TILE : (j + 1) * TILE] = jnp.maximum(lanes(best_ref, 0, j), down)
        best = to_row(jnp.max(fold_ref[...], axis=1, keepdims=True))
        best_ref[:, i * TILE : (i + 1) * TILE] = jnp.maximum(lanes(best_ref, 0, i), best)


def rest_kernel(
    x_ref, sib_hbm, info_ref, sib_info_ref, best_ref, out_ref, mean_ref, near_ref, fold_ref, sib_ref, sems
):
    copies = [
        pltpu.make_async_copy(part(sib_hbm.at, j), part(sib_ref.at, j), sems.at[j])
        for j in range(TILES)
    ]
    for copy in copies:
        copy.start()
    for copy in copies:
        copy.wait()

    def row(i, _):
        rows = pl.ds(pl.multiple_of(i * TILE, TILE), TILE)
        fold = None
        for j in range(TILES):
            dots = lax.dot_general(x_ref[rows, :], part(sib_ref, j), NT, preferred_element_type=F32)
            value = fold_lanes(dots * lanes(sib_info_ref, 0, j) + lanes(sib_info_ref, 1, j))
            fold = value if j == 0 else jnp.maximum(fold, value)
        best = to_row(jnp.max(fold, axis=1, keepdims=True))
        best = jnp.maximum(best, best_ref[:, rows])
        near_ref[:, rows] = jnp.maximum(-1.0, best * info_ref[0:1, rows] / WIDTH)
        return 0

    lax.fori_loop(0, TILES, row, 0)
    total = info_ref[2:3, 0:WIDTH] + sib_info_ref[2:3, 0:WIDTH]
    count = info_ref[2:3, WIDTH : WIDTH + 1] + sib_info_ref[2:3, WIDTH : WIDTH + 1]
    mean_ref[...] = total / count
    scale = lax.rsqrt(jnp.sum(total * total, axis=1, keepdims=True) / WIDTH + EPS)
    parts = jnp.concatenate(split3(total) + (jnp.zeros((13, WIDTH), BF16),), axis=0)
    toward = lax.dot_general(parts, x_ref[...], NT, preferred_element_type=F32)
    toward = toward[0:1] + toward[1:2] + toward[2:3]
    centre = toward * info_ref[0:1, :] * scale / WIDTH
    slot = lax.rem(iota((CAP, SLOTS), 1), CAP) == iota((CAP, SLOTS), 0)
    near = jnp.where(slot, near_ref[...], 0.0)
    centre = jnp.where(slot, centre, 0.0)
    parts = jnp.concatenate(split3(jnp.concatenate([near, centre], axis=0)), axis=0)
    source = (iota((CHIPS, SLOTS), 1) // CAP == iota((CHIPS, SLOTS), 0)).astype(F32).astype(BF16)
    spread = lax.dot_general(source, parts, NT, preferred_element_type=F32)
    out_ref[...] = (
        spread[:, 0 : 2 * CAP] + spread[:, 2 * CAP : 4 * CAP] + spread[:, 4 * CAP : 6 * CAP]
    )


def unpack_kernel(ids_ref, rank_ref, back_ref, near_ref, centre_ref):
    same = iota((CHIPS, ROWS), 0) == chip_of(ids_ref[...])
    onehot = same.astype(F32).astype(BF16)
    parts = jnp.concatenate(split3(back_ref[...]), axis=1)
    picked = lax.dot_general(parts, onehot, TN, preferred_element_type=F32)
    picked = picked[0 : 2 * CAP] + picked[2 * CAP : 4 * CAP] + picked[4 * CAP : 6 * CAP]
    slot = iota((CAP, ROWS), 0) == rank_ref[...]
    near_ref[...] = jnp.sum(jnp.where(slot, picked[0:CAP], 0.0), axis=0, keepdims=True)
    centre_ref[...] = jnp.sum(jnp.where(slot, picked[CAP:], 0.0), axis=0, keepdims=True)


def struct(shape, dtype):
    return jax.ShapeDtypeStruct(shape, dtype)


def call(kernel, outs, flops, scratch=(), grant=20, **specs):
    return pl.pallas_call(
        kernel,
        out_shape=outs,
        scratch_shapes=list(scratch),
        compiler_params=pltpu.CompilerParams(vmem_limit_bytes=grant * 1024 * 1024),
        cost_estimate=pl.CostEstimate(
            flops=int(flops), bytes_accessed=6_000_000, transcendentals=0
        ),
        **specs,
    )


def shards(embeddings, cluster_ids):
    ids = cluster_ids.reshape(1, ROWS)
    block = 2 * SLOTS * SLOTS * WIDTH
    here = pl.BlockSpec(memory_space=pltpu.VMEM)
    send, rank = call(
        pack_kernel,
        (struct((SLOTS, WIDTH), BF16), struct((1, ROWS), jnp.int32)),
        2 * SLOTS * ROWS * WIDTH,
    )(ids, embeddings)
    chips = ("z", "x", "y")
    mine = lax.all_to_all(send.reshape(CHIPS, CAP, WIDTH), chips, 0, 0, tiled=True)
    mine = mine.reshape(SLOTS, WIDTH)
    swap = [(0, 1), (1, 0)]
    sib = lax.ppermute(mine, "core", swap)
    row = struct((1, SLOTS), F32)
    info, best = call(diagonal_kernel, (struct((3, SLOTS), F32), row), block / 4)(mine)
    sib_info = lax.ppermute(info, "core", swap)
    fold = pltpu.VMEM((TILE, 128), F32)
    best = call(own_kernel, row, block * 3 / 8, (fold,))(mine, info, best)
    out, mean = call(
        rest_kernel,
        (struct((CHIPS, 2 * CAP), F32), struct((1, WIDTH), F32)),
        block,
        (
            pltpu.VMEM((1, SLOTS), F32),
            fold,
            pltpu.VMEM((SLOTS, WIDTH), BF16),
            pltpu.SemaphoreType.DMA((TILES,)),
        ),
        in_specs=[here, pl.BlockSpec(memory_space=pltpu.HBM), here, here, here],
    )(mine, sib, info, sib_info, best)
    back = lax.all_to_all(out, chips, 0, 0, tiled=True)
    x = lax.axis_index("x")
    core = lax.axis_index("core")
    means = jnp.zeros((2, WIDTH), F32)
    for k in range(4):
        came = mean if k == 0 else lax.ppermute(mean, "x", [(i, (i + k) % 4) for i in range(4)])
        place = lax.rem(x - k + 4, 4) - 2 * core
        means = jnp.where(jnp.arange(2)[:, None] == place, came, means)
    near, centre = call(
        unpack_kernel, (struct((1, ROWS), F32), struct((1, ROWS), F32)), 1e8
    )(ids, rank, back)
    return near.reshape(ROWS), centre.reshape(ROWS), means


def solution(mesh):
    fine = Mesh(mesh.devices.reshape(4, 8, 2, 4), ("y", "z", "core", "x"))
    owner = ("y", "z", "core")
    every = owner + ("x",)
    return jax.shard_map(
        shards,
        mesh=fine,
        in_specs=(P(every, None), P(every, None)),
        out_specs=(P(every), P(every), P(owner, None)),
        check_vma=False,
    )
```

```python
import jax
import jax.numpy as jnp
from jax import lax
from jax.experimental import pallas as pl
from jax.experimental.pallas import tpu as pltpu
from jax.sharding import Mesh, PartitionSpec as P

EPS = 1e-06
ROWS = 1024
WIDTH = 768
CAP = 16
CHIPS = 128
SLOTS = CHIPS * CAP
MARK = 64.0
LOW = -1e30
TILE = 512
TILES = SLOTS // TILE
NT = (((1,), (1,)), ((), ()))
TN = (((0,), (0,)), ((), ()))
F32 = jnp.float32
BF16 = jnp.bfloat16


def iota(shape, dim):
    return lax.broadcasted_iota(jnp.int32, shape, dim)


def split3(v):
    hi = v.astype(BF16)
    rest = v - hi.astype(F32)
    mid = rest.astype(BF16)
    lo = (rest - mid.astype(F32)).astype(BF16)
    return hi, mid, lo


def chip_of(ids):
    return ((ids >> 2) & 7) * 16 + (ids & 3) * 4 + (ids >> 5)


def eye(n):
    return iota((n, n), 0) == iota((n, n), 1)


def to_row(column):
    blocks = [
        jnp.sum(jnp.where(eye(128), column[k : k + 128], 0.0), axis=0, keepdims=True)
        for k in range(0, column.shape[0], 128)
    ]
    return jnp.concatenate(blocks, axis=1)


def to_column(row):
    blocks = [
        jnp.sum(jnp.where(eye(128), row[:, k : k + 128], 0.0), axis=1, keepdims=True)
        for k in range(0, row.shape[1], 128)
    ]
    return jnp.concatenate(blocks, axis=0)


def fold_lanes(value):
    best = value[:, 0:128]
    for k in range(128, value.shape[1], 128):
        best = jnp.maximum(best, value[:, k : k + 128])
    return best


def part(ref, i):
    return ref[i * TILE : (i + 1) * TILE, :]


def lanes(ref, row, i):
    return ref[row : row + 1, i * TILE : (i + 1) * TILE]


def pack_kernel(ids_ref, x_hbm, send_ref, rank_ref, x_ref, sem):
    copy = pltpu.make_async_copy(x_hbm, x_ref, sem)
    copy.start()
    chip = chip_of(ids_ref[...])
    same = iota((CHIPS, ROWS), 0) == chip
    onehot = same.astype(F32).astype(BF16)
    before = (iota((ROWS, ROWS), 0) < iota((ROWS, ROWS), 1)).astype(F32).astype(BF16)
    earlier = jnp.dot(onehot, before, preferred_element_type=F32)
    rank = jnp.sum(jnp.where(same, earlier, 0.0), axis=0, keepdims=True).astype(jnp.int32)
    rank_ref[...] = rank
    position = chip * CAP + rank
    step = 256
    copy.wait()
    for start in range(0, SLOTS, step):
        pick = (iota((step, ROWS), 0) + start == position).astype(F32)
        live = jnp.sum(pick, axis=1, keepdims=True)
        rows = jnp.dot(pick.astype(BF16), x_ref[...], preferred_element_type=F32)
        mark = jnp.where(iota((step, 128), 1) == 0, (1.0 - live) * MARK, 0.0)
        send_ref[start : start + step, 0:128] = (rows[:, 0:128] + mark).astype(BF16)
        send_ref[start : start + step, 128:] = rows[:, 128:].astype(BF16)


def diagonal_kernel(x_ref, info_ref, best_ref):
    live = to_row((x_ref[:, 0:1].astype(F32) < MARK / 2).astype(F32))
    weights = jnp.broadcast_to(live, (8, SLOTS)).astype(BF16)
    totals = jnp.dot(weights, x_ref[...], preferred_element_type=F32)
    info_ref[1:2, :] = jnp.where(live > 0, 0.0, LOW)
    info_ref[2:3, 0:WIDTH] = totals[0:1]
    count = jnp.sum(live, axis=1, keepdims=True)
    info_ref[2:3, WIDTH:] = jnp.broadcast_to(count, (1, SLOTS - WIDTH))
    for i in range(TILES):
        dots = lax.dot_general(part(x_ref, i), part(x_ref, i), NT, preferred_element_type=F32)
        square = jnp.sum(jnp.where(eye(TILE), dots, 0.0), axis=0, keepdims=True)
        inv = lax.rsqrt(square / WIDTH + EPS)
        info_ref[0:1, i * TILE : (i + 1) * TILE] = inv
        value = jnp.where(eye(TILE), LOW, dots * inv + lanes(info_ref, 1, i))
        best = jnp.max(fold_lanes(value), axis=1, keepdims=True)
        best_ref[:, i * TILE : (i + 1) * TILE] = to_row(best)


def own_kernel(x_ref, info_ref, before_ref, best_ref, fold_ref):
    best_ref[...] = before_ref[...]
    for i in range(TILES - 1):
        inv = to_column(lanes(info_ref, 0, i))
        bias = to_column(lanes(info_ref, 1, i))
        for j in range(i + 1, TILES):
            dots = lax.dot_general(part(x_ref, i), part(x_ref, j), NT, preferred_element_type=F32)
            fold = fold_lanes(dots * lanes(info_ref, 0, j) + lanes(info_ref, 1, j))
            fold_ref[...] = fold if j == i + 1 else jnp.maximum(fold_ref[...], fold)
            down = jnp.max(dots * inv + bias, axis=0, keepdims=True)
            best_ref[:, j * TILE : (j + 1) * TILE] = jnp.maximum(lanes(best_ref, 0, j), down)
        best = to_row(jnp.max(fold_ref[...], axis=1, keepdims=True))
        best_ref[:, i * TILE : (i + 1) * TILE] = jnp.maximum(lanes(best_ref, 0, i), best)


def rest_kernel(
    x_ref, sib_hbm, info_ref, sib_info_ref, best_ref, out_ref, mean_ref, near_ref, fold_ref, sib_ref, sems
):
    def copy(j):
        rows = slice(j * TILE, (j + 1) * TILE)
        return pltpu.make_async_copy(sib_hbm.at[rows, :], sib_ref.at[rows, :], sems.at[j])

    copy(0).start()
    total = info_ref[2:3, 0:WIDTH] + sib_info_ref[2:3, 0:WIDTH]
    count = info_ref[2:3, WIDTH : WIDTH + 1] + sib_info_ref[2:3, WIDTH : WIDTH + 1]
    mean_ref[...] = total / count
    scale = lax.rsqrt(jnp.sum(total * total, axis=1, keepdims=True) / WIDTH + EPS)
    parts = jnp.concatenate(split3(total) + (jnp.zeros((13, WIDTH), BF16),), axis=0)
    toward = lax.dot_general(parts, x_ref[...], NT, preferred_element_type=F32)
    toward = toward[0:1] + toward[1:2] + toward[2:3]
    centre = toward * info_ref[0:1, :] * scale / WIDTH
    for j in range(TILES):
        copy(j).wait()
        if j + 1 < TILES:
            copy(j + 1).start()
        for i in range(TILES):
            dots = lax.dot_general(part(x_ref, i), part(sib_ref, j), NT, preferred_element_type=F32)
            fold = fold_lanes(dots * lanes(sib_info_ref, 0, j) + lanes(sib_info_ref, 1, j))
            fold = fold if j == 0 else jnp.maximum(part(fold_ref, i), fold)
            if j + 1 < TILES:
                fold_ref[i * TILE : (i + 1) * TILE, :] = fold
            else:
                best = to_row(jnp.max(fold, axis=1, keepdims=True))
                best = jnp.maximum(best, lanes(best_ref, 0, i))
                near_ref[:, i * TILE : (i + 1) * TILE] = jnp.maximum(
                    -1.0, best * lanes(info_ref, 0, i) / WIDTH
                )
    slot = lax.rem(iota((CAP, SLOTS), 1), CAP) == iota((CAP, SLOTS), 0)
    near = jnp.where(slot, near_ref[...], 0.0)
    centre = jnp.where(slot, centre, 0.0)
    parts = jnp.concatenate(split3(jnp.concatenate([near, centre], axis=0)), axis=0)
    source = (iota((CHIPS, SLOTS), 1) // CAP == iota((CHIPS, SLOTS), 0)).astype(F32).astype(BF16)
    spread = lax.dot_general(source, parts, NT, preferred_element_type=F32)
    out_ref[...] = (
        spread[:, 0 : 2 * CAP] + spread[:, 2 * CAP : 4 * CAP] + spread[:, 4 * CAP : 6 * CAP]
    )


def unpack_kernel(ids_ref, rank_ref, back_ref, near_ref, centre_ref):
    same = iota((CHIPS, ROWS), 0) == chip_of(ids_ref[...])
    onehot = same.astype(F32).astype(BF16)
    parts = jnp.concatenate(split3(back_ref[...]), axis=1)
    picked = lax.dot_general(parts, onehot, TN, preferred_element_type=F32)
    picked = picked[0 : 2 * CAP] + picked[2 * CAP : 4 * CAP] + picked[4 * CAP : 6 * CAP]
    slot = iota((CAP, ROWS), 0) == rank_ref[...]
    near_ref[...] = jnp.sum(jnp.where(slot, picked[0:CAP], 0.0), axis=0, keepdims=True)
    centre_ref[...] = jnp.sum(jnp.where(slot, picked[CAP:], 0.0), axis=0, keepdims=True)


def struct(shape, dtype):
    return jax.ShapeDtypeStruct(shape, dtype)


def call(kernel, outs, flops, scratch=(), grant=40, **specs):
    return pl.pallas_call(
        kernel,
        out_shape=outs,
        scratch_shapes=list(scratch),
        compiler_params=pltpu.CompilerParams(vmem_limit_bytes=grant * 1024 * 1024),
        cost_estimate=pl.CostEstimate(
            flops=int(flops), bytes_accessed=6_000_000, transcendentals=0
        ),
        **specs,
    )


def share_means(mean):
    x, core = lax.axis_index("x"), lax.axis_index("core")
    first = [(0, 2), (4, 1), (1, 3), (5, 0), (6, 4), (2, 7), (7, 5), (3, 6)]
    second = [(0, 3), (1, 2), (6, 5), (7, 4)]
    one = lax.ppermute(mean, ("core", "x"), first)
    two = lax.ppermute(mean, ("core", "x"), second)
    near = x // 2 == core
    other = jnp.where(near, mean, two)
    low = lax.rem(x, 2) == 0
    own_low = jnp.where(near, low, ~low)
    return jnp.where(own_low == (jnp.arange(2)[:, None] == 0), other, one)


def shards(embeddings, cluster_ids):
    ids = cluster_ids.reshape(1, ROWS)
    block = 2 * SLOTS * SLOTS * WIDTH
    here = pl.BlockSpec(memory_space=pltpu.VMEM)
    send, rank = call(
        pack_kernel,
        (struct((SLOTS, WIDTH), BF16), struct((1, ROWS), jnp.int32)),
        2 * SLOTS * ROWS * WIDTH,
        (pltpu.VMEM((ROWS, WIDTH), BF16), pltpu.SemaphoreType.DMA),
        in_specs=[here, pl.BlockSpec(memory_space=pltpu.HBM)],
    )(ids, embeddings)
    chips = ("z", "x", "y")
    mine = lax.all_to_all(send.reshape(CHIPS, CAP, WIDTH), chips, 0, 0, tiled=True)
    mine = mine.reshape(SLOTS, WIDTH)
    swap = [(0, 1), (1, 0)]
    sib = lax.ppermute(mine, "core", swap)
    row = struct((1, SLOTS), F32)
    info, best = call(diagonal_kernel, (struct((3, SLOTS), F32), row), block / 4)(mine)
    sib_info = lax.ppermute(info, "core", swap)
    fold = pltpu.VMEM((TILE, 128), F32)
    best = call(own_kernel, row, block * 3 / 8, (fold,))(mine, info, best)
    out, mean = call(
        rest_kernel,
        (struct((CHIPS, 2 * CAP), F32), struct((1, WIDTH), F32)),
        block,
        (
            pltpu.VMEM((1, SLOTS), F32),
            pltpu.VMEM((SLOTS, 128), F32),
            pltpu.VMEM((SLOTS, WIDTH), BF16),
            pltpu.SemaphoreType.DMA((TILES,)),
        ),
        in_specs=[here, pl.BlockSpec(memory_space=pltpu.HBM), here, here, here],
    )(mine, sib, info, sib_info, best)
    back = lax.all_to_all(out, chips, 0, 0, tiled=True)
    means = share_means(mean)
    near, centre = call(
        unpack_kernel, (struct((1, ROWS), F32), struct((1, ROWS), F32)), 1e8
    )(ids, rank, back)
    return near.reshape(ROWS), centre.reshape(ROWS), means


def solution(mesh):
    fine = Mesh(mesh.devices.reshape(4, 8, 2, 4), ("y", "z", "core", "x"))
    owner = ("y", "z", "core")
    every = owner + ("x",)
    return jax.shard_map(
        shards,
        mesh=fine,
        in_specs=(P(every, None), P(every, None)),
        out_specs=(P(every), P(every), P(owner, None)),
        check_vma=False,
    )
```

```python
import jax
import jax.numpy as jnp
from jax import lax
from jax.experimental import pallas as pl
from jax.experimental.pallas import tpu as pltpu
from jax.sharding import Mesh, PartitionSpec as P

EPS = 1e-06
ROWS = 1024
WIDTH = 768
CAP = 16
CHIPS = 128
SLOTS = CHIPS * CAP
MARK = 64.0
LOW = -1e30
TILE = 512
TILES = SLOTS // TILE
NT = (((1,), (1,)), ((), ()))
TN = (((0,), (0,)), ((), ()))
F32 = jnp.float32
BF16 = jnp.bfloat16


def iota(shape, dim):
    return lax.broadcasted_iota(jnp.int32, shape, dim)


def split3(v):
    hi = v.astype(BF16)
    rest = v - hi.astype(F32)
    mid = rest.astype(BF16)
    lo = (rest - mid.astype(F32)).astype(BF16)
    return hi, mid, lo


def chip_of(ids):
    return ((ids >> 2) & 7) * 16 + (ids & 3) * 4 + (ids >> 5)


def eye(n):
    return iota((n, n), 0) == iota((n, n), 1)


def to_row(column):
    blocks = [
        jnp.sum(jnp.where(eye(128), column[k : k + 128], 0.0), axis=0, keepdims=True)
        for k in range(0, column.shape[0], 128)
    ]
    return jnp.concatenate(blocks, axis=1)


def to_column(row):
    blocks = [
        jnp.sum(jnp.where(eye(128), row[:, k : k + 128], 0.0), axis=1, keepdims=True)
        for k in range(0, row.shape[1], 128)
    ]
    return jnp.concatenate(blocks, axis=0)


def fold_lanes(value):
    best = value[:, 0:128]
    for k in range(128, value.shape[1], 128):
        best = jnp.maximum(best, value[:, k : k + 128])
    return best


def part(ref, i):
    return ref[i * TILE : (i + 1) * TILE, :]


def lanes(ref, row, i):
    return ref[row : row + 1, i * TILE : (i + 1) * TILE]


def pack_kernel(ids_ref, x_hbm, send_ref, rank_ref, x_ref, sem):
    copy = pltpu.make_async_copy(x_hbm, x_ref, sem)
    copy.start()
    chip = chip_of(ids_ref[...])
    same = iota((CHIPS, ROWS), 0) == chip
    onehot = same.astype(F32).astype(BF16)
    before = (iota((ROWS, ROWS), 0) < iota((ROWS, ROWS), 1)).astype(F32).astype(BF16)
    earlier = jnp.dot(onehot, before, preferred_element_type=F32)
    rank = jnp.sum(jnp.where(same, earlier, 0.0), axis=0, keepdims=True).astype(jnp.int32)
    rank_ref[...] = rank
    position = chip * CAP + rank
    step = 256
    copy.wait()
    for start in range(0, SLOTS, step):
        pick = (iota((step, ROWS), 0) + start == position).astype(F32)
        live = jnp.sum(pick, axis=1, keepdims=True)
        rows = jnp.dot(pick.astype(BF16), x_ref[...], preferred_element_type=F32)
        mark = jnp.where(iota((step, 128), 1) == 0, (1.0 - live) * MARK, 0.0)
        send_ref[start : start + step, 0:128] = (rows[:, 0:128] + mark).astype(BF16)
        send_ref[start : start + step, 128:] = rows[:, 128:].astype(BF16)


def diagonal_kernel(x_ref, info_ref, best_ref):
    live = to_row((x_ref[:, 0:1].astype(F32) < MARK / 2).astype(F32))
    weights = jnp.broadcast_to(live, (8, SLOTS)).astype(BF16)
    totals = jnp.dot(weights, x_ref[...], preferred_element_type=F32)
    info_ref[1:2, :] = jnp.where(live > 0, 0.0, LOW)
    info_ref[2:3, 0:WIDTH] = totals[0:1]
    count = jnp.sum(live, axis=1, keepdims=True)
    info_ref[2:3, WIDTH:] = jnp.broadcast_to(count, (1, SLOTS - WIDTH))
    for i in range(TILES):
        dots = lax.dot_general(part(x_ref, i), part(x_ref, i), NT, preferred_element_type=F32)
        square = jnp.sum(jnp.where(eye(TILE), dots, 0.0), axis=0, keepdims=True)
        inv = lax.rsqrt(square / WIDTH + EPS)
        info_ref[0:1, i * TILE : (i + 1) * TILE] = inv
        value = jnp.where(eye(TILE), LOW, dots * inv + lanes(info_ref, 1, i))
        best = jnp.max(fold_lanes(value), axis=1, keepdims=True)
        best_ref[:, i * TILE : (i + 1) * TILE] = to_row(best)


def own_kernel(x_ref, info_ref, before_ref, best_ref, fold_ref):
    best_ref[...] = before_ref[...]
    for i in range(TILES - 1):
        inv = to_column(lanes(info_ref, 0, i))
        bias = to_column(lanes(info_ref, 1, i))
        for j in range(i + 1, TILES):
            dots = lax.dot_general(part(x_ref, i), part(x_ref, j), NT, preferred_element_type=F32)
            fold = fold_lanes(dots * lanes(info_ref, 0, j) + lanes(info_ref, 1, j))
            fold_ref[...] = fold if j == i + 1 else jnp.maximum(fold_ref[...], fold)
            down = jnp.max(dots * inv + bias, axis=0, keepdims=True)
            best_ref[:, j * TILE : (j + 1) * TILE] = jnp.maximum(lanes(best_ref, 0, j), down)
        best = to_row(jnp.max(fold_ref[...], axis=1, keepdims=True))
        best_ref[:, i * TILE : (i + 1) * TILE] = jnp.maximum(lanes(best_ref, 0, i), best)


def across_kernel(
    core_ref, x_ref, sib_hbm, info_ref, sib_info_ref, before_ref, best_ref, give_ref, fold_ref, sib_ref, sems
):
    core = core_ref[0, 0]

    def rows(k):
        return pl.ds(pl.multiple_of(((core + k) & 3) * TILE, TILE), TILE)

    def copy(k):
        return pltpu.make_async_copy(
            sib_hbm.at[rows(k), :], sib_ref.at[rows(k), :], sems.at[k]
        )

    copy(0).start()
    copy(2).start()
    give_ref[...] = jnp.full((1, SLOTS), LOW, F32)
    for i in range(TILES):
        inv = to_column(lanes(info_ref, 0, i))
        bias = to_column(lanes(info_ref, 1, i))
        fold = None
        for k in (i, i + 2):
            if i < 2:
                copy(k).wait()
                if i == 0:
                    copy(k + 1).start()
            other = rows(k)
            dots = lax.dot_general(
                part(x_ref, i), sib_ref[other, :], NT, preferred_element_type=F32
            )
            value = fold_lanes(dots * sib_info_ref[0:1, other] + sib_info_ref[1:2, other])
            fold = value if fold is None else jnp.maximum(fold, value)
            down = jnp.max(dots * inv + bias, axis=0, keepdims=True)
            give_ref[:, other] = jnp.maximum(give_ref[:, other], down)
        best = to_row(jnp.max(fold, axis=1, keepdims=True))
        best_ref[:, i * TILE : (i + 1) * TILE] = jnp.maximum(lanes(before_ref, 0, i), best)


def centre_kernel(after_ref, x_ref, info_ref, sib_info_ref, centre_ref, mean_ref):
    total = info_ref[2:3, 0:WIDTH] + sib_info_ref[2:3, 0:WIDTH]
    count = info_ref[2:3, WIDTH : WIDTH + 1] + sib_info_ref[2:3, WIDTH : WIDTH + 1]
    mean_ref[...] = total / count
    scale = lax.rsqrt(jnp.sum(total * total, axis=1, keepdims=True) / WIDTH + EPS)
    parts = jnp.concatenate(split3(total) + (jnp.zeros((13, WIDTH), BF16),), axis=0)
    toward = lax.dot_general(parts, x_ref[...], NT, preferred_element_type=F32)
    toward = toward[0:1] + toward[1:2] + toward[2:3]
    centre_ref[...] = toward * info_ref[0:1, :] * scale / WIDTH


def spread_kernel(best_ref, taken_ref, centre_ref, info_ref, out_ref):
    best = jnp.maximum(best_ref[...], taken_ref[...])
    near = jnp.maximum(-1.0, best * info_ref[0:1, :] / WIDTH)
    slot = lax.rem(iota((CAP, SLOTS), 1), CAP) == iota((CAP, SLOTS), 0)
    near = jnp.where(slot, near, 0.0)
    centre = jnp.where(slot, centre_ref[...], 0.0)
    parts = jnp.concatenate(split3(jnp.concatenate([near, centre], axis=0)), axis=0)
    source = (iota((CHIPS, SLOTS), 1) // CAP == iota((CHIPS, SLOTS), 0)).astype(F32).astype(BF16)
    spread = lax.dot_general(source, parts, NT, preferred_element_type=F32)
    out_ref[...] = (
        spread[:, 0 : 2 * CAP] + spread[:, 2 * CAP : 4 * CAP] + spread[:, 4 * CAP : 6 * CAP]
    )


def unpack_kernel(ids_ref, rank_ref, back_ref, near_ref, centre_ref):
    same = iota((CHIPS, ROWS), 0) == chip_of(ids_ref[...])
    onehot = same.astype(F32).astype(BF16)
    parts = jnp.concatenate(split3(back_ref[...]), axis=1)
    picked = lax.dot_general(parts, onehot, TN, preferred_element_type=F32)
    picked = picked[0 : 2 * CAP] + picked[2 * CAP : 4 * CAP] + picked[4 * CAP : 6 * CAP]
    slot = iota((CAP, ROWS), 0) == rank_ref[...]
    near_ref[...] = jnp.sum(jnp.where(slot, picked[0:CAP], 0.0), axis=0, keepdims=True)
    centre_ref[...] = jnp.sum(jnp.where(slot, picked[CAP:], 0.0), axis=0, keepdims=True)


def struct(shape, dtype):
    return jax.ShapeDtypeStruct(shape, dtype)


def call(kernel, outs, flops, scratch=(), grant=40, **specs):
    return pl.pallas_call(
        kernel,
        out_shape=outs,
        scratch_shapes=list(scratch),
        compiler_params=pltpu.CompilerParams(vmem_limit_bytes=grant * 1024 * 1024),
        cost_estimate=pl.CostEstimate(
            flops=int(flops), bytes_accessed=6_000_000, transcendentals=0
        ),
        **specs,
    )


def share_means(mean):
    x, core = lax.axis_index("x"), lax.axis_index("core")
    first = [(0, 2), (4, 1), (1, 3), (5, 0), (6, 4), (2, 7), (7, 5), (3, 6)]
    second = [(0, 3), (1, 2), (6, 5), (7, 4)]
    one = lax.ppermute(mean, ("core", "x"), first)
    two = lax.ppermute(mean, ("core", "x"), second)
    near = x // 2 == core
    other = jnp.where(near, mean, two)
    low = lax.rem(x, 2) == 0
    own_low = jnp.where(near, low, ~low)
    return jnp.where(own_low == (jnp.arange(2)[:, None] == 0), other, one)


def shards(embeddings, cluster_ids):
    ids = cluster_ids.reshape(1, ROWS)
    block = 2 * SLOTS * SLOTS * WIDTH
    here = pl.BlockSpec(memory_space=pltpu.VMEM)
    send, rank = call(
        pack_kernel,
        (struct((SLOTS, WIDTH), BF16), struct((1, ROWS), jnp.int32)),
        2 * SLOTS * ROWS * WIDTH,
        (pltpu.VMEM((ROWS, WIDTH), BF16), pltpu.SemaphoreType.DMA),
        in_specs=[here, pl.BlockSpec(memory_space=pltpu.HBM)],
    )(ids, embeddings)
    chips = ("z", "x", "y")
    mine = lax.all_to_all(send.reshape(CHIPS, CAP, WIDTH), chips, 0, 0, tiled=True)
    mine = mine.reshape(SLOTS, WIDTH)
    swap = [(0, 1), (1, 0)]
    sib = lax.ppermute(mine, "core", swap)
    row = struct((1, SLOTS), F32)
    info, best = call(diagonal_kernel, (struct((3, SLOTS), F32), row), block / 4)(mine)
    sib_info = lax.ppermute(info, "core", swap)
    fold = pltpu.VMEM((TILE, 128), F32)
    best = call(own_kernel, row, block * 3 / 8, (fold,))(mine, info, best)
    core = lax.axis_index("core").astype(jnp.int32).reshape(1, 1)
    best, give = call(
        across_kernel,
        (row, row),
        block / 2,
        (
            fold,
            pltpu.VMEM((SLOTS, WIDTH), BF16),
            pltpu.SemaphoreType.DMA((TILES,)),
        ),
        in_specs=[
            pl.BlockSpec(memory_space=pltpu.SMEM), here, pl.BlockSpec(memory_space=pltpu.HBM),
            here, here, here,
        ],
    )(core, mine, sib, info, sib_info, best)
    taken = lax.ppermute(give, "core", swap)
    centre, mean = call(
        centre_kernel, (row, struct((1, WIDTH), F32)), block / 8
    )(give, mine, info, sib_info)
    out = call(spread_kernel, struct((CHIPS, 2 * CAP), F32), 1e8)(best, taken, centre, info)
    back = lax.all_to_all(out, chips, 0, 0, tiled=True)
    means = share_means(mean)
    near, centre = call(
        unpack_kernel, (struct((1, ROWS), F32), struct((1, ROWS), F32)), 1e8
    )(ids, rank, back)
    return near.reshape(ROWS), centre.reshape(ROWS), means


def solution(mesh):
    fine = Mesh(mesh.devices.reshape(4, 8, 2, 4), ("y", "z", "core", "x"))
    owner = ("y", "z", "core")
    every = owner + ("x",)
    return jax.shard_map(
        shards,
        mesh=fine,
        in_specs=(P(every, None), P(every, None)),
        out_specs=(P(every), P(every), P(owner, None)),
        check_vma=False,
    )
```

```python
import jax
import jax.numpy as jnp
from jax import lax
from jax.experimental import pallas as pl
from jax.experimental.pallas import tpu as pltpu
from jax.sharding import Mesh, PartitionSpec as P

EPS = 1e-06
ROWS = 1024
WIDTH = 768
CAP = 16
CHIPS = 128
XS = 4
PAIR = 2 * CAP
SLOTS = CHIPS * CAP
MARK = 64.0
LOW = -1e30
TILE = 512
TILES = SLOTS // TILE
NT = (((1,), (1,)), ((), ()))
TN = (((0,), (0,)), ((), ()))
F32 = jnp.float32
BF16 = jnp.bfloat16


def iota(shape, dim):
    return lax.broadcasted_iota(jnp.int32, shape, dim)


def split3(v):
    hi = v.astype(BF16)
    rest = v - hi.astype(F32)
    mid = rest.astype(BF16)
    lo = (rest - mid.astype(F32)).astype(BF16)
    return hi, mid, lo


def chip_of(ids):
    return ((ids >> 2) & 7) * 16 + (ids & 3) * 4 + (ids >> 5)


def eye(n):
    return iota((n, n), 0) == iota((n, n), 1)


def to_row(column):
    blocks = [
        jnp.sum(jnp.where(eye(128), column[k : k + 128], 0.0), axis=0, keepdims=True)
        for k in range(0, column.shape[0], 128)
    ]
    return jnp.concatenate(blocks, axis=1)


def to_column(row):
    blocks = [
        jnp.sum(jnp.where(eye(128), row[:, k : k + 128], 0.0), axis=1, keepdims=True)
        for k in range(0, row.shape[1], 128)
    ]
    return jnp.concatenate(blocks, axis=0)


def fold_lanes(value):
    best = value[:, 0:128]
    for k in range(128, value.shape[1], 128):
        best = jnp.maximum(best, value[:, k : k + 128])
    return best


def part(ref, i):
    return ref[i * TILE : (i + 1) * TILE, :]


def lanes(ref, row, i):
    return ref[row : row + 1, i * TILE : (i + 1) * TILE]


def pack_kernel(ids_ref, x_hbm, send_ref, rank_ref, x_ref, sem):
    copy = pltpu.make_async_copy(x_hbm, x_ref, sem)
    copy.start()
    chip = chip_of(ids_ref[...])
    same = iota((CHIPS, ROWS), 0) == chip
    onehot = same.astype(F32).astype(BF16)
    before = (iota((ROWS, ROWS), 0) < iota((ROWS, ROWS), 1)).astype(F32).astype(BF16)
    earlier = jnp.dot(onehot, before, preferred_element_type=F32)
    rank = jnp.sum(jnp.where(same, earlier, 0.0), axis=0, keepdims=True).astype(jnp.int32)
    rank_ref[...] = rank
    position = chip * CAP + rank
    step = 256
    copy.wait()
    for start in range(0, SLOTS, step):
        pick = (iota((step, ROWS), 0) + start == position).astype(F32)
        live = jnp.sum(pick, axis=1, keepdims=True)
        rows = jnp.dot(pick.astype(BF16), x_ref[...], preferred_element_type=F32)
        mark = jnp.where(iota((step, 128), 1) == 0, (1.0 - live) * MARK, 0.0)
        send_ref[start : start + step, 0:128] = (rows[:, 0:128] + mark).astype(BF16)
        send_ref[start : start + step, 128:] = rows[:, 128:].astype(BF16)


def diagonal_kernel(x_ref, info_ref, best_ref):
    live = to_row((x_ref[:, 0:1].astype(F32) < MARK / 2).astype(F32))
    weights = jnp.broadcast_to(live, (8, SLOTS)).astype(BF16)
    totals = jnp.dot(weights, x_ref[...], preferred_element_type=F32)
    info_ref[1:2, :] = jnp.where(live > 0, 0.0, LOW)
    info_ref[2:3, 0:WIDTH] = totals[0:1]
    count = jnp.sum(live, axis=1, keepdims=True)
    info_ref[2:3, WIDTH:] = jnp.broadcast_to(count, (1, SLOTS - WIDTH))
    for i in range(TILES):
        dots = lax.dot_general(part(x_ref, i), part(x_ref, i), NT, preferred_element_type=F32)
        square = jnp.sum(jnp.where(eye(TILE), dots, 0.0), axis=0, keepdims=True)
        inv = lax.rsqrt(square / WIDTH + EPS)
        info_ref[0:1, i * TILE : (i + 1) * TILE] = inv
        value = jnp.where(eye(TILE), LOW, dots * inv + lanes(info_ref, 1, i))
        best = jnp.max(fold_lanes(value), axis=1, keepdims=True)
        best_ref[:, i * TILE : (i + 1) * TILE] = to_row(best)


def own_kernel(x_ref, info_ref, before_ref, best_ref, fold_ref):
    best_ref[...] = before_ref[...]
    for i in range(TILES - 1):
        inv = to_column(lanes(info_ref, 0, i))
        bias = to_column(lanes(info_ref, 1, i))
        for j in range(i + 1, TILES):
            dots = lax.dot_general(part(x_ref, i), part(x_ref, j), NT, preferred_element_type=F32)
            fold = fold_lanes(dots * lanes(info_ref, 0, j) + lanes(info_ref, 1, j))
            fold_ref[...] = fold if j == i + 1 else jnp.maximum(fold_ref[...], fold)
            down = jnp.max(dots * inv + bias, axis=0, keepdims=True)
            best_ref[:, j * TILE : (j + 1) * TILE] = jnp.maximum(lanes(best_ref, 0, j), down)
        best = to_row(jnp.max(fold_ref[...], axis=1, keepdims=True))
        best_ref[:, i * TILE : (i + 1) * TILE] = jnp.maximum(lanes(best_ref, 0, i), best)


def rest_kernel(
    place_ref, x_ref, sib_hbm, info_ref, sib_info_ref, best_ref, *refs
):
    out_refs, (near_ref, fold_ref, sib_ref, sems) = refs[:XS], refs[XS:]

    def copy(j):
        rows = slice(j * TILE, (j + 1) * TILE)
        return pltpu.make_async_copy(sib_hbm.at[rows, :], sib_ref.at[rows, :], sems.at[j])

    copy(0).start()
    total = info_ref[2:3, 0:WIDTH] + sib_info_ref[2:3, 0:WIDTH]
    count = info_ref[2:3, WIDTH : WIDTH + 1] + sib_info_ref[2:3, WIDTH : WIDTH + 1]
    mean = total / count
    scale = lax.rsqrt(jnp.sum(total * total, axis=1, keepdims=True) / WIDTH + EPS)
    parts = jnp.concatenate(split3(total) + (jnp.zeros((13, WIDTH), BF16),), axis=0)
    toward = lax.dot_general(parts, x_ref[...], NT, preferred_element_type=F32)
    toward = toward[0:1] + toward[1:2] + toward[2:3]
    centre = toward * info_ref[0:1, :] * scale / WIDTH
    for j in range(TILES):
        copy(j).wait()
        if j + 1 < TILES:
            copy(j + 1).start()
        for i in range(TILES):
            dots = lax.dot_general(part(x_ref, i), part(sib_ref, j), NT, preferred_element_type=F32)
            fold = fold_lanes(dots * lanes(sib_info_ref, 0, j) + lanes(sib_info_ref, 1, j))
            fold = fold if j == 0 else jnp.maximum(part(fold_ref, i), fold)
            if j + 1 < TILES:
                fold_ref[i * TILE : (i + 1) * TILE, :] = fold
            else:
                best = to_row(jnp.max(fold, axis=1, keepdims=True))
                best = jnp.maximum(best, lanes(best_ref, 0, i))
                near_ref[:, i * TILE : (i + 1) * TILE] = jnp.maximum(
                    -1.0, best * lanes(info_ref, 0, i) / WIDTH
                )
    slot = lax.rem(iota((CAP, SLOTS), 1), CAP) == iota((CAP, SLOTS), 0)
    near = jnp.where(slot, near_ref[...], 0.0)
    centre = jnp.where(slot, centre, 0.0)
    parts = jnp.concatenate(split3(jnp.concatenate([near, centre], axis=0)), axis=0)
    here = place_ref[0, 0]
    chip = iota((1, SLOTS), 1) // CAP
    row = (((chip >> 2) - here) & 3) * 32 + (chip >> 4) * 4 + (chip & 3)
    source = (row == iota((CHIPS, SLOTS), 0)).astype(F32).astype(BF16)
    spread = lax.dot_general(source, parts, NT, preferred_element_type=F32)
    spread = spread[:, 0:PAIR] + spread[:, PAIR : 2 * PAIR] + spread[:, 2 * PAIR : 3 * PAIR]
    spread = jnp.concatenate([spread] * XS, axis=1)
    spread = jnp.where(iota((CHIPS, XS * PAIR), 1) // PAIR == here, spread, 0.0)
    folded = [mean[:, k : k + 128] for k in range(0, WIDTH, 128)]
    folded = jnp.concatenate(folded + [jnp.zeros((2, 128), F32)], axis=0)
    for k in range(XS):
        out_refs[k][0:32, :] = spread[32 * k : 32 * (k + 1)]
        out_refs[k][32:40, :] = folded


def merge_kernel(place_ref, *refs):
    came, (out_ref, mean_ref) = refs[:XS], refs[XS:]
    out_ref[...] = sum(ref[0:32, :] for ref in came)
    for k in range(2):
        offset = (place_ref[0, 0] - 2 * place_ref[0, 1] - k) & 3
        folded = sum(jnp.where(offset == i, ref[32:40, :], 0.0) for i, ref in enumerate(came))
        for j in range(WIDTH // 128):
            mean_ref[k : k + 1, j * 128 : (j + 1) * 128] = folded[j : j + 1]


def unpack_kernel(ids_ref, rank_ref, back_ref, near_ref, centre_ref):
    ids = ids_ref[...]
    same = iota((32, ROWS), 0) == ((ids >> 2) & 7) * 4 + (ids >> 5)
    onehot = same.astype(F32).astype(BF16)
    parts = jnp.concatenate(split3(back_ref[...]), axis=1)
    picked = lax.dot_general(parts, onehot, TN, preferred_element_type=F32)
    picked = picked[0:128] + picked[128:256] + picked[256:384]
    place = (ids & 3) * PAIR + rank_ref[...]
    line = iota((128, ROWS), 0)
    near_ref[...] = jnp.sum(jnp.where(line == place, picked, 0.0), axis=0, keepdims=True)
    centre_ref[...] = jnp.sum(
        jnp.where(line == place + CAP, picked, 0.0), axis=0, keepdims=True
    )


def struct(shape, dtype):
    return jax.ShapeDtypeStruct(shape, dtype)


def call(kernel, outs, flops, scratch=(), grant=40, **specs):
    return pl.pallas_call(
        kernel,
        out_shape=outs,
        scratch_shapes=list(scratch),
        compiler_params=pltpu.CompilerParams(vmem_limit_bytes=grant * 1024 * 1024),
        cost_estimate=pl.CostEstimate(
            flops=int(flops), bytes_accessed=6_000_000, transcendentals=0
        ),
        **specs,
    )


def shards(embeddings, cluster_ids):
    ids = cluster_ids.reshape(1, ROWS)
    block = 2 * SLOTS * SLOTS * WIDTH
    here = pl.BlockSpec(memory_space=pltpu.VMEM)
    send, rank = call(
        pack_kernel,
        (struct((SLOTS, WIDTH), BF16), struct((1, ROWS), jnp.int32)),
        2 * SLOTS * ROWS * WIDTH,
        (pltpu.VMEM((ROWS, WIDTH), BF16), pltpu.SemaphoreType.DMA),
        in_specs=[here, pl.BlockSpec(memory_space=pltpu.HBM)],
    )(ids, embeddings)
    chips = ("z", "x", "y")
    mine = lax.all_to_all(send.reshape(CHIPS, CAP, WIDTH), chips, 0, 0, tiled=True)
    mine = mine.reshape(SLOTS, WIDTH)
    swap = [(0, 1), (1, 0)]
    sib = lax.ppermute(mine, "core", swap)
    row = struct((1, SLOTS), F32)
    info, best = call(diagonal_kernel, (struct((3, SLOTS), F32), row), block / 4)(mine)
    sib_info = lax.ppermute(info, "core", swap)
    fold = pltpu.VMEM((TILE, 128), F32)
    best = call(own_kernel, row, block * 3 / 8, (fold,))(mine, info, best)
    axes = [lax.axis_index("x"), lax.axis_index("core")]
    place = jnp.stack(axes).astype(jnp.int32).reshape(1, 2)
    scalars = pl.BlockSpec(memory_space=pltpu.SMEM)
    line = struct((40, 128), F32)
    outs = call(
        rest_kernel,
        (line,) * XS,
        block,
        (
            pltpu.VMEM((1, SLOTS), F32),
            pltpu.VMEM((SLOTS, 128), F32),
            pltpu.VMEM((SLOTS, WIDTH), BF16),
            pltpu.SemaphoreType.DMA((TILES,)),
        ),
        in_specs=[scalars, here, pl.BlockSpec(memory_space=pltpu.HBM), here, here, here],
    )(place, mine, sib, info, sib_info, best)
    came = [outs[0]]
    for k in range(1, XS):
        came.append(lax.ppermute(outs[k], "x", [(i, (i + k) % XS) for i in range(XS)]))
    out, means = call(
        merge_kernel,
        (struct((32, 128), F32), struct((2, WIDTH), F32)),
        1e6,
        in_specs=[scalars] + [here] * XS,
    )(place, *came)
    back = lax.all_to_all(out, ("z", "y"), 0, 0, tiled=True)
    near, centre = call(
        unpack_kernel, (struct((1, ROWS), F32), struct((1, ROWS), F32)), 1e8
    )(ids, rank, back)
    return near.reshape(ROWS), centre.reshape(ROWS), means


def solution(mesh):
    fine = Mesh(mesh.devices.reshape(4, 8, 2, 4), ("y", "z", "core", "x"))
    owner = ("y", "z", "core")
    every = owner + ("x",)
    return jax.shard_map(
        shards,
        mesh=fine,
        in_specs=(P(every, None), P(every, None)),
        out_specs=(P(every), P(every), P(owner, None)),
        check_vma=False,
    )
```

```python
import jax
import jax.numpy as jnp
from jax import lax
from jax.experimental import pallas as pl
from jax.experimental.pallas import tpu as pltpu
from jax.sharding import Mesh, PartitionSpec as P

EPS = 1e-06
ROWS = 1024
WIDTH = 768
CAP = 16
CHIPS = 128
XS = 4
PAIR = 2 * CAP
SLOTS = CHIPS * CAP
MARK = 64.0
LOW = -1e30
TILE = 512
TILES = SLOTS // TILE
NT = (((1,), (1,)), ((), ()))
TN = (((0,), (0,)), ((), ()))
F32 = jnp.float32
BF16 = jnp.bfloat16


def iota(shape, dim):
    return lax.broadcasted_iota(jnp.int32, shape, dim)


def split3(v):
    hi = v.astype(BF16)
    rest = v - hi.astype(F32)
    mid = rest.astype(BF16)
    lo = (rest - mid.astype(F32)).astype(BF16)
    return hi, mid, lo


def chip_of(ids):
    return ((ids >> 2) & 7) * 16 + (ids & 3) * 4 + (ids >> 5)


def eye(n):
    return iota((n, n), 0) == iota((n, n), 1)


def to_row(column):
    blocks = [
        jnp.sum(jnp.where(eye(128), column[k : k + 128], 0.0), axis=0, keepdims=True)
        for k in range(0, column.shape[0], 128)
    ]
    return jnp.concatenate(blocks, axis=1)


def to_column(row):
    blocks = [
        jnp.sum(jnp.where(eye(128), row[:, k : k + 128], 0.0), axis=1, keepdims=True)
        for k in range(0, row.shape[1], 128)
    ]
    return jnp.concatenate(blocks, axis=0)


def fold_lanes(value):
    best = value[:, 0:128]
    for k in range(128, value.shape[1], 128):
        best = jnp.maximum(best, value[:, k : k + 128])
    return best


def part(ref, i):
    return ref[i * TILE : (i + 1) * TILE, :]


def lanes(ref, row, i):
    return ref[row : row + 1, i * TILE : (i + 1) * TILE]


def pack_kernel(ids_ref, x_hbm, send_ref, rank_ref, x_ref, sem):
    copy = pltpu.make_async_copy(x_hbm, x_ref, sem)
    copy.start()
    chip = chip_of(ids_ref[...])
    same = iota((CHIPS, ROWS), 0) == chip
    onehot = same.astype(F32).astype(BF16)
    before = (iota((ROWS, ROWS), 0) < iota((ROWS, ROWS), 1)).astype(F32).astype(BF16)
    earlier = jnp.dot(onehot, before, preferred_element_type=F32)
    rank = jnp.sum(jnp.where(same, earlier, 0.0), axis=0, keepdims=True).astype(jnp.int32)
    rank_ref[...] = rank
    position = chip * CAP + rank
    step = 256
    copy.wait()
    for start in range(0, SLOTS, step):
        pick = (iota((step, ROWS), 0) + start == position).astype(F32)
        live = jnp.sum(pick, axis=1, keepdims=True)
        rows = jnp.dot(pick.astype(BF16), x_ref[...], preferred_element_type=F32)
        mark = jnp.where(iota((step, 128), 1) == 0, (1.0 - live) * MARK, 0.0)
        send_ref[start : start + step, 0:128] = (rows[:, 0:128] + mark).astype(BF16)
        send_ref[start : start + step, 128:] = rows[:, 128:].astype(BF16)


def diagonal_kernel(x_ref, info_ref, best_ref):
    live = to_row((x_ref[:, 0:1].astype(F32) < MARK / 2).astype(F32))
    weights = jnp.broadcast_to(live, (8, SLOTS)).astype(BF16)
    totals = jnp.dot(weights, x_ref[...], preferred_element_type=F32)
    info_ref[1:2, :] = jnp.where(live > 0, 0.0, LOW)
    info_ref[2:3, 0:WIDTH] = totals[0:1]
    count = jnp.sum(live, axis=1, keepdims=True)
    info_ref[2:3, WIDTH:] = jnp.broadcast_to(count, (1, SLOTS - WIDTH))
    for i in range(TILES):
        dots = lax.dot_general(part(x_ref, i), part(x_ref, i), NT, preferred_element_type=F32)
        square = jnp.sum(jnp.where(eye(TILE), dots, 0.0), axis=0, keepdims=True)
        inv = lax.rsqrt(square / WIDTH + EPS)
        info_ref[0:1, i * TILE : (i + 1) * TILE] = inv
        value = jnp.where(eye(TILE), LOW, dots * inv + lanes(info_ref, 1, i))
        best = jnp.max(fold_lanes(value), axis=1, keepdims=True)
        best_ref[:, i * TILE : (i + 1) * TILE] = to_row(best)


def own_kernel(x_ref, info_ref, before_ref, best_ref, fold_ref):
    best_ref[...] = before_ref[...]
    for i in range(TILES - 2):
        inv = to_column(lanes(info_ref, 0, i))
        bias = to_column(lanes(info_ref, 1, i))
        for j in range(i + 1, TILES):
            dots = lax.dot_general(part(x_ref, i), part(x_ref, j), NT, preferred_element_type=F32)
            fold = fold_lanes(dots * lanes(info_ref, 0, j) + lanes(info_ref, 1, j))
            fold_ref[...] = fold if j == i + 1 else jnp.maximum(fold_ref[...], fold)
            down = jnp.max(dots * inv + bias, axis=0, keepdims=True)
            best_ref[:, j * TILE : (j + 1) * TILE] = jnp.maximum(lanes(best_ref, 0, j), down)
        best = to_row(jnp.max(fold_ref[...], axis=1, keepdims=True))
        best_ref[:, i * TILE : (i + 1) * TILE] = jnp.maximum(lanes(best_ref, 0, i), best)


def across_kernel(
    place_ref, x_ref, sib_hbm, info_ref, sib_info_ref, before_ref,
    best_ref, give_ref, centre_ref, mean_ref, sib_ref, turned_ref, sems,
):
    core = place_ref[0, 1]

    def rows(k):
        return pl.ds(pl.multiple_of(((core + k) & 3) * TILE, TILE), TILE)

    def copy(k):
        return pltpu.make_async_copy(
            sib_hbm.at[rows(k), :], sib_ref.at[k * TILE : (k + 1) * TILE, :], sems.at[k]
        )

    copy(0).start()
    copy(2).start()
    for k in range(TILES):
        turned_ref[:, k * TILE : (k + 1) * TILE] = sib_info_ref[0:2, rows(k)]
    total = info_ref[2:3, 0:WIDTH] + sib_info_ref[2:3, 0:WIDTH]
    count = info_ref[2:3, WIDTH : WIDTH + 1] + sib_info_ref[2:3, WIDTH : WIDTH + 1]
    mean_ref[...] = total / count
    scale = lax.rsqrt(jnp.sum(total * total, axis=1, keepdims=True) / WIDTH + EPS)
    parts = jnp.concatenate(split3(total) + (jnp.zeros((13, WIDTH), BF16),), axis=0)
    toward = lax.dot_general(parts, x_ref[...], NT, preferred_element_type=F32)
    toward = toward[0:1] + toward[1:2] + toward[2:3]
    centre_ref[...] = toward * info_ref[0:1, :] * scale / WIDTH
    columns = [
        (to_column(lanes(info_ref, 0, i)), to_column(lanes(info_ref, 1, i))) for i in range(TILES)
    ]

    def both(i, other, row, bias):
        dots = lax.dot_general(part(x_ref, i), other, NT, preferred_element_type=F32)
        down = jnp.max(dots * columns[i][0] + columns[i][1], axis=0, keepdims=True)
        return fold_lanes(dots * row + bias), down

    i, j = TILES - 2, TILES - 1
    last, own = both(i, part(x_ref, j), lanes(info_ref, 0, j), lanes(info_ref, 1, j))
    give = {}
    for i in range(TILES):
        if i == 0:
            copy(0).wait()
            copy(2).wait()
            copy(1).start()
            copy(3).start()
        if i == 1:
            copy(1).wait()
            copy(3).wait()
        fold = last if i == TILES - 2 else None
        for k in (i, (i + 2) % TILES):
            value, down = both(i, part(sib_ref, k), lanes(turned_ref, 0, k), lanes(turned_ref, 1, k))
            fold = value if fold is None else jnp.maximum(fold, value)
            give[k] = jnp.maximum(give[k], down) if k in give else down
        best = jnp.maximum(
            lanes(before_ref, 0, i), to_row(jnp.max(fold, axis=1, keepdims=True))
        )
        if i == TILES - 1:
            best = jnp.maximum(best, own)
        best_ref[:, i * TILE : (i + 1) * TILE] = best
    for k in range(TILES):
        give_ref[:, rows(k)] = give[k]


def spread_kernel(place_ref, best_ref, taken_ref, info_ref, centre_ref, mean_ref, *out_refs):
    best = jnp.maximum(best_ref[...], taken_ref[...])
    near = jnp.maximum(-1.0, best * info_ref[0:1, :] / WIDTH)
    mean = mean_ref[...]
    slot = lax.rem(iota((CAP, SLOTS), 1), CAP) == iota((CAP, SLOTS), 0)
    near = jnp.where(slot, near, 0.0)
    centre = jnp.where(slot, centre_ref[...], 0.0)
    parts = jnp.concatenate(split3(jnp.concatenate([near, centre], axis=0)), axis=0)
    here = place_ref[0, 0]
    chip = iota((1, SLOTS), 1) // CAP
    row = (((chip >> 2) - here) & 3) * 32 + (chip >> 4) * 4 + (chip & 3)
    source = (row == iota((CHIPS, SLOTS), 0)).astype(F32).astype(BF16)
    spread = lax.dot_general(source, parts, NT, preferred_element_type=F32)
    spread = spread[:, 0:PAIR] + spread[:, PAIR : 2 * PAIR] + spread[:, 2 * PAIR : 3 * PAIR]
    spread = jnp.concatenate([spread] * XS, axis=1)
    spread = jnp.where(iota((CHIPS, XS * PAIR), 1) // PAIR == here, spread, 0.0)
    folded = [mean[:, k : k + 128] for k in range(0, WIDTH, 128)]
    folded = jnp.concatenate(folded + [jnp.zeros((2, 128), F32)], axis=0)
    for k in range(XS):
        out_refs[k][0:32, :] = spread[32 * k : 32 * (k + 1)]
        out_refs[k][32:40, :] = folded


def merge_kernel(*refs):
    refs[XS][...] = sum(ref[0:32, :] for ref in refs[:XS])


def unpack_kernel(place_ref, ids_ref, rank_ref, back_ref, *refs):
    came, (near_ref, centre_ref, mean_ref) = refs[:XS], refs[XS:]
    for k in range(2):
        offset = (place_ref[0, 0] - 2 * place_ref[0, 1] - k) & 3
        folded = sum(jnp.where(offset == i, ref[32:40, :], 0.0) for i, ref in enumerate(came))
        for j in range(WIDTH // 128):
            mean_ref[k : k + 1, j * 128 : (j + 1) * 128] = folded[j : j + 1]
    ids = ids_ref[...]
    same = iota((32, ROWS), 0) == ((ids >> 2) & 7) * 4 + (ids >> 5)
    onehot = same.astype(F32).astype(BF16)
    parts = jnp.concatenate(split3(back_ref[...]), axis=1)
    picked = lax.dot_general(parts, onehot, TN, preferred_element_type=F32)
    picked = picked[0:128] + picked[128:256] + picked[256:384]
    place = (ids & 3) * PAIR + rank_ref[...]
    line = iota((128, ROWS), 0)
    near_ref[...] = jnp.sum(jnp.where(line == place, picked, 0.0), axis=0, keepdims=True)
    centre_ref[...] = jnp.sum(
        jnp.where(line == place + CAP, picked, 0.0), axis=0, keepdims=True
    )


def struct(shape, dtype):
    return jax.ShapeDtypeStruct(shape, dtype)


def call(kernel, outs, flops, scratch=(), grant=40, **specs):
    return pl.pallas_call(
        kernel,
        out_shape=outs,
        scratch_shapes=list(scratch),
        compiler_params=pltpu.CompilerParams(vmem_limit_bytes=grant * 1024 * 1024),
        cost_estimate=pl.CostEstimate(
            flops=int(flops), bytes_accessed=6_000_000, transcendentals=0
        ),
        **specs,
    )


def shards(embeddings, cluster_ids):
    ids = cluster_ids.reshape(1, ROWS)
    block = 2 * SLOTS * SLOTS * WIDTH
    here = pl.BlockSpec(memory_space=pltpu.VMEM)
    send, rank = call(
        pack_kernel,
        (struct((SLOTS, WIDTH), BF16), struct((1, ROWS), jnp.int32)),
        2 * SLOTS * ROWS * WIDTH,
        (pltpu.VMEM((ROWS, WIDTH), BF16), pltpu.SemaphoreType.DMA),
        in_specs=[here, pl.BlockSpec(memory_space=pltpu.HBM)],
    )(ids, embeddings)
    chips = ("z", "x", "y")
    mine = lax.all_to_all(send.reshape(CHIPS, CAP, WIDTH), chips, 0, 0, tiled=True)
    mine = mine.reshape(SLOTS, WIDTH)
    swap = [(0, 1), (1, 0)]
    sib = lax.ppermute(mine, "core", swap)
    row = struct((1, SLOTS), F32)
    info, best = call(diagonal_kernel, (struct((3, SLOTS), F32), row), block / 4)(mine)
    sib_info = lax.ppermute(info, "core", swap)
    fold = pltpu.VMEM((TILE, 128), F32)
    best = call(own_kernel, row, block * 3 / 8, (fold,))(mine, info, best)
    axes = [lax.axis_index("x"), lax.axis_index("core")]
    place = jnp.stack(axes).astype(jnp.int32).reshape(1, 2)
    scalars = pl.BlockSpec(memory_space=pltpu.SMEM)
    line = struct((40, 128), F32)
    best, give, centre, mean = call(
        across_kernel,
        (row, row, row, struct((1, WIDTH), F32)),
        block / 2,
        (
            pltpu.VMEM((SLOTS, WIDTH), BF16),
            pltpu.VMEM((2, SLOTS), F32),
            pltpu.SemaphoreType.DMA((TILES,)),
        ),
        in_specs=[scalars, here, pl.BlockSpec(memory_space=pltpu.HBM), here, here, here],
    )(place, mine, sib, info, sib_info, best)
    taken = lax.ppermute(give, "core", swap)
    outs = call(
        spread_kernel, (line,) * XS, 1e8, in_specs=[scalars] + [here] * 5
    )(place, best, taken, info, centre, mean)
    came = [outs[0]]
    for k in range(1, XS):
        came.append(lax.ppermute(outs[k], "x", [(i, (i + k) % XS) for i in range(XS)]))
    out = call(merge_kernel, struct((32, 128), F32), 1e6)(*came)
    back = lax.all_to_all(out, ("z", "y"), 0, 0, tiled=True)
    near, centre, means = call(
        unpack_kernel,
        (struct((1, ROWS), F32), struct((1, ROWS), F32), struct((2, WIDTH), F32)),
        1e8,
        in_specs=[scalars] + [here] * (3 + XS),
    )(place, ids, rank, back, *came)
    return near.reshape(ROWS), centre.reshape(ROWS), means


def solution(mesh):
    fine = Mesh(mesh.devices.reshape(4, 8, 2, 4), ("y", "z", "core", "x"))
    owner = ("y", "z", "core")
    every = owner + ("x",)
    return jax.shard_map(
        shards,
        mesh=fine,
        in_specs=(P(every, None), P(every, None)),
        out_specs=(P(every), P(every), P(owner, None)),
        check_vma=False,
    )
```

```python
import jax
import jax.numpy as jnp
from jax import lax
from jax.experimental import pallas as pl
from jax.experimental.pallas import tpu as pltpu
from jax.sharding import Mesh, PartitionSpec as P

EPS = 1e-06
ROWS = 1024
WIDTH = 768
CAP = 16
CHIPS = 128
XS = 4
PAIR = 2 * CAP
SLOTS = CHIPS * CAP
MARK = 64.0
LOW = -1e30
TILE = 512
TILES = SLOTS // TILE
NT = (((1,), (1,)), ((), ()))
TN = (((0,), (0,)), ((), ()))
F32 = jnp.float32
BF16 = jnp.bfloat16


def iota(shape, dim):
    return lax.broadcasted_iota(jnp.int32, shape, dim)


def split3(v):
    hi = v.astype(BF16)
    rest = v - hi.astype(F32)
    mid = rest.astype(BF16)
    lo = (rest - mid.astype(F32)).astype(BF16)
    return hi, mid, lo


def chip_of(ids):
    return ((ids >> 2) & 7) * 16 + (ids & 3) * 4 + (ids >> 5)


def eye(n):
    return iota((n, n), 0) == iota((n, n), 1)


def to_row(column):
    blocks = [
        jnp.sum(jnp.where(eye(128), column[k : k + 128], 0.0), axis=0, keepdims=True)
        for k in range(0, column.shape[0], 128)
    ]
    return jnp.concatenate(blocks, axis=1)


def to_column(row):
    blocks = [
        jnp.sum(jnp.where(eye(128), row[:, k : k + 128], 0.0), axis=1, keepdims=True)
        for k in range(0, row.shape[1], 128)
    ]
    return jnp.concatenate(blocks, axis=0)


def fold_lanes(value):
    best = value[:, 0:128]
    for k in range(128, value.shape[1], 128):
        best = jnp.maximum(best, value[:, k : k + 128])
    return best


def part(ref, i):
    return ref[i * TILE : (i + 1) * TILE, :]


def lanes(ref, row, i):
    return ref[row : row + 1, i * TILE : (i + 1) * TILE]


def pack_kernel(ids_ref, x_hbm, send_ref, rank_ref, x_ref, sem):
    copy = pltpu.make_async_copy(x_hbm, x_ref, sem)
    copy.start()
    chip = chip_of(ids_ref[...])
    same = iota((CHIPS, ROWS), 0) == chip
    onehot = same.astype(F32).astype(BF16)
    before = (iota((ROWS, ROWS), 0) < iota((ROWS, ROWS), 1)).astype(F32).astype(BF16)
    earlier = jnp.dot(onehot, before, preferred_element_type=F32)
    rank = jnp.sum(jnp.where(same, earlier, 0.0), axis=0, keepdims=True).astype(jnp.int32)
    rank_ref[...] = rank
    position = chip * CAP + rank
    step = 256
    copy.wait()
    for start in range(0, SLOTS, step):
        pick = (iota((step, ROWS), 0) + start == position).astype(F32)
        live = jnp.sum(pick, axis=1, keepdims=True)
        rows = jnp.dot(pick.astype(BF16), x_ref[...], preferred_element_type=F32)
        mark = jnp.where(iota((step, 128), 1) == 0, (1.0 - live) * MARK, 0.0)
        send_ref[start : start + step, 0:128] = (rows[:, 0:128] + mark).astype(BF16)
        send_ref[start : start + step, 128:] = rows[:, 128:].astype(BF16)


def diagonal_kernel(x_ref, info_ref, best_ref):
    live = to_row((x_ref[:, 0:1].astype(F32) < MARK / 2).astype(F32))
    weights = jnp.broadcast_to(live, (8, SLOTS)).astype(BF16)
    totals = jnp.dot(weights, x_ref[...], preferred_element_type=F32)
    info_ref[1:2, :] = jnp.where(live > 0, 0.0, LOW)
    info_ref[2:3, 0:WIDTH] = totals[0:1]
    count = jnp.sum(live, axis=1, keepdims=True)
    info_ref[2:3, WIDTH:] = jnp.broadcast_to(count, (1, SLOTS - WIDTH))
    for i in range(TILES):
        dots = lax.dot_general(part(x_ref, i), part(x_ref, i), NT, preferred_element_type=F32)
        square = jnp.sum(jnp.where(eye(TILE), dots, 0.0), axis=0, keepdims=True)
        inv = lax.rsqrt(square / WIDTH + EPS)
        info_ref[0:1, i * TILE : (i + 1) * TILE] = inv
        value = jnp.where(eye(TILE), LOW, dots * inv + lanes(info_ref, 1, i))
        best = jnp.max(fold_lanes(value), axis=1, keepdims=True)
        best_ref[:, i * TILE : (i + 1) * TILE] = to_row(best)


def own_kernel(x_ref, info_ref, before_ref, best_ref, fold_ref):
    best_ref[...] = before_ref[...]
    for i in range(TILES - 2):
        inv = to_column(lanes(info_ref, 0, i))
        bias = to_column(lanes(info_ref, 1, i))
        for j in range(i + 1, TILES - i):
            dots = lax.dot_general(part(x_ref, i), part(x_ref, j), NT, preferred_element_type=F32)
            fold = fold_lanes(dots * lanes(info_ref, 0, j) + lanes(info_ref, 1, j))
            fold_ref[...] = fold if j == i + 1 else jnp.maximum(fold_ref[...], fold)
            down = jnp.max(dots * inv + bias, axis=0, keepdims=True)
            best_ref[:, j * TILE : (j + 1) * TILE] = jnp.maximum(lanes(best_ref, 0, j), down)
        best = to_row(jnp.max(fold_ref[...], axis=1, keepdims=True))
        best_ref[:, i * TILE : (i + 1) * TILE] = jnp.maximum(lanes(best_ref, 0, i), best)


def across_kernel(
    place_ref, x_ref, sib_hbm, info_ref, sib_info_ref, before_ref,
    best_ref, give_ref, sib_ref, turned_ref, sems,
):
    core = place_ref[0, 1]

    def rows(k):
        return pl.ds(pl.multiple_of(((core + k) & 3) * TILE, TILE), TILE)

    def copy(k):
        return pltpu.make_async_copy(
            sib_hbm.at[rows(k), :], sib_ref.at[k * TILE : (k + 1) * TILE, :], sems.at[k]
        )

    copy(0).start()
    copy(2).start()
    for k in range(TILES):
        turned_ref[:, k * TILE : (k + 1) * TILE] = sib_info_ref[0:2, rows(k)]
    columns = [
        (to_column(lanes(info_ref, 0, i)), to_column(lanes(info_ref, 1, i))) for i in range(TILES)
    ]

    def both(i, other, row, bias):
        dots = lax.dot_general(part(x_ref, i), other, NT, preferred_element_type=F32)
        down = jnp.max(dots * columns[i][0] + columns[i][1], axis=0, keepdims=True)
        return fold_lanes(dots * row + bias), down

    def own(i):
        j = TILES - 1
        return both(i, part(x_ref, j), lanes(info_ref, 0, j), lanes(info_ref, 1, j))

    folds, downs = {}, {}
    folds[2], downs[2] = own(2)
    give = {}
    for i in range(TILES):
        if i == 0:
            copy(0).wait()
            copy(2).wait()
            copy(1).start()
            copy(3).start()
            folds[1], downs[1] = own(1)
        if i == 1:
            copy(1).wait()
            copy(3).wait()
        fold = folds.get(i)
        for k in (i, (i + 2) % TILES):
            value, down = both(i, part(sib_ref, k), lanes(turned_ref, 0, k), lanes(turned_ref, 1, k))
            fold = value if fold is None else jnp.maximum(fold, value)
            give[k] = jnp.maximum(give[k], down) if k in give else down
        best = jnp.maximum(
            lanes(before_ref, 0, i), to_row(jnp.max(fold, axis=1, keepdims=True))
        )
        if i == TILES - 1:
            best = jnp.maximum(best, jnp.maximum(downs[1], downs[2]))
        best_ref[:, i * TILE : (i + 1) * TILE] = best
    for k in range(TILES):
        give_ref[:, rows(k)] = give[k]


def spread(source, row):
    slot = lax.rem(iota((CAP, SLOTS), 1), CAP) == iota((CAP, SLOTS), 0)
    parts = jnp.concatenate(split3(jnp.where(slot, row, 0.0)), axis=0)
    lines = lax.dot_general(source, parts, NT, preferred_element_type=F32)
    return lines[:, 0:CAP] + lines[:, CAP : 2 * CAP] + lines[:, 2 * CAP : 3 * CAP]


def centre_kernel(
    place_ref, after_ref, x_ref, info_ref, sib_info_ref, source_ref, centre_ref, mean_ref
):
    total = info_ref[2:3, 0:WIDTH] + sib_info_ref[2:3, 0:WIDTH]
    count = info_ref[2:3, WIDTH : WIDTH + 1] + sib_info_ref[2:3, WIDTH : WIDTH + 1]
    mean = total / count
    folded = [mean[:, k : k + 128] for k in range(0, WIDTH, 128)]
    mean_ref[...] = jnp.concatenate(folded + [jnp.zeros((2, 128), F32)], axis=0)
    scale = lax.rsqrt(jnp.sum(total * total, axis=1, keepdims=True) / WIDTH + EPS)
    parts = jnp.concatenate(split3(total) + (jnp.zeros((13, WIDTH), BF16),), axis=0)
    toward = lax.dot_general(parts, x_ref[...], NT, preferred_element_type=F32)
    toward = toward[0:1] + toward[1:2] + toward[2:3]
    centre = toward * info_ref[0:1, :] * scale / WIDTH
    chip = iota((1, SLOTS), 1) // CAP
    line = (((chip >> 2) - place_ref[0, 0]) & 3) * 32 + (chip >> 4) * 4 + (chip & 3)
    source = (line == iota((CHIPS, SLOTS), 0)).astype(F32).astype(BF16)
    source_ref[...] = source
    centre_ref[...] = spread(source, centre)


def spread_kernel(
    place_ref, best_ref, taken_ref, info_ref, source_ref, centre_ref, mean_ref, *out_refs
):
    best = jnp.maximum(best_ref[...], taken_ref[...])
    near = jnp.maximum(-1.0, best * info_ref[0:1, :] / WIDTH)
    lines = jnp.concatenate([spread(source_ref[...], near), centre_ref[...]] * XS, axis=1)
    lines = jnp.where(iota((CHIPS, XS * PAIR), 1) // PAIR == place_ref[0, 0], lines, 0.0)
    for k in range(XS):
        out_refs[k][0:32, :] = lines[32 * k : 32 * (k + 1)]
        out_refs[k][32:40, :] = mean_ref[...]


def merge_kernel(*refs):
    refs[XS][...] = sum(ref[0:32, :] for ref in refs[:XS])


def unpack_kernel(place_ref, ids_ref, rank_ref, back_ref, *refs):
    came, (near_ref, centre_ref, mean_ref) = refs[:XS], refs[XS:]
    for k in range(2):
        offset = (place_ref[0, 0] - 2 * place_ref[0, 1] - k) & 3
        folded = sum(jnp.where(offset == i, ref[32:40, :], 0.0) for i, ref in enumerate(came))
        for j in range(WIDTH // 128):
            mean_ref[k : k + 1, j * 128 : (j + 1) * 128] = folded[j : j + 1]
    ids = ids_ref[...]
    same = iota((32, ROWS), 0) == ((ids >> 2) & 7) * 4 + (ids >> 5)
    onehot = same.astype(F32).astype(BF16)
    parts = jnp.concatenate(split3(back_ref[...]), axis=1)
    picked = lax.dot_general(parts, onehot, TN, preferred_element_type=F32)
    picked = picked[0:128] + picked[128:256] + picked[256:384]
    place = (ids & 3) * PAIR + rank_ref[...]
    line = iota((128, ROWS), 0)
    near_ref[...] = jnp.sum(jnp.where(line == place, picked, 0.0), axis=0, keepdims=True)
    centre_ref[...] = jnp.sum(
        jnp.where(line == place + CAP, picked, 0.0), axis=0, keepdims=True
    )


def struct(shape, dtype):
    return jax.ShapeDtypeStruct(shape, dtype)


def call(kernel, outs, flops, scratch=(), grant=40, **specs):
    return pl.pallas_call(
        kernel,
        out_shape=outs,
        scratch_shapes=list(scratch),
        compiler_params=pltpu.CompilerParams(vmem_limit_bytes=grant * 1024 * 1024),
        cost_estimate=pl.CostEstimate(
            flops=int(flops), bytes_accessed=6_000_000, transcendentals=0
        ),
        **specs,
    )


def shards(embeddings, cluster_ids):
    ids = cluster_ids.reshape(1, ROWS)
    block = 2 * SLOTS * SLOTS * WIDTH
    here = pl.BlockSpec(memory_space=pltpu.VMEM)
    send, rank = call(
        pack_kernel,
        (struct((SLOTS, WIDTH), BF16), struct((1, ROWS), jnp.int32)),
        2 * SLOTS * ROWS * WIDTH,
        (pltpu.VMEM((ROWS, WIDTH), BF16), pltpu.SemaphoreType.DMA),
        in_specs=[here, pl.BlockSpec(memory_space=pltpu.HBM)],
    )(ids, embeddings)
    chips = ("z", "x", "y")
    mine = lax.all_to_all(send.reshape(CHIPS, CAP, WIDTH), chips, 0, 0, tiled=True)
    mine = mine.reshape(SLOTS, WIDTH)
    swap = [(0, 1), (1, 0)]
    sib = lax.ppermute(mine, "core", swap)
    row = struct((1, SLOTS), F32)
    info, best = call(diagonal_kernel, (struct((3, SLOTS), F32), row), block / 4)(mine)
    sib_info = lax.ppermute(info, "core", swap)
    fold = pltpu.VMEM((TILE, 128), F32)
    best = call(own_kernel, row, block * 3 / 8, (fold,))(mine, info, best)
    axes = [lax.axis_index("x"), lax.axis_index("core")]
    place = jnp.stack(axes).astype(jnp.int32).reshape(1, 2)
    scalars = pl.BlockSpec(memory_space=pltpu.SMEM)
    line = struct((40, 128), F32)
    best, give = call(
        across_kernel,
        (row, row),
        block / 2,
        (
            pltpu.VMEM((SLOTS, WIDTH), BF16),
            pltpu.VMEM((2, SLOTS), F32),
            pltpu.SemaphoreType.DMA((TILES,)),
        ),
        in_specs=[scalars, here, pl.BlockSpec(memory_space=pltpu.HBM), here, here, here],
    )(place, mine, sib, info, sib_info, best)
    taken = lax.ppermute(give, "core", swap)
    source, centre, mean = call(
        centre_kernel,
        (struct((CHIPS, SLOTS), BF16), struct((CHIPS, CAP), F32), struct((8, 128), F32)),
        block / 8,
        in_specs=[scalars] + [here] * 4,
    )(place, give, mine, info, sib_info)
    outs = call(
        spread_kernel, (line,) * XS, 1e8, in_specs=[scalars] + [here] * 6
    )(place, best, taken, info, source, centre, mean)
    came = [outs[0]]
    for k in range(1, XS):
        came.append(lax.ppermute(outs[k], "x", [(i, (i + k) % XS) for i in range(XS)]))
    out = call(merge_kernel, struct((32, 128), F32), 1e6)(*came)
    back = lax.all_to_all(out, ("z", "y"), 0, 0, tiled=True)
    near, centre, means = call(
        unpack_kernel,
        (struct((1, ROWS), F32), struct((1, ROWS), F32), struct((2, WIDTH), F32)),
        1e8,
        in_specs=[scalars] + [here] * (3 + XS),
    )(place, ids, rank, back, *came)
    return near.reshape(ROWS), centre.reshape(ROWS), means


def solution(mesh):
    fine = Mesh(mesh.devices.reshape(4, 8, 2, 4), ("y", "z", "core", "x"))
    owner = ("y", "z", "core")
    every = owner + ("x",)
    return jax.shard_map(
        shards,
        mesh=fine,
        in_specs=(P(every, None), P(every, None)),
        out_specs=(P(every), P(every), P(owner, None)),
        check_vma=False,
    )
```

```python
import jax
import jax.numpy as jnp
from jax import lax
from jax.experimental import pallas as pl
from jax.experimental.pallas import tpu as pltpu
from jax.sharding import Mesh, PartitionSpec as P

EPS = 1e-06
ROWS = 1024
WIDTH = 768
CAP = 16
CHIPS = 128
XS = 4
PAIR = 2 * CAP
OFFSETS = (2, 1, 3, 0)
SLOTS = CHIPS * CAP
MARK = 64.0
LOW = -1e30
TILE = 512
TILES = SLOTS // TILE
NT = (((1,), (1,)), ((), ()))
TN = (((0,), (0,)), ((), ()))
F32 = jnp.float32
BF16 = jnp.bfloat16


def iota(shape, dim):
    return lax.broadcasted_iota(jnp.int32, shape, dim)


def split3(v):
    hi = v.astype(BF16)
    rest = v - hi.astype(F32)
    mid = rest.astype(BF16)
    lo = (rest - mid.astype(F32)).astype(BF16)
    return hi, mid, lo


def chip_of(ids):
    return ((ids >> 2) & 7) * 16 + (ids & 3) * 4 + (ids >> 5)


def eye(n):
    return iota((n, n), 0) == iota((n, n), 1)


def to_row(column):
    blocks = [
        jnp.sum(jnp.where(eye(128), column[k : k + 128], 0.0), axis=0, keepdims=True)
        for k in range(0, column.shape[0], 128)
    ]
    return jnp.concatenate(blocks, axis=1)


def to_column(row):
    blocks = [
        jnp.sum(jnp.where(eye(128), row[:, k : k + 128], 0.0), axis=1, keepdims=True)
        for k in range(0, row.shape[1], 128)
    ]
    return jnp.concatenate(blocks, axis=0)


def fold_lanes(value):
    best = value[:, 0:128]
    for k in range(128, value.shape[1], 128):
        best = jnp.maximum(best, value[:, k : k + 128])
    return best


def part(ref, i):
    return ref[i * TILE : (i + 1) * TILE, :]


def lanes(ref, row, i):
    return ref[row : row + 1, i * TILE : (i + 1) * TILE]


def pack_kernel(ids_ref, x_hbm, send_ref, rank_ref, x_ref, sem):
    copy = pltpu.make_async_copy(x_hbm, x_ref, sem)
    copy.start()
    chip = chip_of(ids_ref[...])
    same = iota((CHIPS, ROWS), 0) == chip
    onehot = same.astype(F32).astype(BF16)
    before = (iota((ROWS, ROWS), 0) < iota((ROWS, ROWS), 1)).astype(F32).astype(BF16)
    earlier = jnp.dot(onehot, before, preferred_element_type=F32)
    rank = jnp.sum(jnp.where(same, earlier, 0.0), axis=0, keepdims=True).astype(jnp.int32)
    rank_ref[...] = rank
    position = chip * CAP + rank
    step = 256
    copy.wait()
    for start in range(0, SLOTS, step):
        pick = (iota((step, ROWS), 0) + start == position).astype(F32)
        live = jnp.sum(pick, axis=1, keepdims=True)
        rows = jnp.dot(pick.astype(BF16), x_ref[...], preferred_element_type=F32)
        mark = jnp.where(iota((step, 128), 1) == 0, (1.0 - live) * MARK, 0.0)
        send_ref[start : start + step, 0:128] = (rows[:, 0:128] + mark).astype(BF16)
        send_ref[start : start + step, 128:] = rows[:, 128:].astype(BF16)


def diagonal_kernel(x_ref, info_ref, best_ref):
    live = to_row((x_ref[:, 0:1].astype(F32) < MARK / 2).astype(F32))
    weights = jnp.broadcast_to(live, (8, SLOTS)).astype(BF16)
    totals = jnp.dot(weights, x_ref[...], preferred_element_type=F32)
    info_ref[1:2, :] = jnp.where(live > 0, 0.0, LOW)
    info_ref[2:3, 0:WIDTH] = totals[0:1]
    count = jnp.sum(live, axis=1, keepdims=True)
    info_ref[2:3, WIDTH:] = jnp.broadcast_to(count, (1, SLOTS - WIDTH))
    for i in range(TILES):
        dots = lax.dot_general(part(x_ref, i), part(x_ref, i), NT, preferred_element_type=F32)
        square = jnp.sum(jnp.where(eye(TILE), dots, 0.0), axis=0, keepdims=True)
        inv = lax.rsqrt(square / WIDTH + EPS)
        info_ref[0:1, i * TILE : (i + 1) * TILE] = inv
        value = jnp.where(eye(TILE), LOW, dots * inv + lanes(info_ref, 1, i))
        best = jnp.max(fold_lanes(value), axis=1, keepdims=True)
        best_ref[:, i * TILE : (i + 1) * TILE] = to_row(best)


def own_kernel(x_ref, info_ref, before_ref, best_ref, fold_ref):
    best_ref[...] = before_ref[...]
    for i in range(TILES - 2):
        inv = to_column(lanes(info_ref, 0, i))
        bias = to_column(lanes(info_ref, 1, i))
        for j in range(i + 1, TILES - i):
            dots = lax.dot_general(part(x_ref, i), part(x_ref, j), NT, preferred_element_type=F32)
            fold = fold_lanes(dots * lanes(info_ref, 0, j) + lanes(info_ref, 1, j))
            fold_ref[...] = fold if j == i + 1 else jnp.maximum(fold_ref[...], fold)
            down = jnp.max(dots * inv + bias, axis=0, keepdims=True)
            best_ref[:, j * TILE : (j + 1) * TILE] = jnp.maximum(lanes(best_ref, 0, j), down)
        best = to_row(jnp.max(fold_ref[...], axis=1, keepdims=True))
        best_ref[:, i * TILE : (i + 1) * TILE] = jnp.maximum(lanes(best_ref, 0, i), best)


def across_kernel(
    place_ref, x_ref, sib_hbm, info_ref, sib_info_ref, before_ref,
    best_ref, give_ref, centre_ref, mean_ref, sib_ref, turned_ref, sems,
):
    core = place_ref[0, 1]

    def rows(k):
        return pl.ds(pl.multiple_of(((core + k) & 3) * TILE, TILE), TILE)

    def copy(k):
        return pltpu.make_async_copy(
            sib_hbm.at[rows(k), :], sib_ref.at[k * TILE : (k + 1) * TILE, :], sems.at[k]
        )

    copy(0).start()
    copy(2).start()
    for k in range(TILES):
        turned_ref[:, k * TILE : (k + 1) * TILE] = sib_info_ref[0:2, rows(k)]
    total = info_ref[2:3, 0:WIDTH] + sib_info_ref[2:3, 0:WIDTH]
    count = info_ref[2:3, WIDTH : WIDTH + 1] + sib_info_ref[2:3, WIDTH : WIDTH + 1]
    mean = total / count
    folded = [mean[:, k : k + 128] for k in range(0, WIDTH, 128)]
    mean_ref[...] = jnp.concatenate(folded + [jnp.zeros((2, 128), F32)], axis=0)
    scale = lax.rsqrt(jnp.sum(total * total, axis=1, keepdims=True) / WIDTH + EPS)
    parts = jnp.concatenate(split3(total) + (jnp.zeros((13, WIDTH), BF16),), axis=0)
    toward = lax.dot_general(parts, x_ref[...], NT, preferred_element_type=F32)
    toward = toward[0:1] + toward[1:2] + toward[2:3]
    centre_ref[...] = toward * info_ref[0:1, :] * scale / WIDTH
    columns = [
        (to_column(lanes(info_ref, 0, i)), to_column(lanes(info_ref, 1, i))) for i in range(TILES)
    ]

    def both(i, other, row, bias):
        dots = lax.dot_general(part(x_ref, i), other, NT, preferred_element_type=F32)
        down = jnp.max(dots * columns[i][0] + columns[i][1], axis=0, keepdims=True)
        return fold_lanes(dots * row + bias), down

    def own(i):
        j = TILES - 1
        return both(i, part(x_ref, j), lanes(info_ref, 0, j), lanes(info_ref, 1, j))

    folds, downs = {}, {}
    folds[2], downs[2] = own(2)
    give = {}
    for i in range(TILES):
        if i == 0:
            copy(0).wait()
            copy(2).wait()
            copy(1).start()
            copy(3).start()
            folds[1], downs[1] = own(1)
        if i == 1:
            copy(1).wait()
            copy(3).wait()
        fold = folds.get(i)
        for k in (i, (i + 2) % TILES):
            value, down = both(i, part(sib_ref, k), lanes(turned_ref, 0, k), lanes(turned_ref, 1, k))
            fold = value if fold is None else jnp.maximum(fold, value)
            give[k] = jnp.maximum(give[k], down) if k in give else down
        best = jnp.maximum(
            lanes(before_ref, 0, i), to_row(jnp.max(fold, axis=1, keepdims=True))
        )
        if i == TILES - 1:
            best = jnp.maximum(best, jnp.maximum(downs[1], downs[2]))
        best_ref[:, i * TILE : (i + 1) * TILE] = best
    for k in range(TILES):
        give_ref[:, rows(k)] = give[k]


def spread(source, row):
    slot = lax.rem(iota((CAP, SLOTS), 1), CAP) == iota((CAP, SLOTS), 0)
    parts = jnp.concatenate(split3(jnp.where(slot, row, 0.0)), axis=0)
    lines = lax.dot_general(source, parts, NT, preferred_element_type=F32)
    return lines[:, 0:CAP] + lines[:, CAP : 2 * CAP] + lines[:, 2 * CAP : 3 * CAP]


def centre_kernel(place_ref, after_ref, centre_ref, source_ref, out_ref):
    chip = iota((1, SLOTS), 1) // CAP
    line = (((chip >> 2) - place_ref[0, 0]) & 3) * 32 + (chip >> 4) * 4 + (chip & 3)
    source = (line == iota((CHIPS, SLOTS), 0)).astype(F32).astype(BF16)
    source_ref[...] = source
    out_ref[...] = spread(source, centre_ref[...])


def spread_kernel(
    place_ref, best_ref, taken_ref, info_ref, source_ref, centre_ref, mean_ref, *out_refs
):
    best = jnp.maximum(best_ref[...], taken_ref[...])
    near = jnp.maximum(-1.0, best * info_ref[0:1, :] / WIDTH)
    lines = jnp.concatenate([spread(source_ref[...], near), centre_ref[...]] * XS, axis=1)
    lines = jnp.where(iota((CHIPS, XS * PAIR), 1) // PAIR == place_ref[0, 0], lines, 0.0)
    for k in range(XS):
        out_refs[k][0:32, :] = lines[32 * k : 32 * (k + 1)]
        out_refs[k][32:40, :] = mean_ref[...]


def merge_kernel(*refs):
    refs[XS][...] = sum(ref[0:32, :] for ref in refs[:XS])


def unpack_kernel(place_ref, ids_ref, rank_ref, back_ref, *refs):
    came, (near_ref, centre_ref, mean_ref) = refs[:XS], refs[XS:]
    for k in range(2):
        offset = (place_ref[0, 0] - 2 * place_ref[0, 1] - k) & 3
        folded = sum(jnp.where(offset == i, ref[32:40, :], 0.0) for i, ref in zip(OFFSETS, came))
        for j in range(WIDTH // 128):
            mean_ref[k : k + 1, j * 128 : (j + 1) * 128] = folded[j : j + 1]
    ids = ids_ref[...]
    same = iota((32, ROWS), 0) == ((ids >> 2) & 7) * 4 + (ids >> 5)
    onehot = same.astype(F32).astype(BF16)
    parts = jnp.concatenate(split3(back_ref[...]), axis=1)
    picked = lax.dot_general(parts, onehot, TN, preferred_element_type=F32)
    picked = picked[0:128] + picked[128:256] + picked[256:384]
    place = (ids & 3) * PAIR + rank_ref[...]
    line = iota((128, ROWS), 0)
    near_ref[...] = jnp.sum(jnp.where(line == place, picked, 0.0), axis=0, keepdims=True)
    centre_ref[...] = jnp.sum(
        jnp.where(line == place + CAP, picked, 0.0), axis=0, keepdims=True
    )


def struct(shape, dtype):
    return jax.ShapeDtypeStruct(shape, dtype)


def call(kernel, outs, flops, scratch=(), grant=40, **specs):
    return pl.pallas_call(
        kernel,
        out_shape=outs,
        scratch_shapes=list(scratch),
        compiler_params=pltpu.CompilerParams(vmem_limit_bytes=grant * 1024 * 1024),
        cost_estimate=pl.CostEstimate(
            flops=int(flops), bytes_accessed=6_000_000, transcendentals=0
        ),
        **specs,
    )


def shards(embeddings, cluster_ids):
    ids = cluster_ids.reshape(1, ROWS)
    block = 2 * SLOTS * SLOTS * WIDTH
    here = pl.BlockSpec(memory_space=pltpu.VMEM)
    send, rank = call(
        pack_kernel,
        (struct((SLOTS, WIDTH), BF16), struct((1, ROWS), jnp.int32)),
        2 * SLOTS * ROWS * WIDTH,
        (pltpu.VMEM((ROWS, WIDTH), BF16), pltpu.SemaphoreType.DMA),
        in_specs=[here, pl.BlockSpec(memory_space=pltpu.HBM)],
    )(ids, embeddings)
    chips = ("z", "x", "y")
    mine = lax.all_to_all(send.reshape(CHIPS, CAP, WIDTH), chips, 0, 0, tiled=True)
    mine = mine.reshape(SLOTS, WIDTH)
    swap = [(0, 1), (1, 0)]
    sib = lax.ppermute(mine, "core", swap)
    row = struct((1, SLOTS), F32)
    info, best = call(diagonal_kernel, (struct((3, SLOTS), F32), row), block / 4)(mine)
    sib_info = lax.ppermute(info, "core", swap)
    fold = pltpu.VMEM((TILE, 128), F32)
    best = call(own_kernel, row, block * 3 / 8, (fold,))(mine, info, best)
    axes = [lax.axis_index("x"), lax.axis_index("core")]
    place = jnp.stack(axes).astype(jnp.int32).reshape(1, 2)
    scalars = pl.BlockSpec(memory_space=pltpu.SMEM)
    line = struct((40, 128), F32)
    best, give, centre, mean = call(
        across_kernel,
        (row, row, row, struct((8, 128), F32)),
        block / 2,
        (
            pltpu.VMEM((SLOTS, WIDTH), BF16),
            pltpu.VMEM((2, SLOTS), F32),
            pltpu.SemaphoreType.DMA((TILES,)),
        ),
        in_specs=[scalars, here, pl.BlockSpec(memory_space=pltpu.HBM), here, here, here],
    )(place, mine, sib, info, sib_info, best)
    taken = lax.ppermute(give, "core", swap)
    source, centre = call(
        centre_kernel,
        (struct((CHIPS, SLOTS), BF16), struct((CHIPS, CAP), F32)),
        block / 8,
        in_specs=[scalars, here, here],
    )(place, give, centre)
    outs = call(
        spread_kernel, (line,) * XS, 1e8, in_specs=[scalars] + [here] * 6
    )(place, best, taken, info, source, centre, mean)
    came = [
        lax.ppermute(outs[k], "x", [(i, (i + k) % XS) for i in range(XS)]) if k else outs[k]
        for k in OFFSETS
    ]
    out = call(merge_kernel, struct((32, 128), F32), 1e6)(*came)
    back = lax.all_to_all(out, ("z", "y"), 0, 0, tiled=True)
    near, centre, means = call(
        unpack_kernel,
        (struct((1, ROWS), F32), struct((1, ROWS), F32), struct((2, WIDTH), F32)),
        1e8,
        in_specs=[scalars] + [here] * (3 + XS),
    )(place, ids, rank, back, *came)
    return near.reshape(ROWS), centre.reshape(ROWS), means


def solution(mesh):
    fine = Mesh(mesh.devices.reshape(4, 8, 2, 4), ("y", "z", "core", "x"))
    owner = ("y", "z", "core")
    every = owner + ("x",)
    return jax.shard_map(
        shards,
        mesh=fine,
        in_specs=(P(every, None), P(every, None)),
        out_specs=(P(every), P(every), P(owner, None)),
        check_vma=False,
    )
```

```python
import jax
import jax.numpy as jnp
from jax import lax
from jax.experimental import pallas as pl
from jax.experimental.pallas import tpu as pltpu
from jax.sharding import Mesh, PartitionSpec as P

EPS = 1e-06
ROWS = 1024
WIDTH = 768
CAP = 16
CHIPS = 128
XS = 4
PAIR = 2 * CAP
OFFSETS = (2, 1, 3, 0)
SLOTS = CHIPS * CAP
MARK = 64.0
LOW = -1e30
TILE = 512
TILES = SLOTS // TILE
NT = (((1,), (1,)), ((), ()))
TN = (((0,), (0,)), ((), ()))
F32 = jnp.float32
BF16 = jnp.bfloat16


def iota(shape, dim):
    return lax.broadcasted_iota(jnp.int32, shape, dim)


def split3(v):
    hi = v.astype(BF16)
    rest = v - hi.astype(F32)
    mid = rest.astype(BF16)
    lo = (rest - mid.astype(F32)).astype(BF16)
    return hi, mid, lo


def chip_of(ids):
    return ((ids >> 2) & 7) * 16 + (ids & 3) * 4 + (ids >> 5)


def eye(n):
    return iota((n, n), 0) == iota((n, n), 1)


def to_row(column):
    blocks = [
        jnp.sum(jnp.where(eye(128), column[k : k + 128], 0.0), axis=0, keepdims=True)
        for k in range(0, column.shape[0], 128)
    ]
    return jnp.concatenate(blocks, axis=1)


def to_column(row):
    blocks = [
        jnp.sum(jnp.where(eye(128), row[:, k : k + 128], 0.0), axis=1, keepdims=True)
        for k in range(0, row.shape[1], 128)
    ]
    return jnp.concatenate(blocks, axis=0)


def fold_lanes(value):
    best = value[:, 0:128]
    for k in range(128, value.shape[1], 128):
        best = jnp.maximum(best, value[:, k : k + 128])
    return best


def part(ref, i):
    return ref[i * TILE : (i + 1) * TILE, :]


def lanes(ref, row, i):
    return ref[row : row + 1, i * TILE : (i + 1) * TILE]


def pack_kernel(ids_ref, x_hbm, send_ref, rank_ref, x_ref, sem):
    copy = pltpu.make_async_copy(x_hbm, x_ref, sem)
    copy.start()
    chip = chip_of(ids_ref[...])
    same = iota((CHIPS, ROWS), 0) == chip
    onehot = same.astype(F32).astype(BF16)
    before = (iota((ROWS, ROWS), 0) < iota((ROWS, ROWS), 1)).astype(F32).astype(BF16)
    earlier = jnp.dot(onehot, before, preferred_element_type=F32)
    rank = jnp.sum(jnp.where(same, earlier, 0.0), axis=0, keepdims=True).astype(jnp.int32)
    rank_ref[...] = rank
    position = chip * CAP + rank
    step = 256
    copy.wait()
    for start in range(0, SLOTS, step):
        pick = (iota((step, ROWS), 0) + start == position).astype(F32)
        live = jnp.sum(pick, axis=1, keepdims=True)
        rows = jnp.dot(pick.astype(BF16), x_ref[...], preferred_element_type=F32)
        mark = jnp.where(iota((step, 128), 1) == 0, (1.0 - live) * MARK, 0.0)
        send_ref[start : start + step, 0:128] = (rows[:, 0:128] + mark).astype(BF16)
        send_ref[start : start + step, 128:] = rows[:, 128:].astype(BF16)


def diagonal_kernel(x_ref, info_ref, best_ref):
    live = to_row((x_ref[:, 0:1].astype(F32) < MARK / 2).astype(F32))
    weights = jnp.broadcast_to(live, (8, SLOTS)).astype(BF16)
    totals = jnp.dot(weights, x_ref[...], preferred_element_type=F32)
    info_ref[1:2, :] = jnp.where(live > 0, 0.0, LOW)
    info_ref[2:3, 0:WIDTH] = totals[0:1]
    count = jnp.sum(live, axis=1, keepdims=True)
    info_ref[2:3, WIDTH:] = jnp.broadcast_to(count, (1, SLOTS - WIDTH))
    for i in range(TILES):
        dots = lax.dot_general(part(x_ref, i), part(x_ref, i), NT, preferred_element_type=F32)
        square = jnp.sum(jnp.where(eye(TILE), dots, 0.0), axis=0, keepdims=True)
        inv = lax.rsqrt(square / WIDTH + EPS)
        info_ref[0:1, i * TILE : (i + 1) * TILE] = inv
        value = jnp.where(eye(TILE), LOW, dots * inv + lanes(info_ref, 1, i))
        best = jnp.max(fold_lanes(value), axis=1, keepdims=True)
        best_ref[:, i * TILE : (i + 1) * TILE] = to_row(best)


def own_kernel(x_ref, info_ref, before_ref, best_ref, fold_ref):
    best_ref[...] = before_ref[...]
    for i in range(TILES - 2):
        inv = to_column(lanes(info_ref, 0, i))
        bias = to_column(lanes(info_ref, 1, i))
        for j in range(i + 1, TILES - i):
            dots = lax.dot_general(part(x_ref, i), part(x_ref, j), NT, preferred_element_type=F32)
            fold = fold_lanes(dots * lanes(info_ref, 0, j) + lanes(info_ref, 1, j))
            fold_ref[...] = fold if j == i + 1 else jnp.maximum(fold_ref[...], fold)
            down = jnp.max(dots * inv + bias, axis=0, keepdims=True)
            best_ref[:, j * TILE : (j + 1) * TILE] = jnp.maximum(lanes(best_ref, 0, j), down)
        best = to_row(jnp.max(fold_ref[...], axis=1, keepdims=True))
        best_ref[:, i * TILE : (i + 1) * TILE] = jnp.maximum(lanes(best_ref, 0, i), best)


def across_kernel(
    place_ref, x_ref, sib_hbm, info_ref, sib_info_ref, before_ref,
    best_ref, give_ref, centre_ref, mean_ref, sib_ref, turned_ref, sems,
):
    core = place_ref[0, 1]

    def rows(k):
        return pl.ds(pl.multiple_of(((core + k) & 3) * TILE, TILE), TILE)

    def copy(k):
        return pltpu.make_async_copy(
            sib_hbm.at[rows(k), :], sib_ref.at[k * TILE : (k + 1) * TILE, :], sems.at[k]
        )

    for k in range(TILES):
        copy(k).start()
    for k in range(TILES):
        turned_ref[:, k * TILE : (k + 1) * TILE] = sib_info_ref[0:2, rows(k)]
    total = info_ref[2:3, 0:WIDTH] + sib_info_ref[2:3, 0:WIDTH]
    count = info_ref[2:3, WIDTH : WIDTH + 1] + sib_info_ref[2:3, WIDTH : WIDTH + 1]
    mean = total / count
    folded = [mean[:, k : k + 128] for k in range(0, WIDTH, 128)]
    mean_ref[...] = jnp.concatenate(folded + [jnp.zeros((2, 128), F32)], axis=0)
    scale = lax.rsqrt(jnp.sum(total * total, axis=1, keepdims=True) / WIDTH + EPS)
    parts = jnp.concatenate(split3(total) + (jnp.zeros((13, WIDTH), BF16),), axis=0)
    toward = lax.dot_general(parts, x_ref[...], NT, preferred_element_type=F32)
    toward = toward[0:1] + toward[1:2] + toward[2:3]
    centre_ref[...] = toward * info_ref[0:1, :] * scale / WIDTH
    columns = [
        (to_column(lanes(info_ref, 0, i)), to_column(lanes(info_ref, 1, i))) for i in range(TILES)
    ]

    def both(i, other, row, bias):
        dots = lax.dot_general(part(x_ref, i), other, NT, preferred_element_type=F32)
        down = jnp.max(dots * columns[i][0] + columns[i][1], axis=0, keepdims=True)
        return fold_lanes(dots * row + bias), down

    def own(i):
        j = TILES - 1
        return both(i, part(x_ref, j), lanes(info_ref, 0, j), lanes(info_ref, 1, j))

    folds, downs = {}, {}
    folds[1], downs[1] = own(1)
    folds[2], downs[2] = own(2)
    for k in range(TILES):
        copy(k).wait()
    give = {}
    for i in range(TILES):
        fold = folds.get(i)
        for k in (i, (i + 2) % TILES):
            value, down = both(i, part(sib_ref, k), lanes(turned_ref, 0, k), lanes(turned_ref, 1, k))
            fold = value if fold is None else jnp.maximum(fold, value)
            give[k] = jnp.maximum(give[k], down) if k in give else down
        best = jnp.maximum(
            lanes(before_ref, 0, i), to_row(jnp.max(fold, axis=1, keepdims=True))
        )
        if i == TILES - 1:
            best = jnp.maximum(best, jnp.maximum(downs[1], downs[2]))
        best_ref[:, i * TILE : (i + 1) * TILE] = best
    for k in range(TILES):
        give_ref[:, rows(k)] = give[k]


def spread(source, row):
    slot = lax.rem(iota((CAP, SLOTS), 1), CAP) == iota((CAP, SLOTS), 0)
    parts = jnp.concatenate(split3(jnp.where(slot, row, 0.0)), axis=0)
    lines = lax.dot_general(source, parts, NT, preferred_element_type=F32)
    return lines[:, 0:CAP] + lines[:, CAP : 2 * CAP] + lines[:, 2 * CAP : 3 * CAP]


def centre_kernel(place_ref, after_ref, centre_ref, source_ref, out_ref):
    chip = iota((1, SLOTS), 1) // CAP
    line = (((chip >> 2) - place_ref[0, 0]) & 3) * 32 + (chip >> 4) * 4 + (chip & 3)
    source = (line == iota((CHIPS, SLOTS), 0)).astype(F32).astype(BF16)
    source_ref[...] = source
    out_ref[...] = spread(source, centre_ref[...])


def spread_kernel(
    place_ref, best_ref, taken_ref, info_ref, source_ref, centre_ref, mean_ref, *out_refs
):
    best = jnp.maximum(best_ref[...], taken_ref[...])
    near = jnp.maximum(-1.0, best * info_ref[0:1, :] / WIDTH)
    lines = jnp.concatenate([spread(source_ref[...], near), centre_ref[...]] * XS, axis=1)
    lines = jnp.where(iota((CHIPS, XS * PAIR), 1) // PAIR == place_ref[0, 0], lines, 0.0)
    for k in range(XS):
        out_refs[k][0:32, :] = lines[32 * k : 32 * (k + 1)]
        out_refs[k][32:40, :] = mean_ref[...]


def merge_kernel(*refs):
    refs[XS][...] = sum(ref[0:32, :] for ref in refs[:XS])


def unpack_kernel(place_ref, ids_ref, rank_ref, back_ref, *refs):
    came, (near_ref, centre_ref, mean_ref) = refs[:XS], refs[XS:]
    for k in range(2):
        offset = (place_ref[0, 0] - 2 * place_ref[0, 1] - k) & 3
        folded = sum(jnp.where(offset == i, ref[32:40, :], 0.0) for i, ref in zip(OFFSETS, came))
        for j in range(WIDTH // 128):
            mean_ref[k : k + 1, j * 128 : (j + 1) * 128] = folded[j : j + 1]
    ids = ids_ref[...]
    same = iota((32, ROWS), 0) == ((ids >> 2) & 7) * 4 + (ids >> 5)
    onehot = same.astype(F32).astype(BF16)
    parts = jnp.concatenate(split3(back_ref[...]), axis=1)
    picked = lax.dot_general(parts, onehot, TN, preferred_element_type=F32)
    picked = picked[0:128] + picked[128:256] + picked[256:384]
    place = (ids & 3) * PAIR + rank_ref[...]
    line = iota((128, ROWS), 0)
    near_ref[...] = jnp.sum(jnp.where(line == place, picked, 0.0), axis=0, keepdims=True)
    centre_ref[...] = jnp.sum(
        jnp.where(line == place + CAP, picked, 0.0), axis=0, keepdims=True
    )


def struct(shape, dtype):
    return jax.ShapeDtypeStruct(shape, dtype)


def call(kernel, outs, flops, scratch=(), grant=40, **specs):
    return pl.pallas_call(
        kernel,
        out_shape=outs,
        scratch_shapes=list(scratch),
        compiler_params=pltpu.CompilerParams(vmem_limit_bytes=grant * 1024 * 1024),
        cost_estimate=pl.CostEstimate(
            flops=int(flops), bytes_accessed=6_000_000, transcendentals=0
        ),
        **specs,
    )


def shards(embeddings, cluster_ids):
    ids = cluster_ids.reshape(1, ROWS)
    block = 2 * SLOTS * SLOTS * WIDTH
    here = pl.BlockSpec(memory_space=pltpu.VMEM)
    send, rank = call(
        pack_kernel,
        (struct((SLOTS, WIDTH), BF16), struct((1, ROWS), jnp.int32)),
        2 * SLOTS * ROWS * WIDTH,
        (pltpu.VMEM((ROWS, WIDTH), BF16), pltpu.SemaphoreType.DMA),
        in_specs=[here, pl.BlockSpec(memory_space=pltpu.HBM)],
    )(ids, embeddings)
    chips = ("z", "x", "y")
    mine = lax.all_to_all(send.reshape(CHIPS, CAP, WIDTH), chips, 0, 0, tiled=True)
    mine = mine.reshape(SLOTS, WIDTH)
    swap = [(0, 1), (1, 0)]
    sib = lax.ppermute(mine, "core", swap)
    row = struct((1, SLOTS), F32)
    info, best = call(diagonal_kernel, (struct((3, SLOTS), F32), row), block / 4)(mine)
    sib_info = lax.ppermute(info, "core", swap)
    fold = pltpu.VMEM((TILE, 128), F32)
    best = call(own_kernel, row, block * 3 / 8, (fold,))(mine, info, best)
    axes = [lax.axis_index("x"), lax.axis_index("core")]
    place = jnp.stack(axes).astype(jnp.int32).reshape(1, 2)
    scalars = pl.BlockSpec(memory_space=pltpu.SMEM)
    line = struct((40, 128), F32)
    best, give, centre, mean = call(
        across_kernel,
        (row, row, row, struct((8, 128), F32)),
        block / 2,
        (
            pltpu.VMEM((SLOTS, WIDTH), BF16),
            pltpu.VMEM((2, SLOTS), F32),
            pltpu.SemaphoreType.DMA((TILES,)),
        ),
        in_specs=[scalars, here, pl.BlockSpec(memory_space=pltpu.HBM), here, here, here],
    )(place, mine, sib, info, sib_info, best)
    taken = lax.ppermute(give, "core", swap)
    source, centre = call(
        centre_kernel,
        (struct((CHIPS, SLOTS), BF16), struct((CHIPS, CAP), F32)),
        block / 8,
        in_specs=[scalars, here, here],
    )(place, give, centre)
    outs = call(
        spread_kernel, (line,) * XS, 1e8, in_specs=[scalars] + [here] * 6
    )(place, best, taken, info, source, centre, mean)
    came = [
        lax.ppermute(outs[k], "x", [(i, (i + k) % XS) for i in range(XS)]) if k else outs[k]
        for k in OFFSETS
    ]
    out = call(merge_kernel, struct((32, 128), F32), 1e6)(*came)
    back = lax.all_to_all(out, ("z", "y"), 0, 0, tiled=True)
    near, centre, means = call(
        unpack_kernel,
        (struct((1, ROWS), F32), struct((1, ROWS), F32), struct((2, WIDTH), F32)),
        1e8,
        in_specs=[scalars] + [here] * (3 + XS),
    )(place, ids, rank, back, *came)
    return near.reshape(ROWS), centre.reshape(ROWS), means


def solution(mesh):
    fine = Mesh(mesh.devices.reshape(4, 8, 2, 4), ("y", "z", "core", "x"))
    owner = ("y", "z", "core")
    every = owner + ("x",)
    return jax.shard_map(
        shards,
        mesh=fine,
        in_specs=(P(every, None), P(every, None)),
        out_specs=(P(every), P(every), P(owner, None)),
        check_vma=False,
    )
```

```python
import jax
import jax.numpy as jnp
from jax import lax
from jax.experimental import pallas as pl
from jax.experimental.pallas import tpu as pltpu
from jax.sharding import Mesh, PartitionSpec as P

EPS = 1e-06
ROWS = 1024
WIDTH = 768
CAP = 16
CHIPS = 128
XS = 4
PAIR = 2 * CAP
SLOTS = CHIPS * CAP
MARK = 64.0
LOW = -1e30
TILE = 512
TILES = SLOTS // TILE
NT = (((1,), (1,)), ((), ()))
TN = (((0,), (0,)), ((), ()))
F32 = jnp.float32
BF16 = jnp.bfloat16


def iota(shape, dim):
    return lax.broadcasted_iota(jnp.int32, shape, dim)


def split3(v):
    hi = v.astype(BF16)
    rest = v - hi.astype(F32)
    mid = rest.astype(BF16)
    lo = (rest - mid.astype(F32)).astype(BF16)
    return hi, mid, lo


def chip_of(ids):
    return (ids & 3) * 32 + ((ids >> 2) & 7) * 4 + (ids >> 5)


def eye(n):
    return iota((n, n), 0) == iota((n, n), 1)


def to_row(column):
    blocks = [
        jnp.sum(jnp.where(eye(128), column[k : k + 128], 0.0), axis=0, keepdims=True)
        for k in range(0, column.shape[0], 128)
    ]
    return jnp.concatenate(blocks, axis=1)


def to_column(row):
    blocks = [
        jnp.sum(jnp.where(eye(128), row[:, k : k + 128], 0.0), axis=1, keepdims=True)
        for k in range(0, row.shape[1], 128)
    ]
    return jnp.concatenate(blocks, axis=0)


def fold_lanes(value):
    best = value[:, 0:128]
    for k in range(128, value.shape[1], 128):
        best = jnp.maximum(best, value[:, k : k + 128])
    return best


def part(ref, i):
    return ref[i * TILE : (i + 1) * TILE, :]


def lanes(ref, row, i):
    return ref[row : row + 1, i * TILE : (i + 1) * TILE]


def pack_kernel(ids_ref, x_hbm, send_ref, rank_ref, x_ref, sem):
    copy = pltpu.make_async_copy(x_hbm, x_ref, sem)
    copy.start()
    chip = chip_of(ids_ref[...])
    same = iota((CHIPS, ROWS), 0) == chip
    onehot = same.astype(F32).astype(BF16)
    before = (iota((ROWS, ROWS), 0) < iota((ROWS, ROWS), 1)).astype(F32).astype(BF16)
    earlier = jnp.dot(onehot, before, preferred_element_type=F32)
    rank = jnp.sum(jnp.where(same, earlier, 0.0), axis=0, keepdims=True).astype(jnp.int32)
    rank_ref[...] = rank
    position = chip * CAP + rank
    step = 256
    copy.wait()
    for start in range(0, SLOTS, step):
        pick = (iota((step, ROWS), 0) + start == position).astype(F32)
        live = jnp.sum(pick, axis=1, keepdims=True)
        rows = jnp.dot(pick.astype(BF16), x_ref[...], preferred_element_type=F32)
        mark = jnp.where(iota((step, 128), 1) == 0, (1.0 - live) * MARK, 0.0)
        send_ref[start : start + step, 0:128] = (rows[:, 0:128] + mark).astype(BF16)
        send_ref[start : start + step, 128:] = rows[:, 128:].astype(BF16)


def diagonal_kernel(x_ref, info_ref, best_ref):
    live = to_row((x_ref[:, 0:1].astype(F32) < MARK / 2).astype(F32))
    weights = jnp.broadcast_to(live, (8, SLOTS)).astype(BF16)
    totals = jnp.dot(weights, x_ref[...], preferred_element_type=F32)
    info_ref[1:2, :] = jnp.where(live > 0, 0.0, LOW)
    info_ref[2:3, 0:WIDTH] = totals[0:1]
    count = jnp.sum(live, axis=1, keepdims=True)
    info_ref[2:3, WIDTH:] = jnp.broadcast_to(count, (1, SLOTS - WIDTH))
    for i in range(TILES):
        dots = lax.dot_general(part(x_ref, i), part(x_ref, i), NT, preferred_element_type=F32)
        square = jnp.sum(jnp.where(eye(TILE), dots, 0.0), axis=0, keepdims=True)
        inv = lax.rsqrt(square / WIDTH + EPS)
        info_ref[0:1, i * TILE : (i + 1) * TILE] = inv
        value = jnp.where(eye(TILE), LOW, dots * inv + lanes(info_ref, 1, i))
        best = jnp.max(fold_lanes(value), axis=1, keepdims=True)
        best_ref[:, i * TILE : (i + 1) * TILE] = to_row(best)


def own_kernel(x_ref, info_ref, before_ref, best_ref, fold_ref):
    best_ref[...] = before_ref[...]
    for i in range(TILES - 2):
        inv = to_column(lanes(info_ref, 0, i))
        bias = to_column(lanes(info_ref, 1, i))
        for j in range(i + 1, TILES - i):
            dots = lax.dot_general(part(x_ref, i), part(x_ref, j), NT, preferred_element_type=F32)
            fold = fold_lanes(dots * lanes(info_ref, 0, j) + lanes(info_ref, 1, j))
            fold_ref[...] = fold if j == i + 1 else jnp.maximum(fold_ref[...], fold)
            down = jnp.max(dots * inv + bias, axis=0, keepdims=True)
            best_ref[:, j * TILE : (j + 1) * TILE] = jnp.maximum(lanes(best_ref, 0, j), down)
        best = to_row(jnp.max(fold_ref[...], axis=1, keepdims=True))
        best_ref[:, i * TILE : (i + 1) * TILE] = jnp.maximum(lanes(best_ref, 0, i), best)


def across_kernel(
    place_ref, x_ref, sib_hbm, info_ref, sib_info_ref, before_ref,
    best_ref, give_ref, sib_ref, turned_ref, sems,
):
    core = place_ref[0, 1]

    def rows(k):
        return pl.ds(pl.multiple_of(((core + k) & 3) * TILE, TILE), TILE)

    def copy(k):
        return pltpu.make_async_copy(
            sib_hbm.at[rows(k), :], sib_ref.at[k * TILE : (k + 1) * TILE, :], sems.at[k]
        )

    copy(0).start()
    copy(2).start()
    for k in range(TILES):
        turned_ref[:, k * TILE : (k + 1) * TILE] = sib_info_ref[0:2, rows(k)]
    columns = [
        (to_column(lanes(info_ref, 0, i)), to_column(lanes(info_ref, 1, i))) for i in range(TILES)
    ]

    def both(i, other, row, bias):
        dots = lax.dot_general(part(x_ref, i), other, NT, preferred_element_type=F32)
        down = jnp.max(dots * columns[i][0] + columns[i][1], axis=0, keepdims=True)
        return fold_lanes(dots * row + bias), down

    def own(i):
        j = TILES - 1
        return both(i, part(x_ref, j), lanes(info_ref, 0, j), lanes(info_ref, 1, j))

    folds, downs = {}, {}
    folds[2], downs[2] = own(2)
    give = {}
    for i in range(TILES):
        if i == 0:
            copy(0).wait()
            copy(2).wait()
            copy(1).start()
            copy(3).start()
            folds[1], downs[1] = own(1)
        if i == 1:
            copy(1).wait()
            copy(3).wait()
        fold = folds.get(i)
        for k in (i, (i + 2) % TILES):
            value, down = both(i, part(sib_ref, k), lanes(turned_ref, 0, k), lanes(turned_ref, 1, k))
            fold = value if fold is None else jnp.maximum(fold, value)
            give[k] = jnp.maximum(give[k], down) if k in give else down
        best = jnp.maximum(
            lanes(before_ref, 0, i), to_row(jnp.max(fold, axis=1, keepdims=True))
        )
        if i == TILES - 1:
            best = jnp.maximum(best, jnp.maximum(downs[1], downs[2]))
        best_ref[:, i * TILE : (i + 1) * TILE] = best
    for k in range(TILES):
        give_ref[:, rows(k)] = give[k]


def centre_kernel(after_ref, x_ref, info_ref, sib_info_ref, centre_ref, mean_ref):
    total = info_ref[2:3, 0:WIDTH] + sib_info_ref[2:3, 0:WIDTH]
    count = info_ref[2:3, WIDTH : WIDTH + 1] + sib_info_ref[2:3, WIDTH : WIDTH + 1]
    mean = total / count
    folded = [mean[:, k : k + 128] for k in range(0, WIDTH, 128)]
    mean_ref[...] = jnp.concatenate(folded + [jnp.zeros((2, 128), F32)], axis=0)
    scale = lax.rsqrt(jnp.sum(total * total, axis=1, keepdims=True) / WIDTH + EPS)
    parts = jnp.concatenate(split3(total) + (jnp.zeros((13, WIDTH), BF16),), axis=0)
    toward = lax.dot_general(parts, x_ref[...], NT, preferred_element_type=F32)
    toward = toward[0:1] + toward[1:2] + toward[2:3]
    centre_ref[...] = toward * info_ref[0:1, :] * scale / WIDTH


def lines_kernel(place_ref, best_ref, taken_ref, info_ref, centre_ref, mean_ref, *refs):
    out_refs, near_ref = refs[:XS], refs[XS]
    best = jnp.maximum(best_ref[...], taken_ref[...])
    near_ref[...] = jnp.maximum(-1.0, best * info_ref[0:1, :] / WIDTH)
    for k in range(XS):
        first = ((place_ref[0, 0] + k) & 3) * TILE
        for line in range(4):
            lane = pl.ds(pl.multiple_of(first + line * 128, 128), 128)
            out_refs[k][line : line + 1, :] = near_ref[:, lane]
            out_refs[k][4 + line : 5 + line, :] = centre_ref[:, lane]
        out_refs[k][8:16, :] = mean_ref[...]


def merge_kernel(*refs):
    came, out_ref = refs[:XS], refs[XS]
    group, line = iota((8, 128), 1) // CAP, iota((8, 128), 0)
    for s in range(4):
        rows = [ref[4 * t + s : 4 * t + s + 1, :] for ref in came for t in range(2)]
        value = jnp.concatenate(rows, axis=0)
        out = jnp.zeros((8, 128), F32)
        for d in range(8):
            turned = pltpu.roll(value, CAP * d, 1) if d else value
            picked = jnp.sum(jnp.where(group == line, turned, 0.0), axis=0, keepdims=True)
            out = jnp.where(((group - line) & 7) == d, picked, out)
        out_ref[8 * s : 8 * (s + 1), :] = out


def unpack_kernel(place_ref, ids_ref, rank_ref, back_ref, *refs):
    came, (near_ref, centre_ref, mean_ref) = refs[:XS], refs[XS:]
    for k in range(2):
        offset = (place_ref[0, 0] - 2 * place_ref[0, 1] - k) & 3
        folded = sum(jnp.where(offset == i, ref[8:16, :], 0.0) for i, ref in enumerate(came))
        for j in range(WIDTH // 128):
            mean_ref[k : k + 1, j * 128 : (j + 1) * 128] = folded[j : j + 1]
    ids = ids_ref[...]
    same = iota((32, ROWS), 0) == ((ids >> 2) & 7) * 4 + (ids >> 5)
    onehot = same.astype(F32).astype(BF16)
    parts = jnp.concatenate(split3(back_ref[...]), axis=1)
    picked = lax.dot_general(parts, onehot, TN, preferred_element_type=F32)
    picked = picked[0:128] + picked[128:256] + picked[256:384]
    place = ((place_ref[0, 0] - ids) & 3) * PAIR + rank_ref[...]
    line = iota((128, ROWS), 0)
    near_ref[...] = jnp.sum(jnp.where(line == place, picked, 0.0), axis=0, keepdims=True)
    centre_ref[...] = jnp.sum(
        jnp.where(line == place + CAP, picked, 0.0), axis=0, keepdims=True
    )


def struct(shape, dtype):
    return jax.ShapeDtypeStruct(shape, dtype)


def call(kernel, outs, flops, scratch=(), grant=40, **specs):
    return pl.pallas_call(
        kernel,
        out_shape=outs,
        scratch_shapes=list(scratch),
        compiler_params=pltpu.CompilerParams(vmem_limit_bytes=grant * 1024 * 1024),
        cost_estimate=pl.CostEstimate(
            flops=int(flops), bytes_accessed=6_000_000, transcendentals=0
        ),
        **specs,
    )


def shards(embeddings, cluster_ids):
    ids = cluster_ids.reshape(1, ROWS)
    block = 2 * SLOTS * SLOTS * WIDTH
    here = pl.BlockSpec(memory_space=pltpu.VMEM)
    send, rank = call(
        pack_kernel,
        (struct((SLOTS, WIDTH), BF16), struct((1, ROWS), jnp.int32)),
        2 * SLOTS * ROWS * WIDTH,
        (pltpu.VMEM((ROWS, WIDTH), BF16), pltpu.SemaphoreType.DMA),
        in_specs=[here, pl.BlockSpec(memory_space=pltpu.HBM)],
    )(ids, embeddings)
    chips = ("x", "z", "y")
    mine = lax.all_to_all(send.reshape(CHIPS, CAP, WIDTH), chips, 0, 0, tiled=True)
    mine = mine.reshape(SLOTS, WIDTH)
    swap = [(0, 1), (1, 0)]
    sib = lax.ppermute(mine, "core", swap)
    row = struct((1, SLOTS), F32)
    info, best = call(diagonal_kernel, (struct((3, SLOTS), F32), row), block / 4)(mine)
    sib_info = lax.ppermute(info, "core", swap)
    fold = pltpu.VMEM((TILE, 128), F32)
    best = call(own_kernel, row, block * 3 / 8, (fold,))(mine, info, best)
    axes = [lax.axis_index("x"), lax.axis_index("core")]
    place = jnp.stack(axes).astype(jnp.int32).reshape(1, 2)
    scalars = pl.BlockSpec(memory_space=pltpu.SMEM)
    line = struct((16, 128), F32)
    best, give = call(
        across_kernel,
        (row, row),
        block / 2,
        (
            pltpu.VMEM((SLOTS, WIDTH), BF16),
            pltpu.VMEM((2, SLOTS), F32),
            pltpu.SemaphoreType.DMA((TILES,)),
        ),
        in_specs=[scalars, here, pl.BlockSpec(memory_space=pltpu.HBM), here, here, here],
    )(place, mine, sib, info, sib_info, best)
    taken = lax.ppermute(give, "core", swap)
    centre, mean = call(
        centre_kernel, (row, struct((8, 128), F32)), block / 8
    )(give, mine, info, sib_info)
    outs = call(
        lines_kernel,
        (line,) * XS,
        1e7,
        (pltpu.VMEM((1, SLOTS), F32),),
        in_specs=[scalars] + [here] * 5,
    )(place, best, taken, info, centre, mean)
    came = [outs[0]]
    for k in range(1, XS):
        came.append(lax.ppermute(outs[k], "x", [(i, (i + k) % XS) for i in range(XS)]))
    out = call(merge_kernel, struct((32, 128), F32), 1e6)(*came)
    back = lax.all_to_all(out, ("z", "y"), 0, 0, tiled=True)
    near, centre, means = call(
        unpack_kernel,
        (struct((1, ROWS), F32), struct((1, ROWS), F32), struct((2, WIDTH), F32)),
        1e8,
        in_specs=[scalars] + [here] * (3 + XS),
    )(place, ids, rank, back, *came)
    return near.reshape(ROWS), centre.reshape(ROWS), means


def solution(mesh):
    fine = Mesh(mesh.devices.reshape(4, 8, 2, 4), ("y", "z", "core", "x"))
    owner = ("y", "z", "core")
    every = owner + ("x",)
    return jax.shard_map(
        shards,
        mesh=fine,
        in_specs=(P(every, None), P(every, None)),
        out_specs=(P(every), P(every), P(owner, None)),
        check_vma=False,
    )
```

```python
import jax
import jax.numpy as jnp
from jax import lax
from jax.experimental import pallas as pl
from jax.experimental.pallas import tpu as pltpu
from jax.sharding import Mesh, PartitionSpec as P

EPS = 1e-06
ROWS = 1024
WIDTH = 768
CAP = 16
CHIPS = 128
XS = 4
PAIR = 2 * CAP
SLOTS = CHIPS * CAP
MARK = 64.0
LOW = -1e30
TILE = 512
TILES = SLOTS // TILE
NT = (((1,), (1,)), ((), ()))
TN = (((0,), (0,)), ((), ()))
F32 = jnp.float32
BF16 = jnp.bfloat16


def iota(shape, dim):
    return lax.broadcasted_iota(jnp.int32, shape, dim)


def split3(v):
    hi = v.astype(BF16)
    rest = v - hi.astype(F32)
    mid = rest.astype(BF16)
    lo = (rest - mid.astype(F32)).astype(BF16)
    return hi, mid, lo


def chip_of(ids):
    return (ids & 3) * 32 + ((ids >> 2) & 7) * 4 + (ids >> 5)


def eye(n):
    return iota((n, n), 0) == iota((n, n), 1)


def to_row(column):
    blocks = [
        jnp.sum(jnp.where(eye(128), column[k : k + 128], 0.0), axis=0, keepdims=True)
        for k in range(0, column.shape[0], 128)
    ]
    return jnp.concatenate(blocks, axis=1)


def to_column(row):
    blocks = [
        jnp.sum(jnp.where(eye(128), row[:, k : k + 128], 0.0), axis=1, keepdims=True)
        for k in range(0, row.shape[1], 128)
    ]
    return jnp.concatenate(blocks, axis=0)


def fold_lanes(value):
    best = value[:, 0:128]
    for k in range(128, value.shape[1], 128):
        best = jnp.maximum(best, value[:, k : k + 128])
    return best


def part(ref, i):
    return ref[i * TILE : (i + 1) * TILE, :]


def lanes(ref, row, i):
    return ref[row : row + 1, i * TILE : (i + 1) * TILE]


def pack_kernel(ids_ref, x_hbm, send_ref, rank_ref, x_ref, sem):
    copy = pltpu.make_async_copy(x_hbm, x_ref, sem)
    copy.start()
    chip = chip_of(ids_ref[...])
    same = iota((CHIPS, ROWS), 0) == chip
    onehot = same.astype(F32).astype(BF16)
    before = (iota((ROWS, ROWS), 0) < iota((ROWS, ROWS), 1)).astype(F32).astype(BF16)
    earlier = jnp.dot(onehot, before, preferred_element_type=F32)
    rank = jnp.sum(jnp.where(same, earlier, 0.0), axis=0, keepdims=True).astype(jnp.int32)
    rank_ref[...] = rank
    position = chip * CAP + rank
    step = 256
    copy.wait()
    for start in range(0, SLOTS, step):
        pick = (iota((step, ROWS), 0) + start == position).astype(F32)
        live = jnp.sum(pick, axis=1, keepdims=True)
        rows = jnp.dot(pick.astype(BF16), x_ref[...], preferred_element_type=F32)
        mark = jnp.where(iota((step, 128), 1) == 0, (1.0 - live) * MARK, 0.0)
        send_ref[start : start + step, 0:128] = (rows[:, 0:128] + mark).astype(BF16)
        send_ref[start : start + step, 128:] = rows[:, 128:].astype(BF16)


def diagonal_kernel(x_ref, info_ref, best_ref):
    first = x_ref[:, 0:1].astype(F32)
    live = to_row((first < MARK / 2).astype(F32))
    info_ref[1:2, :] = jnp.where(live > 0, 0.0, LOW)
    total = jnp.zeros((8, WIDTH), F32)
    for i in range(TILES):
        rows = part(x_ref, i).astype(F32)
        total = total + jnp.sum(rows.reshape(TILE // 8, 8, WIDTH), axis=0)
    total = jnp.sum(total, axis=0, keepdims=True)
    lead = jnp.sum(jnp.where(first < MARK / 2, first, 0.0), axis=0, keepdims=True)
    info_ref[2:3, 0:WIDTH] = jnp.where(iota((1, WIDTH), 1) == 0, lead, total)
    count = jnp.sum(live, axis=1, keepdims=True)
    info_ref[2:3, WIDTH:] = jnp.broadcast_to(count, (1, SLOTS - WIDTH))
    for i in range(TILES):
        dots = lax.dot_general(part(x_ref, i), part(x_ref, i), NT, preferred_element_type=F32)
        square = jnp.sum(jnp.where(eye(TILE), dots, 0.0), axis=0, keepdims=True)
        inv = lax.rsqrt(square / WIDTH + EPS)
        info_ref[0:1, i * TILE : (i + 1) * TILE] = inv
        value = jnp.where(eye(TILE), LOW, dots * inv + lanes(info_ref, 1, i))
        best = jnp.max(fold_lanes(value), axis=1, keepdims=True)
        best_ref[:, i * TILE : (i + 1) * TILE] = to_row(best)


def own_kernel(x_ref, info_ref, before_ref, best_ref, fold_ref):
    best_ref[...] = before_ref[...]
    for i in range(TILES - 2):
        inv = to_column(lanes(info_ref, 0, i))
        bias = to_column(lanes(info_ref, 1, i))
        for j in range(i + 1, TILES):
            dots = lax.dot_general(part(x_ref, i), part(x_ref, j), NT, preferred_element_type=F32)
            fold = fold_lanes(dots * lanes(info_ref, 0, j) + lanes(info_ref, 1, j))
            fold_ref[...] = fold if j == i + 1 else jnp.maximum(fold_ref[...], fold)
            down = jnp.max(dots * inv + bias, axis=0, keepdims=True)
            best_ref[:, j * TILE : (j + 1) * TILE] = jnp.maximum(lanes(best_ref, 0, j), down)
        best = to_row(jnp.max(fold_ref[...], axis=1, keepdims=True))
        best_ref[:, i * TILE : (i + 1) * TILE] = jnp.maximum(lanes(best_ref, 0, i), best)


def across_kernel(
    place_ref, x_ref, sib_hbm, info_ref, sib_info_ref, before_ref,
    best_ref, give_ref, sib_ref, turned_ref, sems,
):
    core = place_ref[0, 1]

    def rows(k):
        return pl.ds(pl.multiple_of(((core + k) & 3) * TILE, TILE), TILE)

    def copy(k):
        return pltpu.make_async_copy(
            sib_hbm.at[rows(k), :], sib_ref.at[k * TILE : (k + 1) * TILE, :], sems.at[k]
        )

    copy(0).start()
    copy(2).start()
    for k in range(TILES):
        turned_ref[:, k * TILE : (k + 1) * TILE] = sib_info_ref[0:2, rows(k)]
    columns = [
        (to_column(lanes(info_ref, 0, i)), to_column(lanes(info_ref, 1, i))) for i in range(TILES)
    ]

    def both(i, other, row, bias):
        dots = lax.dot_general(part(x_ref, i), other, NT, preferred_element_type=F32)
        down = jnp.max(dots * columns[i][0] + columns[i][1], axis=0, keepdims=True)
        return fold_lanes(dots * row + bias), down

    j = TILES - 1
    last, own = both(2, part(x_ref, j), lanes(info_ref, 0, j), lanes(info_ref, 1, j))
    give = {}
    for i in range(TILES):
        if i == 0:
            copy(0).wait()
            copy(2).wait()
            copy(1).start()
            copy(3).start()
        if i == 1:
            copy(1).wait()
            copy(3).wait()
        fold = last if i == 2 else None
        for k in (i, (i + 2) % TILES):
            value, down = both(i, part(sib_ref, k), lanes(turned_ref, 0, k), lanes(turned_ref, 1, k))
            fold = value if fold is None else jnp.maximum(fold, value)
            give[k] = jnp.maximum(give[k], down) if k in give else down
        best = jnp.maximum(
            lanes(before_ref, 0, i), to_row(jnp.max(fold, axis=1, keepdims=True))
        )
        if i == TILES - 1:
            best = jnp.maximum(best, own)
        best_ref[:, i * TILE : (i + 1) * TILE] = best
    for k in range(TILES):
        give_ref[:, rows(k)] = give[k]


def centre_kernel(after_ref, x_ref, info_ref, sib_info_ref, centre_ref, mean_ref):
    total = info_ref[2:3, 0:WIDTH] + sib_info_ref[2:3, 0:WIDTH]
    count = info_ref[2:3, WIDTH : WIDTH + 1] + sib_info_ref[2:3, WIDTH : WIDTH + 1]
    mean = total / count
    folded = [mean[:, k : k + 128] for k in range(0, WIDTH, 128)]
    mean_ref[...] = jnp.concatenate(folded + [jnp.zeros((2, 128), F32)], axis=0)
    scale = lax.rsqrt(jnp.sum(total * total, axis=1, keepdims=True) / WIDTH + EPS)
    parts = jnp.concatenate(split3(total) + (jnp.zeros((13, WIDTH), BF16),), axis=0)
    toward = lax.dot_general(parts, x_ref[...], NT, preferred_element_type=F32)
    toward = toward[0:1] + toward[1:2] + toward[2:3]
    centre_ref[...] = toward * info_ref[0:1, :] * scale / WIDTH


def lines_kernel(place_ref, best_ref, taken_ref, info_ref, centre_ref, mean_ref, *refs):
    out_refs, near_ref = refs[:XS], refs[XS]
    best = jnp.maximum(best_ref[...], taken_ref[...])
    near_ref[...] = jnp.maximum(-1.0, best * info_ref[0:1, :] / WIDTH)
    for k in range(XS):
        first = ((place_ref[0, 0] + k) & 3) * TILE
        for line in range(4):
            lane = pl.ds(pl.multiple_of(first + line * 128, 128), 128)
            out_refs[k][line : line + 1, :] = near_ref[:, lane]
            out_refs[k][4 + line : 5 + line, :] = centre_ref[:, lane]
        out_refs[k][8:16, :] = mean_ref[...]


def merge_kernel(*refs):
    came, out_ref = refs[:XS], refs[XS]
    group, line = iota((8, 128), 1) // CAP, iota((8, 128), 0)
    for s in range(4):
        rows = [ref[4 * t + s : 4 * t + s + 1, :] for ref in came for t in range(2)]
        value = jnp.concatenate(rows, axis=0)
        out = jnp.zeros((8, 128), F32)
        for d in range(8):
            turned = pltpu.roll(value, CAP * d, 1) if d else value
            picked = jnp.sum(jnp.where(group == line, turned, 0.0), axis=0, keepdims=True)
            out = jnp.where(((group - line) & 7) == d, picked, out)
        out_ref[8 * s : 8 * (s + 1), :] = out


def unpack_kernel(place_ref, ids_ref, rank_ref, back_ref, *refs):
    came, (near_ref, centre_ref, mean_ref) = refs[:XS], refs[XS:]
    for k in range(2):
        offset = (place_ref[0, 0] - 2 * place_ref[0, 1] - k) & 3
        folded = sum(jnp.where(offset == i, ref[8:16, :], 0.0) for i, ref in enumerate(came))
        for j in range(WIDTH // 128):
            mean_ref[k : k + 1, j * 128 : (j + 1) * 128] = folded[j : j + 1]
    ids = ids_ref[...]
    same = iota((32, ROWS), 0) == ((ids >> 2) & 7) * 4 + (ids >> 5)
    onehot = same.astype(F32).astype(BF16)
    parts = jnp.concatenate(split3(back_ref[...]), axis=1)
    picked = lax.dot_general(parts, onehot, TN, preferred_element_type=F32)
    picked = picked[0:128] + picked[128:256] + picked[256:384]
    place = ((place_ref[0, 0] - ids) & 3) * PAIR + rank_ref[...]
    line = iota((128, ROWS), 0)
    near_ref[...] = jnp.sum(jnp.where(line == place, picked, 0.0), axis=0, keepdims=True)
    centre_ref[...] = jnp.sum(
        jnp.where(line == place + CAP, picked, 0.0), axis=0, keepdims=True
    )


def struct(shape, dtype):
    return jax.ShapeDtypeStruct(shape, dtype)


def call(kernel, outs, flops, scratch=(), grant=40, **specs):
    return pl.pallas_call(
        kernel,
        out_shape=outs,
        scratch_shapes=list(scratch),
        compiler_params=pltpu.CompilerParams(vmem_limit_bytes=grant * 1024 * 1024),
        cost_estimate=pl.CostEstimate(
            flops=int(flops), bytes_accessed=6_000_000, transcendentals=0
        ),
        **specs,
    )


def shards(embeddings, cluster_ids):
    ids = cluster_ids.reshape(1, ROWS)
    block = 2 * SLOTS * SLOTS * WIDTH
    here = pl.BlockSpec(memory_space=pltpu.VMEM)
    send, rank = call(
        pack_kernel,
        (struct((SLOTS, WIDTH), BF16), struct((1, ROWS), jnp.int32)),
        2 * SLOTS * ROWS * WIDTH,
        (pltpu.VMEM((ROWS, WIDTH), BF16), pltpu.SemaphoreType.DMA),
        in_specs=[here, pl.BlockSpec(memory_space=pltpu.HBM)],
    )(ids, embeddings)
    chips = ("x", "z", "y")
    mine = lax.all_to_all(send.reshape(CHIPS, CAP, WIDTH), chips, 0, 0, tiled=True)
    mine = mine.reshape(SLOTS, WIDTH)
    swap = [(0, 1), (1, 0)]
    sib = lax.ppermute(mine, "core", swap)
    row = struct((1, SLOTS), F32)
    info, best = call(diagonal_kernel, (struct((3, SLOTS), F32), row), block / 4)(mine)
    sib_info = lax.ppermute(info, "core", swap)
    fold = pltpu.VMEM((TILE, 128), F32)
    best = call(own_kernel, row, block * 3 / 8, (fold,))(mine, info, best)
    axes = [lax.axis_index("x"), lax.axis_index("core")]
    place = jnp.stack(axes).astype(jnp.int32).reshape(1, 2)
    scalars = pl.BlockSpec(memory_space=pltpu.SMEM)
    line = struct((16, 128), F32)
    best, give = call(
        across_kernel,
        (row, row),
        block / 2,
        (
            pltpu.VMEM((SLOTS, WIDTH), BF16),
            pltpu.VMEM((2, SLOTS), F32),
            pltpu.SemaphoreType.DMA((TILES,)),
        ),
        in_specs=[scalars, here, pl.BlockSpec(memory_space=pltpu.HBM), here, here, here],
    )(place, mine, sib, info, sib_info, best)
    taken = lax.ppermute(give, "core", swap)
    centre, mean = call(
        centre_kernel, (row, struct((8, 128), F32)), block / 8
    )(give, mine, info, sib_info)
    outs = call(
        lines_kernel,
        (line,) * XS,
        1e7,
        (pltpu.VMEM((1, SLOTS), F32),),
        in_specs=[scalars] + [here] * 5,
    )(place, best, taken, info, centre, mean)
    came = [outs[0]]
    for k in range(1, XS):
        came.append(lax.ppermute(outs[k], "x", [(i, (i + k) % XS) for i in range(XS)]))
    out = call(merge_kernel, struct((32, 128), F32), 1e6)(*came)
    back = lax.all_to_all(out, ("z", "y"), 0, 0, tiled=True)
    near, centre, means = call(
        unpack_kernel,
        (struct((1, ROWS), F32), struct((1, ROWS), F32), struct((2, WIDTH), F32)),
        1e8,
        in_specs=[scalars] + [here] * (3 + XS),
    )(place, ids, rank, back, *came)
    return near.reshape(ROWS), centre.reshape(ROWS), means


def solution(mesh):
    fine = Mesh(mesh.devices.reshape(4, 8, 2, 4), ("y", "z", "core", "x"))
    owner = ("y", "z", "core")
    every = owner + ("x",)
    return jax.shard_map(
        shards,
        mesh=fine,
        in_specs=(P(every, None), P(every, None)),
        out_specs=(P(every), P(every), P(owner, None)),
        check_vma=False,
    )
```

```python
import jax
import jax.numpy as jnp
from jax import lax
from jax.experimental import pallas as pl
from jax.experimental.pallas import tpu as pltpu
from jax.sharding import Mesh, PartitionSpec as P

EPS = 1e-06
ROWS = 1024
WIDTH = 768
CAP = 16
CHIPS = 128
XS = 4
PAIR = 2 * CAP
SLOTS = CHIPS * CAP
MARK = 64.0
LOW = -1e30
TILE = 512
TILES = SLOTS // TILE
NT = (((1,), (1,)), ((), ()))
TN = (((0,), (0,)), ((), ()))
F32 = jnp.float32
BF16 = jnp.bfloat16


def iota(shape, dim):
    return lax.broadcasted_iota(jnp.int32, shape, dim)


def split3(v):
    hi = v.astype(BF16)
    rest = v - hi.astype(F32)
    mid = rest.astype(BF16)
    lo = (rest - mid.astype(F32)).astype(BF16)
    return hi, mid, lo


def chip_of(ids):
    return (ids & 3) * 32 + ((ids >> 2) & 7) * 4 + (ids >> 5)


def eye(n):
    return iota((n, n), 0) == iota((n, n), 1)


def to_row(column):
    blocks = [
        jnp.sum(jnp.where(eye(128), column[k : k + 128], 0.0), axis=0, keepdims=True)
        for k in range(0, column.shape[0], 128)
    ]
    return jnp.concatenate(blocks, axis=1)


def to_column(row):
    blocks = [
        jnp.sum(jnp.where(eye(128), row[:, k : k + 128], 0.0), axis=1, keepdims=True)
        for k in range(0, row.shape[1], 128)
    ]
    return jnp.concatenate(blocks, axis=0)


def fold_lanes(value):
    best = value[:, 0:128]
    for k in range(128, value.shape[1], 128):
        best = jnp.maximum(best, value[:, k : k + 128])
    return best


def part(ref, i):
    return ref[i * TILE : (i + 1) * TILE, :]


def lanes(ref, row, i):
    return ref[row : row + 1, i * TILE : (i + 1) * TILE]


def pack_kernel(ids_ref, x_hbm, send_ref, rank_ref, x_ref, sem):
    copy = pltpu.make_async_copy(x_hbm, x_ref, sem)
    copy.start()
    chip = chip_of(ids_ref[...])
    same = iota((CHIPS, ROWS), 0) == chip
    onehot = same.astype(F32).astype(BF16)
    before = (iota((ROWS, ROWS), 0) < iota((ROWS, ROWS), 1)).astype(F32).astype(BF16)
    earlier = jnp.dot(onehot, before, preferred_element_type=F32)
    rank = jnp.sum(jnp.where(same, earlier, 0.0), axis=0, keepdims=True).astype(jnp.int32)
    rank_ref[...] = rank
    position = chip * CAP + rank
    step = 256
    copy.wait()
    for start in range(0, SLOTS, step):
        pick = (iota((step, ROWS), 0) + start == position).astype(F32)
        live = jnp.sum(pick, axis=1, keepdims=True)
        rows = jnp.dot(pick.astype(BF16), x_ref[...], preferred_element_type=F32)
        mark = jnp.where(iota((step, 128), 1) == 0, (1.0 - live) * MARK, 0.0)
        send_ref[start : start + step, 0:128] = (rows[:, 0:128] + mark).astype(BF16)
        send_ref[start : start + step, 128:] = rows[:, 128:].astype(BF16)


def diagonal_kernel(x_ref, info_ref, best_ref):
    live = to_row((x_ref[:, 0:1].astype(F32) < MARK / 2).astype(F32))
    weights = jnp.broadcast_to(live, (8, SLOTS)).astype(BF16)
    totals = jnp.dot(weights, x_ref[...], preferred_element_type=F32)
    info_ref[1:2, :] = jnp.where(live > 0, 0.0, LOW)
    info_ref[2:3, 0:WIDTH] = totals[0:1]
    count = jnp.sum(live, axis=1, keepdims=True)
    info_ref[2:3, WIDTH:] = jnp.broadcast_to(count, (1, SLOTS - WIDTH))
    for i in range(TILES):
        dots = lax.dot_general(part(x_ref, i), part(x_ref, i), NT, preferred_element_type=F32)
        square = jnp.sum(jnp.where(eye(TILE), dots, 0.0), axis=0, keepdims=True)
        inv = lax.rsqrt(square / WIDTH + EPS)
        info_ref[0:1, i * TILE : (i + 1) * TILE] = inv
        value = jnp.where(eye(TILE), LOW, dots * inv + lanes(info_ref, 1, i))
        best = jnp.max(fold_lanes(value), axis=1, keepdims=True)
        best_ref[:, i * TILE : (i + 1) * TILE] = to_row(best)


def own_kernel(x_ref, info_ref, before_ref, best_ref, fold_ref):
    best_ref[...] = before_ref[...]
    for i in range(TILES - 2):
        inv = to_column(lanes(info_ref, 0, i))
        bias = to_column(lanes(info_ref, 1, i))
        for j in range(i + 1, TILES - i):
            dots = lax.dot_general(part(x_ref, i), part(x_ref, j), NT, preferred_element_type=F32)
            fold = fold_lanes(dots * lanes(info_ref, 0, j) + lanes(info_ref, 1, j))
            fold_ref[...] = fold if j == i + 1 else jnp.maximum(fold_ref[...], fold)
            down = jnp.max(dots * inv + bias, axis=0, keepdims=True)
            best_ref[:, j * TILE : (j + 1) * TILE] = jnp.maximum(lanes(best_ref, 0, j), down)
        best = to_row(jnp.max(fold_ref[...], axis=1, keepdims=True))
        best_ref[:, i * TILE : (i + 1) * TILE] = jnp.maximum(lanes(best_ref, 0, i), best)


def across_kernel(
    x_ref, sib_hbm, info_ref, sib_info_ref, before_ref,
    best_ref, give_ref, sib_ref, turned_ref, sems,
):
    core = lax.axis_index("core")

    def rows(k):
        return pl.ds(pl.multiple_of(((core + k) & 3) * TILE, TILE), TILE)

    def copy(k):
        return pltpu.make_async_copy(
            sib_hbm.at[rows(k), :], sib_ref.at[k * TILE : (k + 1) * TILE, :], sems.at[k]
        )

    copy(0).start()
    copy(2).start()
    for k in range(TILES):
        turned_ref[:, k * TILE : (k + 1) * TILE] = sib_info_ref[0:2, rows(k)]
    columns = [
        (to_column(lanes(info_ref, 0, i)), to_column(lanes(info_ref, 1, i))) for i in range(TILES)
    ]

    def both(i, other, row, bias):
        dots = lax.dot_general(part(x_ref, i), other, NT, preferred_element_type=F32)
        down = jnp.max(dots * columns[i][0] + columns[i][1], axis=0, keepdims=True)
        return fold_lanes(dots * row + bias), down

    def own(i):
        j = TILES - 1
        return both(i, part(x_ref, j), lanes(info_ref, 0, j), lanes(info_ref, 1, j))

    folds, downs = {}, {}
    folds[2], downs[2] = own(2)
    give = {}
    for i in range(TILES):
        if i == 0:
            copy(0).wait()
            copy(2).wait()
            copy(1).start()
            copy(3).start()
            folds[1], downs[1] = own(1)
        if i == 1:
            copy(1).wait()
            copy(3).wait()
        fold = folds.get(i)
        for k in (i, (i + 2) % TILES):
            value, down = both(i, part(sib_ref, k), lanes(turned_ref, 0, k), lanes(turned_ref, 1, k))
            fold = value if fold is None else jnp.maximum(fold, value)
            give[k] = jnp.maximum(give[k], down) if k in give else down
        best = jnp.maximum(
            lanes(before_ref, 0, i), to_row(jnp.max(fold, axis=1, keepdims=True))
        )
        if i == TILES - 1:
            best = jnp.maximum(best, jnp.maximum(downs[1], downs[2]))
        best_ref[:, i * TILE : (i + 1) * TILE] = best
    for k in range(TILES):
        give_ref[:, rows(k)] = give[k]


def centre_kernel(after_ref, x_ref, info_ref, sib_info_ref, centre_ref, mean_ref):
    total = info_ref[2:3, 0:WIDTH] + sib_info_ref[2:3, 0:WIDTH]
    count = info_ref[2:3, WIDTH : WIDTH + 1] + sib_info_ref[2:3, WIDTH : WIDTH + 1]
    mean = total / count
    folded = [mean[:, k : k + 128] for k in range(0, WIDTH, 128)]
    mean_ref[...] = jnp.concatenate(folded + [jnp.zeros((2, 128), F32)], axis=0)
    scale = lax.rsqrt(jnp.sum(total * total, axis=1, keepdims=True) / WIDTH + EPS)
    parts = jnp.concatenate(split3(total) + (jnp.zeros((13, WIDTH), BF16),), axis=0)
    toward = lax.dot_general(parts, x_ref[...], NT, preferred_element_type=F32)
    toward = toward[0:1] + toward[1:2] + toward[2:3]
    centre_ref[...] = toward * info_ref[0:1, :] * scale / WIDTH


def lines_kernel(best_ref, taken_ref, info_ref, centre_ref, mean_ref, *refs):
    out_refs, near_ref = refs[:XS], refs[XS]
    best = jnp.maximum(best_ref[...], taken_ref[...])
    near_ref[...] = jnp.maximum(-1.0, best * info_ref[0:1, :] / WIDTH)
    for k in range(XS):
        first = ((lax.axis_index("x") + k) & 3) * TILE
        for line in range(4):
            lane = pl.ds(pl.multiple_of(first + line * 128, 128), 128)
            out_refs[k][line : line + 1, :] = near_ref[:, lane]
            out_refs[k][4 + line : 5 + line, :] = centre_ref[:, lane]
        out_refs[k][8:16, :] = mean_ref[...]


def merge_kernel(*refs):
    came, out_ref = refs[:XS], refs[XS]
    group, line = iota((8, 128), 1) // CAP, iota((8, 128), 0)
    for s in range(4):
        rows = [ref[4 * t + s : 4 * t + s + 1, :] for ref in came for t in range(2)]
        value = jnp.concatenate(rows, axis=0)
        out = jnp.zeros((8, 128), F32)
        for d in range(8):
            turned = pltpu.roll(value, CAP * d, 1) if d else value
            picked = jnp.sum(jnp.where(group == line, turned, 0.0), axis=0, keepdims=True)
            out = jnp.where(((group - line) & 7) == d, picked, out)
        out_ref[8 * s : 8 * (s + 1), :] = out


def unpack_kernel(ids_ref, rank_ref, back_ref, *refs):
    came, (near_ref, centre_ref, mean_ref) = refs[:XS], refs[XS:]
    x, core = lax.axis_index("x"), lax.axis_index("core")
    for k in range(2):
        offset = (x - 2 * core - k) & 3
        folded = sum(jnp.where(offset == i, ref[8:16, :], 0.0) for i, ref in enumerate(came))
        for j in range(WIDTH // 128):
            mean_ref[k : k + 1, j * 128 : (j + 1) * 128] = folded[j : j + 1]
    ids = ids_ref[...]
    same = iota((32, ROWS), 0) == ((ids >> 2) & 7) * 4 + (ids >> 5)
    onehot = same.astype(F32).astype(BF16)
    parts = jnp.concatenate(split3(back_ref[...]), axis=1)
    picked = lax.dot_general(parts, onehot, TN, preferred_element_type=F32)
    picked = picked[0:128] + picked[128:256] + picked[256:384]
    place = ((x - ids) & 3) * PAIR + rank_ref[...]
    line = iota((128, ROWS), 0)
    near_ref[...] = jnp.sum(jnp.where(line == place, picked, 0.0), axis=0, keepdims=True)
    centre_ref[...] = jnp.sum(
        jnp.where(line == place + CAP, picked, 0.0), axis=0, keepdims=True
    )


def struct(shape, dtype):
    return jax.ShapeDtypeStruct(shape, dtype)


def call(kernel, outs, flops, scratch=(), grant=40, **specs):
    return pl.pallas_call(
        kernel,
        out_shape=outs,
        scratch_shapes=list(scratch),
        compiler_params=pltpu.CompilerParams(vmem_limit_bytes=grant * 1024 * 1024),
        cost_estimate=pl.CostEstimate(
            flops=int(flops), bytes_accessed=6_000_000, transcendentals=0
        ),
        **specs,
    )


def shards(embeddings, cluster_ids):
    ids = cluster_ids.reshape(1, ROWS)
    block = 2 * SLOTS * SLOTS * WIDTH
    here = pl.BlockSpec(memory_space=pltpu.VMEM)
    send, rank = call(
        pack_kernel,
        (struct((SLOTS, WIDTH), BF16), struct((1, ROWS), jnp.int32)),
        2 * SLOTS * ROWS * WIDTH,
        (pltpu.VMEM((ROWS, WIDTH), BF16), pltpu.SemaphoreType.DMA),
        in_specs=[here, pl.BlockSpec(memory_space=pltpu.HBM)],
    )(ids, embeddings)
    chips = ("x", "z", "y")
    mine = lax.all_to_all(send.reshape(CHIPS, CAP, WIDTH), chips, 0, 0, tiled=True)
    mine = mine.reshape(SLOTS, WIDTH)
    swap = [(0, 1), (1, 0)]
    sib = lax.ppermute(mine, "core", swap)
    row = struct((1, SLOTS), F32)
    info, best = call(diagonal_kernel, (struct((3, SLOTS), F32), row), block / 4)(mine)
    sib_info = lax.ppermute(info, "core", swap)
    fold = pltpu.VMEM((TILE, 128), F32)
    best = call(own_kernel, row, block * 3 / 8, (fold,))(mine, info, best)
    line = struct((16, 128), F32)
    best, give = call(
        across_kernel,
        (row, row),
        block / 2,
        (
            pltpu.VMEM((SLOTS, WIDTH), BF16),
            pltpu.VMEM((2, SLOTS), F32),
            pltpu.SemaphoreType.DMA((TILES,)),
        ),
        in_specs=[here, pl.BlockSpec(memory_space=pltpu.HBM), here, here, here],
    )(mine, sib, info, sib_info, best)
    taken = lax.ppermute(give, "core", swap)
    centre, mean = call(
        centre_kernel, (row, struct((8, 128), F32)), block / 8
    )(give, mine, info, sib_info)
    outs = call(
        lines_kernel,
        (line,) * XS,
        1e7,
        (pltpu.VMEM((1, SLOTS), F32),),
    )(best, taken, info, centre, mean)
    came = [outs[0]]
    for k in range(1, XS):
        came.append(lax.ppermute(outs[k], "x", [(i, (i + k) % XS) for i in range(XS)]))
    out = call(merge_kernel, struct((32, 128), F32), 1e6)(*came)
    back = lax.all_to_all(out, ("z", "y"), 0, 0, tiled=True)
    near, centre, means = call(
        unpack_kernel,
        (struct((1, ROWS), F32), struct((1, ROWS), F32), struct((2, WIDTH), F32)),
        1e8,
    )(ids, rank, back, *came)
    return near.reshape(ROWS), centre.reshape(ROWS), means


def solution(mesh):
    fine = Mesh(mesh.devices.reshape(4, 8, 2, 4), ("y", "z", "core", "x"))
    owner = ("y", "z", "core")
    every = owner + ("x",)
    return jax.shard_map(
        shards,
        mesh=fine,
        in_specs=(P(every, None), P(every, None)),
        out_specs=(P(every), P(every), P(owner, None)),
        check_vma=False,
    )
```

```python
import jax
import jax.numpy as jnp
from jax import lax
from jax.experimental import pallas as pl
from jax.experimental.pallas import tpu as pltpu
from jax.sharding import Mesh, PartitionSpec as P

EPS = 1e-06
ROWS = 1024
WIDTH = 768
CAP = 16
CHIPS = 128
XS = 4
PAIR = 2 * CAP
SLOTS = CHIPS * CAP
MARK = 64.0
LOW = -1e30
TILE = 512
TILES = SLOTS // TILE
NT = (((1,), (1,)), ((), ()))
TN = (((0,), (0,)), ((), ()))
F32 = jnp.float32
BF16 = jnp.bfloat16


def iota(shape, dim):
    return lax.broadcasted_iota(jnp.int32, shape, dim)


def split3(v):
    hi = v.astype(BF16)
    rest = v - hi.astype(F32)
    mid = rest.astype(BF16)
    lo = (rest - mid.astype(F32)).astype(BF16)
    return hi, mid, lo


def chip_of(ids):
    return (ids & 3) * 32 + ((ids >> 2) & 7) * 4 + (ids >> 5)


def eye(n):
    return iota((n, n), 0) == iota((n, n), 1)


def to_row(column):
    blocks = [
        jnp.sum(jnp.where(eye(128), column[k : k + 128], 0.0), axis=0, keepdims=True)
        for k in range(0, column.shape[0], 128)
    ]
    return jnp.concatenate(blocks, axis=1)


def to_column(row):
    blocks = [
        jnp.sum(jnp.where(eye(128), row[:, k : k + 128], 0.0), axis=1, keepdims=True)
        for k in range(0, row.shape[1], 128)
    ]
    return jnp.concatenate(blocks, axis=0)


def fold_lanes(value):
    best = value[:, 0:128]
    for k in range(128, value.shape[1], 128):
        best = jnp.maximum(best, value[:, k : k + 128])
    return best


def part(ref, i):
    return ref[i * TILE : (i + 1) * TILE, :]


def lanes(ref, row, i):
    return ref[row : row + 1, i * TILE : (i + 1) * TILE]


def rank_kernel(ids_ref, rank_ref, slot_ref):
    chip = chip_of(ids_ref[...])
    same = iota((CHIPS, ROWS), 0) == chip
    onehot = same.astype(F32).astype(BF16)
    before = (iota((ROWS, ROWS), 0) < iota((ROWS, ROWS), 1)).astype(F32).astype(BF16)
    earlier = jnp.dot(onehot, before, preferred_element_type=F32)
    rank = jnp.sum(jnp.where(same, earlier, 0.0), axis=0, keepdims=True).astype(jnp.int32)
    rank_ref[...] = rank
    slot_ref[...] = chip * CAP + rank


def pack_kernel(slot_ref, x_ref, send_ref):
    position = slot_ref[...]
    step = 256
    for start in range(0, SLOTS, step):
        pick = (iota((step, ROWS), 0) + start == position).astype(F32)
        live = jnp.sum(pick, axis=1, keepdims=True)
        rows = jnp.dot(pick.astype(BF16), x_ref[...], preferred_element_type=F32)
        mark = jnp.where(iota((step, 128), 1) == 0, (1.0 - live) * MARK, 0.0)
        send_ref[start : start + step, 0:128] = (rows[:, 0:128] + mark).astype(BF16)
        send_ref[start : start + step, 128:] = rows[:, 128:].astype(BF16)


def diagonal_kernel(x_ref, info_ref, best_ref):
    live = to_row((x_ref[:, 0:1].astype(F32) < MARK / 2).astype(F32))
    weights = jnp.broadcast_to(live, (8, SLOTS)).astype(BF16)
    totals = jnp.dot(weights, x_ref[...], preferred_element_type=F32)
    info_ref[1:2, :] = jnp.where(live > 0, 0.0, LOW)
    info_ref[2:3, 0:WIDTH] = totals[0:1]
    count = jnp.sum(live, axis=1, keepdims=True)
    info_ref[2:3, WIDTH:] = jnp.broadcast_to(count, (1, SLOTS - WIDTH))
    for i in range(TILES):
        dots = lax.dot_general(part(x_ref, i), part(x_ref, i), NT, preferred_element_type=F32)
        square = jnp.sum(jnp.where(eye(TILE), dots, 0.0), axis=0, keepdims=True)
        inv = lax.rsqrt(square / WIDTH + EPS)
        info_ref[0:1, i * TILE : (i + 1) * TILE] = inv
        value = jnp.where(eye(TILE), LOW, dots * inv + lanes(info_ref, 1, i))
        best = jnp.max(fold_lanes(value), axis=1, keepdims=True)
        best_ref[:, i * TILE : (i + 1) * TILE] = to_row(best)


def own_kernel(x_ref, info_ref, before_ref, best_ref, fold_ref):
    best_ref[...] = before_ref[...]
    for i in range(TILES - 2):
        inv = to_column(lanes(info_ref, 0, i))
        bias = to_column(lanes(info_ref, 1, i))
        for j in range(i + 1, TILES - i):
            dots = lax.dot_general(part(x_ref, i), part(x_ref, j), NT, preferred_element_type=F32)
            fold = fold_lanes(dots * lanes(info_ref, 0, j) + lanes(info_ref, 1, j))
            fold_ref[...] = fold if j == i + 1 else jnp.maximum(fold_ref[...], fold)
            down = jnp.max(dots * inv + bias, axis=0, keepdims=True)
            best_ref[:, j * TILE : (j + 1) * TILE] = jnp.maximum(lanes(best_ref, 0, j), down)
        best = to_row(jnp.max(fold_ref[...], axis=1, keepdims=True))
        best_ref[:, i * TILE : (i + 1) * TILE] = jnp.maximum(lanes(best_ref, 0, i), best)


def across_kernel(
    x_ref, sib_hbm, info_ref, sib_info_ref, before_ref,
    best_ref, give_ref, sib_ref, turned_ref, sems,
):
    core = lax.axis_index("core")

    def rows(k):
        return pl.ds(pl.multiple_of(((core + k) & 3) * TILE, TILE), TILE)

    def copy(k):
        return pltpu.make_async_copy(
            sib_hbm.at[rows(k), :], sib_ref.at[k * TILE : (k + 1) * TILE, :], sems.at[k]
        )

    copy(0).start()
    copy(2).start()
    for k in range(TILES):
        turned_ref[:, k * TILE : (k + 1) * TILE] = sib_info_ref[0:2, rows(k)]
    columns = [
        (to_column(lanes(info_ref, 0, i)), to_column(lanes(info_ref, 1, i))) for i in range(TILES)
    ]

    def both(i, other, row, bias):
        dots = lax.dot_general(part(x_ref, i), other, NT, preferred_element_type=F32)
        down = jnp.max(dots * columns[i][0] + columns[i][1], axis=0, keepdims=True)
        return fold_lanes(dots * row + bias), down

    def own(i):
        j = TILES - 1
        return both(i, part(x_ref, j), lanes(info_ref, 0, j), lanes(info_ref, 1, j))

    folds, downs = {}, {}
    folds[2], downs[2] = own(2)
    give = {}
    for i in range(TILES):
        if i == 0:
            copy(0).wait()
            copy(2).wait()
            copy(1).start()
            copy(3).start()
            folds[1], downs[1] = own(1)
        if i == 1:
            copy(1).wait()
            copy(3).wait()
        fold = folds.get(i)
        for k in (i, (i + 2) % TILES):
            value, down = both(i, part(sib_ref, k), lanes(turned_ref, 0, k), lanes(turned_ref, 1, k))
            fold = value if fold is None else jnp.maximum(fold, value)
            give[k] = jnp.maximum(give[k], down) if k in give else down
        best = jnp.maximum(
            lanes(before_ref, 0, i), to_row(jnp.max(fold, axis=1, keepdims=True))
        )
        if i == TILES - 1:
            best = jnp.maximum(best, jnp.maximum(downs[1], downs[2]))
        best_ref[:, i * TILE : (i + 1) * TILE] = best
    for k in range(TILES):
        give_ref[:, rows(k)] = give[k]


def centre_kernel(after_ref, x_ref, info_ref, sib_info_ref, centre_ref, mean_ref):
    total = info_ref[2:3, 0:WIDTH] + sib_info_ref[2:3, 0:WIDTH]
    count = info_ref[2:3, WIDTH : WIDTH + 1] + sib_info_ref[2:3, WIDTH : WIDTH + 1]
    mean = total / count
    folded = [mean[:, k : k + 128] for k in range(0, WIDTH, 128)]
    mean_ref[...] = jnp.concatenate(folded + [jnp.zeros((2, 128), F32)], axis=0)
    scale = lax.rsqrt(jnp.sum(total * total, axis=1, keepdims=True) / WIDTH + EPS)
    parts = jnp.concatenate(split3(total) + (jnp.zeros((13, WIDTH), BF16),), axis=0)
    toward = lax.dot_general(parts, x_ref[...], NT, preferred_element_type=F32)
    toward = toward[0:1] + toward[1:2] + toward[2:3]
    centre_ref[...] = toward * info_ref[0:1, :] * scale / WIDTH


def lines_kernel(best_ref, taken_ref, info_ref, centre_ref, mean_ref, *refs):
    out_refs, near_ref = refs[:XS], refs[XS]
    best = jnp.maximum(best_ref[...], taken_ref[...])
    near_ref[...] = jnp.maximum(-1.0, best * info_ref[0:1, :] / WIDTH)
    for k in range(XS):
        first = ((lax.axis_index("x") + k) & 3) * TILE
        for line in range(4):
            lane = pl.ds(pl.multiple_of(first + line * 128, 128), 128)
            out_refs[k][line : line + 1, :] = near_ref[:, lane]
            out_refs[k][4 + line : 5 + line, :] = centre_ref[:, lane]
        out_refs[k][8:16, :] = mean_ref[...]


def merge_kernel(*refs):
    came, out_ref = refs[:XS], refs[XS]
    group, line = iota((8, 128), 1) // CAP, iota((8, 128), 0)
    for s in range(4):
        rows = [ref[4 * t + s : 4 * t + s + 1, :] for ref in came for t in range(2)]
        value = jnp.concatenate(rows, axis=0)
        out = jnp.zeros((8, 128), F32)
        for d in range(8):
            turned = pltpu.roll(value, CAP * d, 1) if d else value
            picked = jnp.sum(jnp.where(group == line, turned, 0.0), axis=0, keepdims=True)
            out = jnp.where(((group - line) & 7) == d, picked, out)
        out_ref[8 * s : 8 * (s + 1), :] = out


def unpack_kernel(ids_ref, rank_ref, back_ref, *refs):
    came, (near_ref, centre_ref, mean_ref) = refs[:XS], refs[XS:]
    x, core = lax.axis_index("x"), lax.axis_index("core")
    for k in range(2):
        offset = (x - 2 * core - k) & 3
        folded = sum(jnp.where(offset == i, ref[8:16, :], 0.0) for i, ref in enumerate(came))
        for j in range(WIDTH // 128):
            mean_ref[k : k + 1, j * 128 : (j + 1) * 128] = folded[j : j + 1]
    ids = ids_ref[...]
    same = iota((32, ROWS), 0) == ((ids >> 2) & 7) * 4 + (ids >> 5)
    onehot = same.astype(F32).astype(BF16)
    parts = jnp.concatenate(split3(back_ref[...]), axis=1)
    picked = lax.dot_general(parts, onehot, TN, preferred_element_type=F32)
    picked = picked[0:128] + picked[128:256] + picked[256:384]
    place = ((x - ids) & 3) * PAIR + rank_ref[...]
    line = iota((128, ROWS), 0)
    near_ref[...] = jnp.sum(jnp.where(line == place, picked, 0.0), axis=0, keepdims=True)
    centre_ref[...] = jnp.sum(
        jnp.where(line == place + CAP, picked, 0.0), axis=0, keepdims=True
    )


def struct(shape, dtype):
    return jax.ShapeDtypeStruct(shape, dtype)


def call(kernel, outs, flops, scratch=(), grant=40, **specs):
    return pl.pallas_call(
        kernel,
        out_shape=outs,
        scratch_shapes=list(scratch),
        compiler_params=pltpu.CompilerParams(vmem_limit_bytes=grant * 1024 * 1024),
        cost_estimate=pl.CostEstimate(
            flops=int(flops), bytes_accessed=6_000_000, transcendentals=0
        ),
        **specs,
    )


def shards(embeddings, cluster_ids):
    ids = cluster_ids.reshape(1, ROWS)
    block = 2 * SLOTS * SLOTS * WIDTH
    here = pl.BlockSpec(memory_space=pltpu.VMEM)
    whole = struct((1, ROWS), jnp.int32)
    rank, slot = call(rank_kernel, (whole, whole), 3e10)(ids)
    send = call(pack_kernel, struct((SLOTS, WIDTH), BF16), 2 * SLOTS * ROWS * WIDTH)(
        slot, embeddings
    )
    chips = ("x", "z", "y")
    mine = lax.all_to_all(send.reshape(CHIPS, CAP, WIDTH), chips, 0, 0, tiled=True)
    mine = mine.reshape(SLOTS, WIDTH)
    swap = [(0, 1), (1, 0)]
    sib = lax.ppermute(mine, "core", swap)
    row = struct((1, SLOTS), F32)
    info, best = call(diagonal_kernel, (struct((3, SLOTS), F32), row), block / 4)(mine)
    sib_info = lax.ppermute(info, "core", swap)
    fold = pltpu.VMEM((TILE, 128), F32)
    best = call(own_kernel, row, block * 3 / 8, (fold,))(mine, info, best)
    line = struct((16, 128), F32)
    best, give = call(
        across_kernel,
        (row, row),
        block / 2,
        (
            pltpu.VMEM((SLOTS, WIDTH), BF16),
            pltpu.VMEM((2, SLOTS), F32),
            pltpu.SemaphoreType.DMA((TILES,)),
        ),
        in_specs=[here, pl.BlockSpec(memory_space=pltpu.HBM), here, here, here],
    )(mine, sib, info, sib_info, best)
    taken = lax.ppermute(give, "core", swap)
    centre, mean = call(
        centre_kernel, (row, struct((8, 128), F32)), block / 8
    )(give, mine, info, sib_info)
    outs = call(
        lines_kernel,
        (line,) * XS,
        1e7,
        (pltpu.VMEM((1, SLOTS), F32),),
    )(best, taken, info, centre, mean)
    came = [outs[0]]
    for k in range(1, XS):
        came.append(lax.ppermute(outs[k], "x", [(i, (i + k) % XS) for i in range(XS)]))
    out = call(merge_kernel, struct((32, 128), F32), 1e6)(*came)
    back = lax.all_to_all(out, ("z", "y"), 0, 0, tiled=True)
    near, centre, means = call(
        unpack_kernel,
        (struct((1, ROWS), F32), struct((1, ROWS), F32), struct((2, WIDTH), F32)),
        1e8,
    )(ids, rank, back, *came)
    return near.reshape(ROWS), centre.reshape(ROWS), means


def solution(mesh):
    fine = Mesh(mesh.devices.reshape(4, 8, 2, 4), ("y", "z", "core", "x"))
    owner = ("y", "z", "core")
    every = owner + ("x",)
    return jax.shard_map(
        shards,
        mesh=fine,
        in_specs=(P(every, None), P(every, None)),
        out_specs=(P(every), P(every), P(owner, None)),
        check_vma=False,
    )
```

```python
import jax
import jax.numpy as jnp
from jax import lax
from jax.experimental import pallas as pl
from jax.experimental.pallas import tpu as pltpu
from jax.sharding import Mesh, PartitionSpec as P

EPS = 1e-06
ROWS = 1024
WIDTH = 768
CAP = 16
CHIPS = 128
XS = 4
PAIR = 2 * CAP
SLOTS = CHIPS * CAP
MARK = 64.0
LOW = -1e30
TILE = 512
TILES = SLOTS // TILE
NT = (((1,), (1,)), ((), ()))
TN = (((0,), (0,)), ((), ()))
F32 = jnp.float32
BF16 = jnp.bfloat16


def iota(shape, dim):
    return lax.broadcasted_iota(jnp.int32, shape, dim)


def split3(v):
    hi = v.astype(BF16)
    rest = v - hi.astype(F32)
    mid = rest.astype(BF16)
    lo = (rest - mid.astype(F32)).astype(BF16)
    return hi, mid, lo


def chip_of(ids):
    return (ids & 3) * 32 + ((ids >> 2) & 7) * 4 + (ids >> 5)


def eye(n):
    return iota((n, n), 0) == iota((n, n), 1)


def to_row(column):
    blocks = [
        jnp.sum(jnp.where(eye(128), column[k : k + 128], 0.0), axis=0, keepdims=True)
        for k in range(0, column.shape[0], 128)
    ]
    return jnp.concatenate(blocks, axis=1)


def to_column(row):
    blocks = [
        jnp.sum(jnp.where(eye(128), row[:, k : k + 128], 0.0), axis=1, keepdims=True)
        for k in range(0, row.shape[1], 128)
    ]
    return jnp.concatenate(blocks, axis=0)


def fold_lanes(value):
    best = value[:, 0:128]
    for k in range(128, value.shape[1], 128):
        best = jnp.maximum(best, value[:, k : k + 128])
    return best


def part(ref, i):
    return ref[i * TILE : (i + 1) * TILE, :]


def lanes(ref, row, i):
    return ref[row : row + 1, i * TILE : (i + 1) * TILE]


def rank_kernel(chip_ref, rank_ref, slot_ref):
    chip = chip_ref[...]
    same = iota((CHIPS, ROWS), 0) == chip
    onehot = same.astype(F32).astype(BF16)
    before = (iota((ROWS, ROWS), 0) < iota((ROWS, ROWS), 1)).astype(F32).astype(BF16)
    earlier = jnp.dot(onehot, before, preferred_element_type=F32)
    rank = jnp.sum(jnp.where(same, earlier, 0.0), axis=0, keepdims=True).astype(jnp.int32)
    rank_ref[...] = rank
    slot_ref[...] = chip * CAP + rank


def pack_kernel(slot_ref, x_ref, send_ref):
    position = slot_ref[...]
    step = 256
    for start in range(0, SLOTS, step):
        pick = (iota((step, ROWS), 0) + start == position).astype(F32)
        live = jnp.sum(pick, axis=1, keepdims=True)
        rows = jnp.dot(pick.astype(BF16), x_ref[...], preferred_element_type=F32)
        mark = jnp.where(iota((step, 128), 1) == 0, (1.0 - live) * MARK, 0.0)
        send_ref[start : start + step, 0:128] = (rows[:, 0:128] + mark).astype(BF16)
        send_ref[start : start + step, 128:] = rows[:, 128:].astype(BF16)


def diagonal_kernel(x_ref, info_ref, best_ref):
    live = to_row((x_ref[:, 0:1].astype(F32) < MARK / 2).astype(F32))
    weights = jnp.broadcast_to(live, (8, SLOTS)).astype(BF16)
    totals = jnp.dot(weights, x_ref[...], preferred_element_type=F32)
    info_ref[1:2, :] = jnp.where(live > 0, 0.0, LOW)
    info_ref[2:3, 0:WIDTH] = totals[0:1]
    count = jnp.sum(live, axis=1, keepdims=True)
    info_ref[2:3, WIDTH:] = jnp.broadcast_to(count, (1, SLOTS - WIDTH))
    for i in range(TILES):
        dots = lax.dot_general(part(x_ref, i), part(x_ref, i), NT, preferred_element_type=F32)
        square = jnp.sum(jnp.where(eye(TILE), dots, 0.0), axis=0, keepdims=True)
        inv = lax.rsqrt(square / WIDTH + EPS)
        info_ref[0:1, i * TILE : (i + 1) * TILE] = inv
        value = jnp.where(eye(TILE), LOW, dots * inv + lanes(info_ref, 1, i))
        best = jnp.max(fold_lanes(value), axis=1, keepdims=True)
        best_ref[:, i * TILE : (i + 1) * TILE] = to_row(best)


def own_kernel(x_ref, info_ref, before_ref, best_ref):
    best_ref[...] = before_ref[...]
    for i in range(TILES - 2):
        inv = to_column(lanes(info_ref, 0, i))
        bias = to_column(lanes(info_ref, 1, i))
        for j in range(i + 1, TILES - i):
            dots = lax.dot_general(part(x_ref, i), part(x_ref, j), NT, preferred_element_type=F32)
            fold = fold_lanes(dots * lanes(info_ref, 0, j) + lanes(info_ref, 1, j))
            best = fold if j == i + 1 else jnp.maximum(best, fold)
            down = jnp.max(dots * inv + bias, axis=0, keepdims=True)
            best_ref[:, j * TILE : (j + 1) * TILE] = jnp.maximum(lanes(best_ref, 0, j), down)
        best = to_row(jnp.max(best, axis=1, keepdims=True))
        best_ref[:, i * TILE : (i + 1) * TILE] = jnp.maximum(lanes(best_ref, 0, i), best)


def across_kernel(
    x_ref, sib_hbm, info_ref, sib_info_ref, before_ref,
    best_ref, give_ref, sib_ref, turned_ref, sems,
):
    core = lax.axis_index("core")

    def rows(k):
        return pl.ds(pl.multiple_of(((core + k) & 3) * TILE, TILE), TILE)

    def copy(k):
        return pltpu.make_async_copy(
            sib_hbm.at[rows(k), :], sib_ref.at[k * TILE : (k + 1) * TILE, :], sems.at[k]
        )

    copy(0).start()
    copy(2).start()
    for k in range(TILES):
        turned_ref[:, k * TILE : (k + 1) * TILE] = sib_info_ref[0:2, rows(k)]
    columns = [
        (to_column(lanes(info_ref, 0, i)), to_column(lanes(info_ref, 1, i))) for i in range(TILES)
    ]

    def both(i, other, row, bias):
        dots = lax.dot_general(part(x_ref, i), other, NT, preferred_element_type=F32)
        down = jnp.max(dots * columns[i][0] + columns[i][1], axis=0, keepdims=True)
        return fold_lanes(dots * row + bias), down

    def own(i):
        j = TILES - 1
        return both(i, part(x_ref, j), lanes(info_ref, 0, j), lanes(info_ref, 1, j))

    folds, downs = {}, {}
    folds[2], downs[2] = own(2)
    give = {}
    for i in range(TILES):
        if i == 0:
            copy(0).wait()
            copy(2).wait()
            copy(1).start()
            copy(3).start()
            folds[1], downs[1] = own(1)
        if i == 1:
            copy(1).wait()
            copy(3).wait()
        fold = folds.get(i)
        for k in (i, (i + 2) % TILES):
            value, down = both(i, part(sib_ref, k), lanes(turned_ref, 0, k), lanes(turned_ref, 1, k))
            fold = value if fold is None else jnp.maximum(fold, value)
            give[k] = jnp.maximum(give[k], down) if k in give else down
        best = jnp.maximum(
            lanes(before_ref, 0, i), to_row(jnp.max(fold, axis=1, keepdims=True))
        )
        if i == TILES - 1:
            best = jnp.maximum(best, jnp.maximum(downs[1], downs[2]))
        best_ref[:, i * TILE : (i + 1) * TILE] = best
    for k in range(TILES):
        give_ref[:, rows(k)] = give[k]


def centre_kernel(after_ref, x_ref, info_ref, sib_info_ref, centre_ref, mean_ref):
    total = info_ref[2:3, 0:WIDTH] + sib_info_ref[2:3, 0:WIDTH]
    count = info_ref[2:3, WIDTH : WIDTH + 1] + sib_info_ref[2:3, WIDTH : WIDTH + 1]
    mean = total / count
    folded = [mean[:, k : k + 128] for k in range(0, WIDTH, 128)]
    mean_ref[...] = jnp.concatenate(folded + [jnp.zeros((2, 128), F32)], axis=0)
    scale = lax.rsqrt(jnp.sum(total * total, axis=1, keepdims=True) / WIDTH + EPS)
    parts = jnp.concatenate(split3(total) + (jnp.zeros((13, WIDTH), BF16),), axis=0)
    toward = lax.dot_general(parts, x_ref[...], NT, preferred_element_type=F32)
    toward = toward[0:1] + toward[1:2] + toward[2:3]
    centre_ref[...] = toward * info_ref[0:1, :] * scale / WIDTH


def lines_kernel(best_ref, taken_ref, info_ref, centre_ref, mean_ref, *refs):
    out_refs, near_ref = refs[:XS], refs[XS]
    best = jnp.maximum(best_ref[...], taken_ref[...])
    near_ref[...] = jnp.maximum(-1.0, best * info_ref[0:1, :] / WIDTH)
    for k in range(XS):
        first = ((lax.axis_index("x") + k) & 3) * TILE
        for line in range(4):
            lane = pl.ds(pl.multiple_of(first + line * 128, 128), 128)
            out_refs[k][line : line + 1, :] = near_ref[:, lane]
            out_refs[k][4 + line : 5 + line, :] = centre_ref[:, lane]
        out_refs[k][8:16, :] = mean_ref[...]


def merge_kernel(*refs):
    came, out_ref = refs[:XS], refs[XS]
    group, line = iota((8, 128), 1) // CAP, iota((8, 128), 0)
    for s in range(4):
        rows = [ref[4 * t + s : 4 * t + s + 1, :] for ref in came for t in range(2)]
        value = jnp.concatenate(rows, axis=0)
        out = jnp.zeros((8, 128), F32)
        for d in range(8):
            turned = pltpu.roll(value, CAP * d, 1) if d else value
            picked = jnp.sum(jnp.where(group == line, turned, 0.0), axis=0, keepdims=True)
            out = jnp.where(((group - line) & 7) == d, picked, out)
        out_ref[8 * s : 8 * (s + 1), :] = out


def unpack_kernel(ids_ref, rank_ref, back_ref, *refs):
    came, (near_ref, centre_ref, mean_ref) = refs[:XS], refs[XS:]
    x, core = lax.axis_index("x"), lax.axis_index("core")
    for k in range(2):
        offset = (x - 2 * core - k) & 3
        folded = sum(jnp.where(offset == i, ref[8:16, :], 0.0) for i, ref in enumerate(came))
        for j in range(WIDTH // 128):
            mean_ref[k : k + 1, j * 128 : (j + 1) * 128] = folded[j : j + 1]
    ids = ids_ref[...]
    same = iota((32, ROWS), 0) == ((ids >> 2) & 7) * 4 + (ids >> 5)
    onehot = same.astype(F32).astype(BF16)
    parts = jnp.concatenate(split3(back_ref[...]), axis=1)
    picked = lax.dot_general(parts, onehot, TN, preferred_element_type=F32)
    picked = picked[0:128] + picked[128:256] + picked[256:384]
    place = ((x - ids) & 3) * PAIR + rank_ref[...]
    line = iota((128, ROWS), 0)
    near_ref[...] = jnp.sum(jnp.where(line == place, picked, 0.0), axis=0, keepdims=True)
    centre_ref[...] = jnp.sum(
        jnp.where(line == place + CAP, picked, 0.0), axis=0, keepdims=True
    )


def struct(shape, dtype):
    return jax.ShapeDtypeStruct(shape, dtype)


def call(kernel, outs, flops, scratch=(), grant=40, **specs):
    return pl.pallas_call(
        kernel,
        out_shape=outs,
        scratch_shapes=list(scratch),
        compiler_params=pltpu.CompilerParams(vmem_limit_bytes=grant * 1024 * 1024),
        cost_estimate=pl.CostEstimate(
            flops=int(flops), bytes_accessed=6_000_000, transcendentals=0
        ),
        **specs,
    )


def shards(embeddings, cluster_ids):
    ids = cluster_ids.reshape(1, ROWS)
    block = 2 * SLOTS * SLOTS * WIDTH
    here = pl.BlockSpec(memory_space=pltpu.VMEM)
    whole = struct((1, ROWS), jnp.int32)
    rank, slot = call(rank_kernel, (whole, whole), 3e10)(chip_of(ids))
    send = call(pack_kernel, struct((SLOTS, WIDTH), BF16), 2 * SLOTS * ROWS * WIDTH)(
        slot, embeddings
    )
    chips = ("x", "z", "y")
    mine = lax.all_to_all(send.reshape(CHIPS, CAP, WIDTH), chips, 0, 0, tiled=True)
    mine = mine.reshape(SLOTS, WIDTH)
    swap = [(0, 1), (1, 0)]
    sib = lax.ppermute(mine, "core", swap)
    row = struct((1, SLOTS), F32)
    info, best = call(diagonal_kernel, (struct((3, SLOTS), F32), row), block / 4)(mine)
    sib_info = lax.ppermute(info, "core", swap)
    best = call(own_kernel, row, block / 4)(mine, info, best)
    line = struct((16, 128), F32)
    best, give = call(
        across_kernel,
        (row, row),
        block / 2,
        (
            pltpu.VMEM((SLOTS, WIDTH), BF16),
            pltpu.VMEM((2, SLOTS), F32),
            pltpu.SemaphoreType.DMA((TILES,)),
        ),
        in_specs=[here, pl.BlockSpec(memory_space=pltpu.HBM), here, here, here],
    )(mine, sib, info, sib_info, best)
    taken = lax.ppermute(give, "core", swap)
    centre, mean = call(
        centre_kernel, (row, struct((8, 128), F32)), block / 8
    )(give, mine, info, sib_info)
    outs = call(
        lines_kernel,
        (line,) * XS,
        1e7,
        (pltpu.VMEM((1, SLOTS), F32),),
    )(best, taken, info, centre, mean)
    came = [outs[0]]
    for k in range(1, XS):
        came.append(lax.ppermute(outs[k], "x", [(i, (i + k) % XS) for i in range(XS)]))
    out = call(merge_kernel, struct((32, 128), F32), 1e6)(*came)
    back = lax.all_to_all(out, ("z", "y"), 0, 0, tiled=True)
    near, centre, means = call(
        unpack_kernel,
        (struct((1, ROWS), F32), struct((1, ROWS), F32), struct((2, WIDTH), F32)),
        1e8,
    )(ids, rank, back, *came)
    return near.reshape(ROWS), centre.reshape(ROWS), means


def solution(mesh):
    fine = Mesh(mesh.devices.reshape(4, 8, 2, 4), ("y", "z", "core", "x"))
    owner = ("y", "z", "core")
    every = owner + ("x",)
    return jax.shard_map(
        shards,
        mesh=fine,
        in_specs=(P(every, None), P(every, None)),
        out_specs=(P(every), P(every), P(owner, None)),
        check_vma=False,
    )
```

```python
import jax
import jax.numpy as jnp
from jax import lax
from jax.experimental import pallas as pl
from jax.experimental.pallas import tpu as pltpu
from jax.sharding import Mesh, PartitionSpec as P

EPS = 1e-06
ROWS = 1024
WIDTH = 768
CAP = 16
CHIPS = 128
XS = 4
PAIR = 2 * CAP
SLOTS = CHIPS * CAP
MARK = 64.0
LOW = -1e30
TILE = 512
TILES = SLOTS // TILE
NT = (((1,), (1,)), ((), ()))
TN = (((0,), (0,)), ((), ()))
F32 = jnp.float32
BF16 = jnp.bfloat16


def iota(shape, dim):
    return lax.broadcasted_iota(jnp.int32, shape, dim)


def split3(v):
    hi = v.astype(BF16)
    rest = v - hi.astype(F32)
    mid = rest.astype(BF16)
    lo = (rest - mid.astype(F32)).astype(BF16)
    return hi, mid, lo


def chip_of(ids):
    return (ids & 3) * 32 + ((ids >> 2) & 7) * 4 + (ids >> 5)


def eye(n):
    return iota((n, n), 0) == iota((n, n), 1)


def to_row(column):
    blocks = [
        jnp.sum(jnp.where(eye(128), column[k : k + 128], 0.0), axis=0, keepdims=True)
        for k in range(0, column.shape[0], 128)
    ]
    return jnp.concatenate(blocks, axis=1)


def to_column(row):
    blocks = [
        jnp.sum(jnp.where(eye(128), row[:, k : k + 128], 0.0), axis=1, keepdims=True)
        for k in range(0, row.shape[1], 128)
    ]
    return jnp.concatenate(blocks, axis=0)


def fold_lanes(value):
    best = value[:, 0:128]
    for k in range(128, value.shape[1], 128):
        best = jnp.maximum(best, value[:, k : k + 128])
    return best


def part(ref, i):
    return ref[i * TILE : (i + 1) * TILE, :]


def lanes(ref, row, i):
    return ref[row : row + 1, i * TILE : (i + 1) * TILE]


def rank_kernel(chip_ref, rank_ref, slot_ref):
    chip = chip_ref[...]
    same = iota((CHIPS, ROWS), 0) == chip
    onehot = same.astype(F32).astype(BF16)
    before = (iota((ROWS, ROWS), 0) < iota((ROWS, ROWS), 1)).astype(F32).astype(BF16)
    earlier = jnp.dot(onehot, before, preferred_element_type=F32)
    rank = jnp.sum(jnp.where(same, earlier, 0.0), axis=0, keepdims=True).astype(jnp.int32)
    rank_ref[...] = rank
    slot_ref[...] = chip * CAP + rank


def pack_kernel(slot_ref, x_ref, send_ref):
    position = slot_ref[...]
    step = 256
    for start in range(0, SLOTS, step):
        pick = (iota((step, ROWS), 0) + start == position).astype(F32)
        live = jnp.sum(pick, axis=1, keepdims=True)
        rows = jnp.dot(pick.astype(BF16), x_ref[...], preferred_element_type=F32)
        mark = jnp.where(iota((step, 128), 1) == 0, (1.0 - live) * MARK, 0.0)
        send_ref[start : start + step, 0:128] = (rows[:, 0:128] + mark).astype(BF16)
        send_ref[start : start + step, 128:] = rows[:, 128:].astype(BF16)


def diagonal_kernel(x_ref, info_ref, best_ref):
    live = to_row((x_ref[:, 0:1].astype(F32) < MARK / 2).astype(F32))
    weights = jnp.broadcast_to(live, (8, SLOTS)).astype(BF16)
    totals = jnp.dot(weights, x_ref[...], preferred_element_type=F32)
    info_ref[1:2, :] = jnp.where(live > 0, 0.0, LOW)
    info_ref[2:3, 0:WIDTH] = totals[0:1]
    count = jnp.sum(live, axis=1, keepdims=True)
    info_ref[2:3, WIDTH:] = jnp.broadcast_to(count, (1, SLOTS - WIDTH))
    for i in range(TILES):
        dots = lax.dot_general(part(x_ref, i), part(x_ref, i), NT, preferred_element_type=F32)
        square = jnp.sum(jnp.where(eye(TILE), dots, 0.0), axis=0, keepdims=True)
        inv = lax.rsqrt(square / WIDTH + EPS)
        info_ref[0:1, i * TILE : (i + 1) * TILE] = inv
        value = jnp.where(eye(TILE), LOW, dots * inv + lanes(info_ref, 1, i))
        best = jnp.max(fold_lanes(value), axis=1, keepdims=True)
        best_ref[:, i * TILE : (i + 1) * TILE] = to_row(best)


def own_kernel(x_ref, info_ref, before_ref, best_ref):
    best_ref[...] = before_ref[...]
    for i in range(TILES - 2):
        inv = to_column(lanes(info_ref, 0, i))
        bias = to_column(lanes(info_ref, 1, i))
        for j in range(i + 1, TILES - i):
            dots = lax.dot_general(part(x_ref, i), part(x_ref, j), NT, preferred_element_type=F32)
            fold = fold_lanes(dots * lanes(info_ref, 0, j) + lanes(info_ref, 1, j))
            best = fold if j == i + 1 else jnp.maximum(best, fold)
            down = jnp.max(dots * inv + bias, axis=0, keepdims=True)
            best_ref[:, j * TILE : (j + 1) * TILE] = jnp.maximum(lanes(best_ref, 0, j), down)
        best = to_row(jnp.max(best, axis=1, keepdims=True))
        best_ref[:, i * TILE : (i + 1) * TILE] = jnp.maximum(lanes(best_ref, 0, i), best)


def across_kernel(
    x_ref, sib_hbm, info_ref, sib_info_ref, before_ref,
    best_ref, give_ref, sib_ref, turned_ref, sems,
):
    core = lax.axis_index("core")

    def rows(k):
        return pl.ds(pl.multiple_of(((core + k) & 3) * TILE, TILE), TILE)

    def copy(k):
        return pltpu.make_async_copy(
            sib_hbm.at[rows(k), :], sib_ref.at[k * TILE : (k + 1) * TILE, :], sems.at[k]
        )

    copy(0).start()
    copy(2).start()
    for k in range(TILES):
        turned_ref[:, k * TILE : (k + 1) * TILE] = sib_info_ref[0:2, rows(k)]
    columns = [
        (to_column(lanes(info_ref, 0, i)), to_column(lanes(info_ref, 1, i))) for i in range(TILES)
    ]

    def both(i, other, row, bias):
        dots = lax.dot_general(part(x_ref, i), other, NT, preferred_element_type=F32)
        down = jnp.max(dots * columns[i][0] + columns[i][1], axis=0, keepdims=True)
        return fold_lanes(dots * row + bias), down

    def own(i):
        j = TILES - 1
        return both(i, part(x_ref, j), lanes(info_ref, 0, j), lanes(info_ref, 1, j))

    folds, downs = {}, {}
    folds[2], downs[2] = own(2)
    give = {}
    for i in range(TILES):
        if i == 0:
            copy(0).wait()
            copy(2).wait()
            copy(1).start()
            copy(3).start()
            folds[1], downs[1] = own(1)
        if i == 1:
            copy(1).wait()
            copy(3).wait()
        fold = folds.get(i)
        for k in (i, (i + 2) % TILES):
            value, down = both(i, part(sib_ref, k), lanes(turned_ref, 0, k), lanes(turned_ref, 1, k))
            fold = value if fold is None else jnp.maximum(fold, value)
            give[k] = jnp.maximum(give[k], down) if k in give else down
        best = jnp.maximum(
            lanes(before_ref, 0, i), to_row(jnp.max(fold, axis=1, keepdims=True))
        )
        if i == TILES - 1:
            best = jnp.maximum(best, jnp.maximum(downs[1], downs[2]))
        best_ref[:, i * TILE : (i + 1) * TILE] = best
    for k in range(TILES):
        give_ref[:, rows(k)] = give[k]


def centre_kernel(after_ref, x_ref, info_ref, sib_info_ref, centre_ref, mean_ref):
    total = info_ref[2:3, 0:WIDTH] + sib_info_ref[2:3, 0:WIDTH]
    count = info_ref[2:3, WIDTH : WIDTH + 1] + sib_info_ref[2:3, WIDTH : WIDTH + 1]
    mean = total / count
    folded = [mean[:, k : k + 128] for k in range(0, WIDTH, 128)]
    mean_ref[...] = jnp.concatenate(folded + [jnp.zeros((2, 128), F32)], axis=0)
    scale = lax.rsqrt(jnp.sum(total * total, axis=1, keepdims=True) / WIDTH + EPS)
    parts = jnp.concatenate(split3(total) + (jnp.zeros((13, WIDTH), BF16),), axis=0)
    toward = lax.dot_general(parts, x_ref[...], NT, preferred_element_type=F32)
    toward = toward[0:1] + toward[1:2] + toward[2:3]
    centre_ref[...] = toward * info_ref[0:1, :] * scale / WIDTH


def lines_kernel(best_ref, taken_ref, info_ref, centre_ref, mean_ref, *refs):
    out_refs, near_ref = refs[:XS], refs[XS]
    best = jnp.maximum(best_ref[...], taken_ref[...])
    near_ref[...] = jnp.maximum(-1.0, best * info_ref[0:1, :] / WIDTH)
    for k in range(XS):
        first = ((lax.axis_index("x") + k) & 3) * TILE
        for line in range(4):
            lane = pl.ds(pl.multiple_of(first + line * 128, 128), 128)
            out_refs[k][line : line + 1, :] = near_ref[:, lane]
            out_refs[k][4 + line : 5 + line, :] = centre_ref[:, lane]
        out_refs[k][8:16, :] = mean_ref[...]


def merge_kernel(*refs):
    came, out_ref = refs[:XS], refs[XS]
    group, line = iota((8, 128), 1) // CAP, iota((8, 128), 0)
    for s in range(4):
        rows = [ref[4 * t + s : 4 * t + s + 1, :] for ref in came for t in range(2)]
        value = jnp.concatenate(rows, axis=0)
        out = jnp.zeros((8, 128), F32)
        for d in range(8):
            turned = pltpu.roll(value, CAP * d, 1) if d else value
            picked = jnp.sum(jnp.where(group == line, turned, 0.0), axis=0, keepdims=True)
            out = jnp.where(((group - line) & 7) == d, picked, out)
        out_ref[8 * s : 8 * (s + 1), :] = out


def unpack_kernel(ids_ref, rank_ref, back_ref, *refs):
    came, (near_ref, centre_ref, mean_ref) = refs[:XS], refs[XS:]
    x, core = lax.axis_index("x"), lax.axis_index("core")
    for k in range(2):
        offset = (x - 2 * core - k) & 3
        folded = sum(jnp.where(offset == i, ref[8:16, :], 0.0) for i, ref in enumerate(came))
        for j in range(WIDTH // 128):
            mean_ref[k : k + 1, j * 128 : (j + 1) * 128] = folded[j : j + 1]
    ids = ids_ref[...]
    same = iota((32, ROWS), 0) == ((ids >> 2) & 7) * 4 + (ids >> 5)
    onehot = same.astype(F32).astype(BF16)
    parts = jnp.concatenate(split3(back_ref[...]), axis=1)
    picked = lax.dot_general(parts, onehot, TN, preferred_element_type=F32)
    picked = picked[0:128] + picked[128:256] + picked[256:384]
    place = ((x - ids) & 3) * PAIR + rank_ref[...]
    line = iota((128, ROWS), 0)
    near_ref[...] = jnp.sum(jnp.where(line == place, picked, 0.0), axis=0, keepdims=True)
    centre_ref[...] = jnp.sum(
        jnp.where(line == place + CAP, picked, 0.0), axis=0, keepdims=True
    )


def struct(shape, dtype):
    return jax.ShapeDtypeStruct(shape, dtype)


def call(kernel, outs, flops, scratch=(), grant=40, **specs):
    return pl.pallas_call(
        kernel,
        out_shape=outs,
        scratch_shapes=list(scratch),
        compiler_params=pltpu.CompilerParams(vmem_limit_bytes=grant * 1024 * 1024),
        cost_estimate=pl.CostEstimate(
            flops=int(flops), bytes_accessed=6_000_000, transcendentals=0
        ),
        **specs,
    )


def shards(embeddings, cluster_ids):
    ids = cluster_ids.reshape(1, ROWS)
    block = 2 * SLOTS * SLOTS * WIDTH
    here = pl.BlockSpec(memory_space=pltpu.VMEM)
    whole = struct((1, ROWS), jnp.int32)
    rank, slot = call(rank_kernel, (whole, whole), 1e9)(chip_of(ids))
    send = call(pack_kernel, struct((SLOTS, WIDTH), BF16), 2 * SLOTS * ROWS * WIDTH)(
        slot, embeddings
    )
    chips = ("x", "z", "y")
    mine = lax.all_to_all(send.reshape(CHIPS, CAP, WIDTH), chips, 0, 0, tiled=True)
    mine = mine.reshape(SLOTS, WIDTH)
    swap = [(0, 1), (1, 0)]
    sib = lax.ppermute(mine, "core", swap)
    row = struct((1, SLOTS), F32)
    info, best = call(diagonal_kernel, (struct((3, SLOTS), F32), row), block / 4)(mine)
    sib_info = lax.ppermute(info, "core", swap)
    best = call(own_kernel, row, block / 4)(mine, info, best)
    line = struct((16, 128), F32)
    best, give = call(
        across_kernel,
        (row, row),
        block / 2,
        (
            pltpu.VMEM((SLOTS, WIDTH), BF16),
            pltpu.VMEM((2, SLOTS), F32),
            pltpu.SemaphoreType.DMA((TILES,)),
        ),
        in_specs=[here, pl.BlockSpec(memory_space=pltpu.HBM), here, here, here],
    )(mine, sib, info, sib_info, best)
    taken = lax.ppermute(give, "core", swap)
    centre, mean = call(
        centre_kernel, (row, struct((8, 128), F32)), block / 8
    )(give, mine, info, sib_info)
    outs = call(
        lines_kernel,
        (line,) * XS,
        1e7,
        (pltpu.VMEM((1, SLOTS), F32),),
    )(best, taken, info, centre, mean)
    came = [outs[0]]
    for k in range(1, XS):
        came.append(lax.ppermute(outs[k], "x", [(i, (i + k) % XS) for i in range(XS)]))
    out = call(merge_kernel, struct((32, 128), F32), 1e6)(*came)
    back = lax.all_to_all(out, ("z", "y"), 0, 0, tiled=True)
    near, centre, means = call(
        unpack_kernel,
        (struct((1, ROWS), F32), struct((1, ROWS), F32), struct((2, WIDTH), F32)),
        1e8,
    )(ids, rank, back, *came)
    return near.reshape(ROWS), centre.reshape(ROWS), means


def solution(mesh):
    fine = Mesh(mesh.devices.reshape(4, 8, 2, 4), ("y", "z", "core", "x"))
    owner = ("y", "z", "core")
    every = owner + ("x",)
    return jax.shard_map(
        shards,
        mesh=fine,
        in_specs=(P(every, None), P(every, None)),
        out_specs=(P(every), P(every), P(owner, None)),
        check_vma=False,
    )
```
